32 devices in a mesh: groups: 2 (over y), patch: 4 (over z), sub: 4 (over x, core).
Axes of the slice: x: 2, y: 2, z: 4, core: 2. Of those that a mesh axis runs over, the one named last changes fastest.
Arguments:
- points: float32 [1024, 3, 128], P(('groups', 'patch', 'sub')), parts along dimension 0, may hold values from -3 to 3
- normals: float32 [1024, 3, 128], P(('groups', 'patch', 'sub')), parts along dimension 0, may hold values from -2 to 2
- density: float32 [1024, 128], P(('groups', 'patch', 'sub')), parts along dimension 0
- counts: int32 [32], P(('groups', 'patch', 'sub')), parts along dimension 0, may hold values from 16 to 32, as said below
- near_list: int32 [1024, 9], P(('groups', 'patch', 'sub')), parts along dimension 0, may hold values from 0 to 511, as said below
- leaf_far: int32 [1024, 8], P(('groups', 'patch', 'sub')), parts along dimension 0, may hold values from 0 to 511, as said below
- leaf_basis: float32 [1024, 64, 128], P(('groups', 'patch', 'sub')), parts along dimension 0, may hold values from -0.5 to 0.5
- leaf_to_box_transfer: float32 [1024, 64, 64], P(('groups', 'patch', 'sub')), parts along dimension 0, may hold values from -0.25 to 0.25
- leaf_coupling: float32 [8, 64, 64], replicated, may hold values from -0.25 to 0.25
- box_far: int32 [32, 8], P(('groups', 'patch', 'sub')), parts along dimension 0, may hold values from 0 to 15
- box_coupling: float32 [8, 64, 64], replicated, may hold values from -0.25 to 0.25
Outputs:
- next_basis: float32 [1024, 128], P(('groups', 'patch', 'sub')), parts along dimension 0
- hessenberg: float32 [6, 2], P('groups'), parts along dimension 0
The draws below stay inside these ranges and needn't reach their ends.
There are 2 independent parts, one for each index of `groups`. The reference program is written for one: setup_inputs(seed, part) draws one part's arguments, and reference() takes and returns one part's arrays. A program takes and returns all parts, laid end to end along the dimension named above; an argument that names none is the same for every part. Nothing has to cross between parts.
Inputs may be any that keep to these rules, and one draw needn't show every extreme that they name: `counts`: between 16 and 32 slots of each device are in use; some device of each surface uses all 32. `near_list`: entry 0 of every slot is the slot itself; all entries of a slot not in use are the slot itself. The other entries of a slot in use name slots in use of the same patch. The leaves of one other device that a device's lists name are at most 4, and exactly 4 for some pair of devices in every draw. `leaf_far`: every entry names a slot in use of the same patch.
All inputs are finite; a program needn't handle non-finite values.
Results may differ from the reference program's by a relative error of at most 0.0003.
Values sent between devices are 32-bit elements; how exact they have to be, the bound alone decides.
No kernel may reach another device: no remote copies, remote signals or barrier semaphores. Data moves between devices by JAX's collectives and lax.ppermute only.
A program may use at most 64 MiB of HBM per device.

```python
import math
import jax
import jax.numpy as jnp
from jax import lax

LEAF = 128
RANK = 64
LEAF_DEV = 32
KN = 9
KLOC = 2
CAP = 4
KF = 8
KB = 8
BOXES = 16
LEAVES = 512
N_SUB = 4


def common_counts(key):
    key = jax.random.fold_in(key, 11)
    key_spread, key_full = jax.random.split(key)
    half_slots = LEAF_DEV // 2
    drawn = half_slots + jax.random.randint(key_spread, (BOXES,), 0, LEAF_DEV - half_slots + 1)
    full_box = jax.random.randint(key_full, (), 0, BOXES)
    drawn = jnp.where(jnp.arange(BOXES) == full_box, LEAF_DEV, drawn)
    return drawn.astype(jnp.int32)


def draw_counts(key, part):
    return common_counts(key)


def draw_near_list(key, part):
    box_counts = common_counts(key)
    key = jax.random.fold_in(key, 5)
    key_share, key_score, key_own = jax.random.split(key, 3)
    box_index = jnp.arange(BOXES, dtype=jnp.int32)
    sub_of = box_index % N_SUB
    patch_of = box_index // N_SUB
    peer_index = jnp.arange(N_SUB, dtype=jnp.int32)
    share_count = jax.random.randint(key_share, (BOXES, N_SUB), 0, CAP + 1)
    far_peer = (sub_of + N_SUB // 2) % N_SUB
    share_count = jnp.where(peer_index[None, :] == far_peer[:, None], CAP, share_count)
    share_count = jnp.where(peer_index[None, :] == sub_of[:, None], 0, share_count)
    peer_box = patch_of[:, None] * N_SUB + peer_index[None, :]
    peer_count = box_counts[peer_box]
    slot_index = jnp.arange(LEAF_DEV, dtype=jnp.int32)
    scores = jax.random.randint(key_score, (BOXES, N_SUB, LEAF_DEV), 0, 1 << 20) * LEAF_DEV + slot_index
    scores = jnp.where(slot_index[None, None, :] < peer_count[:, :, None], scores, (1 << 20) * LEAF_DEV + slot_index)
    ordering = jnp.argsort(scores, axis=2)
    candidate = ordering[:, :, :CAP]
    is_live = jnp.arange(CAP)[None, None, :] < share_count[:, :, None]
    global_leaf = peer_box[:, :, None] * LEAF_DEV + candidate
    flat_live = is_live.reshape(BOXES, N_SUB * CAP)
    flat_leaf = global_leaf.reshape(BOXES, N_SUB * CAP)
    sorting_key = jnp.where(flat_live, 0, 1) * (N_SUB * CAP) + jnp.arange(N_SUB * CAP)
    placed = jnp.argsort(sorting_key, axis=1)
    pool_rows = jnp.take_along_axis(flat_leaf, placed, axis=1)
    pool_size = jnp.sum(share_count, axis=1)
    remote_count = KN - 1 - KLOC
    pool_pick = slot_index[:, None] * remote_count + jnp.arange(remote_count)[None, :]
    pool_pick = pool_pick[None, :, :] % pool_size[:, None, None]
    remote = jnp.take_along_axis(pool_rows, pool_pick.reshape(BOXES, LEAF_DEV * remote_count), axis=1)
    remote = remote.reshape(BOXES, LEAF_DEV, remote_count)
    own_rows = jax.random.randint(key_own, (BOXES, LEAF_DEV, KLOC), 0, 1 << 20) % box_counts[:, None, None]
    own_rows = own_rows + box_index[:, None, None] * LEAF_DEV
    self_rows = box_index[:, None] * LEAF_DEV + slot_index[None, :]
    entries = jnp.concatenate([self_rows[:, :, None], own_rows, remote], axis=2)
    usable = slot_index[None, :] < box_counts[:, None]
    entries = jnp.where(usable[:, :, None], entries, self_rows[:, :, None])
    return entries.reshape(LEAVES, KN).astype(jnp.int32)


def draw_leaf_far(key, part):
    box_counts = common_counts(key)
    key = jax.random.fold_in(key, 7)
    key_peer, key_slot = jax.random.split(key)
    leaf_index = jnp.arange(LEAVES, dtype=jnp.int32)
    patch_index = leaf_index // (LEAF_DEV * N_SUB)
    peer_pick = jax.random.randint(key_peer, (LEAVES, KF), 0, N_SUB)
    box_pick = patch_index[:, None] * N_SUB + peer_pick
    slot_pick = jax.random.randint(key_slot, (LEAVES, KF), 0, 1 << 20) % box_counts[box_pick]
    return (box_pick * LEAF_DEV + slot_pick).astype(jnp.int32)


def draw_density(key, part):
    key = jax.random.fold_in(key, 3)
    key_row, key_col, key_base = jax.random.split(key, 3)
    leaf_index = jnp.arange(LEAVES).astype(jnp.float32)
    ascending = 1.0 + 2.0 * leaf_index / (LEAVES - 1)
    row_scale = jnp.exp(jax.random.uniform(key_row, (LEAVES, 1)) * math.log(10.0))
    col_scale = jnp.exp(jax.random.uniform(key_col, (1, LEAF)) * math.log(3.0))
    base_sample = jax.random.normal(key_base, (LEAVES, LEAF))
    return (base_sample * ascending[:, None] * row_scale * col_scale * 0.25).astype(jnp.float32)


def with_ends(array, rng, least, largest):
    longest = array.shape.index(max(array.shape))
    spots = []
    for shift in (0, 1):
        where = [jax.random.randint(jax.random.fold_in(rng, axis), (), 0, length) for axis, length in enumerate(array.shape)]
        where[longest] = (where[longest] + shift) % array.shape[longest]
        spots.append(tuple(where))
    return array.at[spots[0]].set(least).at[spots[1]].set(largest)


def level_of(stream_key, shape, shards, low, top_value):
    def one(dim, shards_of):
        draws = jax.random.uniform(jax.random.fold_in(jax.random.fold_in(stream_key, 6), dim), (shards_of,), jnp.float32, low / len(shards), top_value / len(shards))
        return jnp.repeat(jnp.exp(draws), shape[dim] // shards_of).reshape((-1,) + (1,) * (len(shape) - dim - 1))

    loudness = one(*shards[0])
    for cut in shards[1:]:
        loudness = loudness * one(*cut)
    return loudness


def scatter_about(key, extent, width, bound, cuts=(), kind=jnp.bfloat16):
    level = level_of(key, extent, cuts, -0.22, 0.18) if cuts else 1.0
    values = jax.random.normal(key, extent, jnp.float32) * width * level
    return jnp.minimum(jnp.maximum(values, -bound), bound).astype(kind)


def setup_inputs(seed: int = 0, part: int = 0) -> dict:
    splits = jax.random.split(jax.random.key(seed), 12)
    part_keys = jax.random.split(jax.random.fold_in(splits[11], part), 12)
    points = scatter_about(part_keys[0], (LEAVES, 3, LEAF), 0.6, 3.0, ((0, 16),), jnp.float32)
    normals = scatter_about(part_keys[1], (LEAVES, 3, LEAF), 0.3, 2.0, ((0, 16),), jnp.float32)
    density = draw_density(jax.random.fold_in(jax.random.fold_in(splits[11], part), 71), part)
    counts = draw_counts(jax.random.fold_in(jax.random.fold_in(splits[11], part), 71), part)
    near_list = draw_near_list(jax.random.fold_in(jax.random.fold_in(splits[11], part), 71), part)
    leaf_far = draw_leaf_far(jax.random.fold_in(jax.random.fold_in(splits[11], part), 71), part)
    leaf_basis = scatter_about(part_keys[6], (LEAVES, RANK, LEAF), LEAF ** -0.5, 0.5, ((0, 16),), jnp.float32)
    leaf_to_box_transfer = scatter_about(part_keys[7], (LEAVES, RANK, RANK), (8 * RANK) ** -0.5, 0.25, ((0, 16),), jnp.float32)
    leaf_coupling = scatter_about(splits[8], (KF, RANK, RANK), (KF * RANK) ** -0.5, 0.25, (), jnp.float32)
    box_far = with_ends(jax.random.randint(part_keys[9], (BOXES, KB), 0, BOXES), jax.random.fold_in(part_keys[9], 1), 0, BOXES - 1).astype(jnp.int32)
    box_coupling = scatter_about(splits[10], (KB, RANK, RANK), (KB * RANK) ** -0.5, 0.25, (), jnp.float32)
    return {"points": points, "normals": normals, "density": density, "counts": counts, "near_list": near_list, "leaf_far": leaf_far, "leaf_basis": leaf_basis, "leaf_to_box_transfer": leaf_to_box_transfer, "leaf_coupling": leaf_coupling, "box_far": box_far, "box_coupling": box_coupling}


SOFTEN = 0.05
EPSILON = 1e-06
HIGH_PRECISION = lax.Precision.HIGHEST

def kernel_tile(target, source, normal):
    delta_x = source[:, 0, None, :] - target[:, 0, :, None]
    delta_y = source[:, 1, None, :] - target[:, 1, :, None]
    delta_z = source[:, 2, None, :] - target[:, 2, :, None]
    radius_sq = delta_x * delta_x + delta_y * delta_y + delta_z * delta_z + SOFTEN
    inverse = lax.rsqrt(radius_sq)
    normal_part = delta_x * normal[:, 0, None, :] + delta_y * normal[:, 1, None, :] + delta_z * normal[:, 2, None, :]
    return normal_part * inverse * inverse * inverse * (0.25 / math.pi)

def operator(vector, in_use, points, normals, near_list, leaf_far, leaf_basis, leaf_to_box_transfer, leaf_coupling, box_far, box_coupling):
    vector = jnp.where(in_use[:, None], vector, 0.0)

    def per_box(pieces):
        target, near_rows = pieces
        summed = jnp.zeros((LEAF_DEV, LEAF), jnp.float32)
        for column in range(KN):
            source_rows = near_rows[:, column]
            block_tile = kernel_tile(target, points[source_rows], normals[source_rows])
            summed = summed + lax.optimization_barrier(jnp.sum(block_tile * vector[source_rows][:, None, :], axis=2))
        return summed
    near_part = lax.map(per_box, (points.reshape(BOXES, LEAF_DEV, 3, LEAF), near_list.reshape(BOXES, LEAF_DEV, KN)))
    near_part = near_part.reshape(LEAVES, LEAF)
    moments = jnp.einsum('lrp,lp->lr', leaf_basis, vector, precision=HIGH_PRECISION)
    local_field = jnp.einsum('krs,lks->lr', leaf_coupling, moments[leaf_far], precision=HIGH_PRECISION)
    transfer = leaf_to_box_transfer.reshape(BOXES, LEAF_DEV, RANK, RANK)
    box_moments = jnp.einsum('blrs,bls->br', transfer, moments.reshape(BOXES, LEAF_DEV, RANK), precision=HIGH_PRECISION)
    box_local_part = jnp.einsum('krs,bks->br', box_coupling, box_moments[box_far], precision=HIGH_PRECISION)
    local_field = local_field + jnp.einsum('blsr,bs->blr', transfer, box_local_part, precision=HIGH_PRECISION).reshape(LEAVES, RANK)
    far_part = jnp.einsum('lrp,lr->lp', leaf_basis, local_field, precision=HIGH_PRECISION)
    return jnp.where(in_use[:, None], 0.5 * vector + near_part + far_part, 0.0)

def reference(points, normals, density, counts, near_list, leaf_far, leaf_basis, leaf_to_box_transfer, leaf_coupling, box_far, box_coupling):
    slot_index = jnp.arange(LEAVES, dtype=jnp.int32)
    in_use = slot_index % LEAF_DEV < counts[slot_index // LEAF_DEV]
    unknowns = LEAF * jnp.sum(counts).astype(jnp.float32)

    def mean_product(left_side, right_side):
        return jnp.sum(left_side * right_side) / unknowns

    def apply_operator(vector):
        return operator(vector, in_use, points, normals, near_list, leaf_far, leaf_basis, leaf_to_box_transfer, leaf_coupling, box_far, box_coupling)
    initial = jnp.where(in_use[:, None], density, 0.0)
    basis_one = initial / jnp.sqrt(mean_product(initial, initial) + EPSILON)
    mapped_one = apply_operator(basis_one)
    upper_first = mean_product(basis_one, mapped_one)
    residual_one = mapped_one - upper_first * basis_one
    lower_first = jnp.sqrt(mean_product(residual_one, residual_one) + EPSILON)
    basis_two = residual_one / lower_first
    mapped_two = apply_operator(basis_two)
    upper_second = mean_product(basis_one, mapped_two)
    partial_two = mapped_two - upper_second * basis_one
    middle_second = mean_product(basis_two, partial_two)
    residual_two = partial_two - middle_second * basis_two
    lower_second = jnp.sqrt(mean_product(residual_two, residual_two) + EPSILON)
    next_basis = residual_two / lower_second
    zero_entry = jnp.zeros_like(upper_first)
    hessenberg = jnp.stack([jnp.stack([upper_first, upper_second]), jnp.stack([lower_first, middle_second]), jnp.stack([zero_entry, lower_second])])
    return (next_basis, hessenberg)
```

```python
import math

import jax
import jax.numpy as jnp
from jax import lax
from jax.sharding import PartitionSpec as P

SOFTEN = 0.05
EPSILON = 1e-06
HIGH_PRECISION = lax.Precision.HIGHEST


def from_peers(value, axis):
    size = lax.axis_size(axis)
    arrived = [
        lax.ppermute(value, axis, [(i, i ^ turn) for i in range(size)]) for turn in range(1, size)
    ]
    return [value] + arrived


def place_of(owner, axis):
    return lax.axis_index(axis) ^ owner


def tree_sum(parts):
    while len(parts) > 1:
        parts = [parts[i] + parts[i + 1] for i in range(0, len(parts), 2)]
    return parts[0]


def kernel_tile(target, source, normal):
    delta_x = source[:, 0, None, :] - target[:, 0, :, None]
    delta_y = source[:, 1, None, :] - target[:, 1, :, None]
    delta_z = source[:, 2, None, :] - target[:, 2, :, None]
    radius_sq = delta_x * delta_x + delta_y * delta_y + delta_z * delta_z + SOFTEN
    inverse = lax.rsqrt(radius_sq)
    normal_part = (
        delta_x * normal[:, 0, None, :]
        + delta_y * normal[:, 1, None, :]
        + delta_z * normal[:, 2, None, :]
    )
    return normal_part * inverse * inverse * inverse * (0.25 / math.pi)


def shards(
    points,
    normals,
    density,
    counts,
    near_list,
    leaf_far,
    leaf_basis,
    leaf_to_box_transfer,
    leaf_coupling,
    box_far,
    box_coupling,
):
    leaf_slots = points.shape[0]
    leaf_width = points.shape[2]
    rank_width = leaf_basis.shape[1]
    neighbours = near_list.shape[1]
    sub_count = lax.axis_size("sub")
    patch_start = lax.axis_index("patch") * (leaf_slots * sub_count)
    in_use = (jnp.arange(leaf_slots) < counts[0])[:, None]

    def row_of(leaf):
        leaf = leaf - patch_start
        return place_of(leaf // leaf_slots, "sub") * leaf_slots + leaf % leaf_slots

    near_rows = row_of(near_list)
    far_rows = row_of(leaf_far)
    box_rows = (
        place_of(box_far[0] // sub_count, "patch") * sub_count
        + box_far[0] % sub_count
    )

    initial = jnp.where(in_use, density, 0.0)
    geometry = jnp.concatenate([points, normals, initial[:, None]], axis=1)
    gathered = jnp.concatenate(from_peers(geometry, "sub"), axis=0)
    sources = gathered[near_rows]

    def near_field(values):
        summed = jnp.zeros((leaf_slots, leaf_width), jnp.float32)
        for column in range(neighbours):
            tile = kernel_tile(points, sources[:, column, :3], sources[:, column, 3:6])
            summed = summed + jnp.sum(tile * values[:, column, None, :], axis=2)
        return summed

    def coefficients(vector, sums):
        moments = jnp.einsum("lrp,lp->lr", leaf_basis, vector, precision=HIGH_PRECISION)
        box_moment = jnp.einsum(
            "lrs,ls->r", leaf_to_box_transfer, moments, precision=HIGH_PRECISION
        )
        row = jnp.zeros((rank_width,), jnp.float32).at[: len(sums)].set(jnp.stack(sums))
        message = jnp.concatenate([moments, box_moment[None], row[None]], axis=0)
        parts = from_peers(message, "sub")
        patch_moments = jnp.concatenate([part[:leaf_slots] for part in parts], axis=0)
        stacked = jnp.stack([part[leaf_slots] for part in parts])
        order = place_of(jnp.arange(sub_count), "sub")
        summed = tree_sum([part[leaf_slots + 1] for part in parts])
        parts = from_peers(jnp.concatenate([stacked[order], summed[None]], axis=0), "patch")
        all_boxes = jnp.concatenate([part[:sub_count] for part in parts], axis=0)
        return patch_moments, all_boxes, tree_sum([part[sub_count] for part in parts])

    def far_field(patch_moments, all_boxes):
        local_field = jnp.einsum(
            "krs,lks->lr", leaf_coupling, patch_moments[far_rows], precision=HIGH_PRECISION
        )
        box_local_part = jnp.einsum(
            "krs,ks->r", box_coupling, all_boxes[box_rows], precision=HIGH_PRECISION
        )
        local_field = local_field + jnp.einsum(
            "idc,d->ic", leaf_to_box_transfer, box_local_part, precision=HIGH_PRECISION
        )
        return jnp.einsum("lrp,lr->lp", leaf_basis, local_field, precision=HIGH_PRECISION)

    patch_moments, all_boxes, sums = coefficients(
        initial, [jnp.sum(initial * initial), counts[0].astype(jnp.float32)]
    )
    square_sum, unknowns = sums[0], leaf_width * sums[1]
    start_scale = jnp.sqrt(square_sum / unknowns + EPSILON)
    near = near_field(sources[:, :, 6])
    image = jnp.where(in_use, near + far_field(patch_moments, all_boxes), 0.0) / start_scale
    basis_one = initial / start_scale
    one_one = square_sum / (start_scale * start_scale)

    rows = jnp.concatenate(from_peers(image, "sub"), axis=0)
    patch_moments, all_boxes, sums = coefficients(
        image, [jnp.sum(basis_one * image), jnp.sum(image * image)]
    )
    along, image_sq = sums[0], sums[1]
    near = near_field(rows[near_rows])
    second = jnp.where(in_use, near + far_field(patch_moments, all_boxes), 0.0)

    upper_first = 0.5 * one_one / unknowns + along / unknowns
    shift = upper_first - 0.5
    residual_squared = image_sq - 2.0 * shift * along + shift * shift * one_one
    lower_first = jnp.sqrt(residual_squared / unknowns + EPSILON)
    basis_two = (image - shift * basis_one) / lower_first
    one_two = (along - shift * one_one) / lower_first
    two_two = residual_squared / (lower_first * lower_first)
    image_two = (second - shift * image) / lower_first

    partial = jnp.stack(
        [
            jnp.sum(basis_one * image_two),
            jnp.sum(basis_two * image_two),
            jnp.sum(image_two * image_two),
        ]
    )
    partial = jnp.zeros((8, 128), jnp.float32).at[0, :3].set(partial)
    partial = tree_sum(from_peers(partial, "sub"))
    partial = tree_sum(from_peers(partial, "patch"))
    k_one, k_two, k_sq = partial[0, 0], partial[0, 1], partial[0, 2]
    upper_second = (0.5 * one_two + k_one) / unknowns
    first_part = upper_second
    middle_second = (0.5 * two_two + k_two - upper_second * one_two) / unknowns
    second_part = middle_second - 0.5
    final_sq = (
        k_sq
        - 2.0 * first_part * k_one
        - 2.0 * second_part * k_two
        + first_part * first_part * one_one
        + 2.0 * first_part * second_part * one_two
        + second_part * second_part * two_two
    )
    lower_second = jnp.sqrt(final_sq / unknowns + EPSILON)
    basis_three = (
        image_two - first_part * basis_one - second_part * basis_two
    ) / lower_second
    zero_entry = jnp.zeros_like(upper_first)
    hessenberg = jnp.stack(
        [
            jnp.stack([upper_first, upper_second]),
            jnp.stack([lower_first, middle_second]),
            jnp.stack([zero_entry, lower_second]),
        ]
    )
    return (basis_three, hessenberg)


def solution(mesh):
    in_specs = (
        P(("groups", "patch", "sub"), None, None),
        P(("groups", "patch", "sub"), None, None),
        P(("groups", "patch", "sub"), None),
        P(("groups", "patch", "sub")),
        P(("groups", "patch", "sub"), None),
        P(("groups", "patch", "sub"), None),
        P(("groups", "patch", "sub"), None, None),
        P(("groups", "patch", "sub"), None, None),
        P(),
        P(("groups", "patch", "sub"), None),
        P(),
    )
    out_specs = (P(("groups", "patch", "sub"), None), P("groups", None))
    return jax.shard_map(shards, mesh=mesh, in_specs=in_specs, out_specs=out_specs, check_vma=False)
```

```python
import functools
import math

import jax
import jax.numpy as jnp
from jax import lax
from jax.experimental import pallas as pl
from jax.experimental.pallas import tpu as pltpu
from jax.sharding import PartitionSpec as P

SOFTEN = 0.05
EPSILON = 1e-06
KERNEL_SCALE = 0.25 / math.pi
HIGH_PRECISION = lax.Precision.HIGHEST
LANES = 128
TILE_ROWS = 8
VMEM_LIMIT = 16 << 20


def from_peers(value, axis):
    size = lax.axis_size(axis)
    arrived = [
        lax.ppermute(value, axis, [(i, i ^ turn) for i in range(size)]) for turn in range(1, size)
    ]
    return [value] + arrived


def place_of(owner, axis):
    return lax.axis_index(axis) ^ owner


def tree_sum(parts):
    while len(parts) > 1:
        parts = [parts[i] + parts[i + 1] for i in range(0, len(parts), 2)]
    return parts[0]


def device_call(kernel, outputs, scalars, arrays, scratch=()):
    smem = pl.BlockSpec(memory_space=pltpu.SMEM)
    vmem = pl.BlockSpec(memory_space=pltpu.VMEM)
    return pl.pallas_call(
        kernel,
        out_shape=tuple(outputs),
        in_specs=[smem] * len(scalars) + [vmem] * len(arrays),
        out_specs=tuple([vmem] * len(outputs)),
        scratch_shapes=tuple(scratch),
        compiler_params=pltpu.CompilerParams(vmem_limit_bytes=VMEM_LIMIT),
    )(*scalars, *arrays)


def f32(*shape):
    return jax.ShapeDtypeStruct(shape, jnp.float32)


def iota(shape, dimension):
    return lax.broadcasted_iota(jnp.int32, shape, dimension)


def split_three(value):
    first = value.astype(jnp.bfloat16).astype(jnp.float32)
    rest = value - first
    second = rest.astype(jnp.bfloat16).astype(jnp.float32)
    third = (rest - second).astype(jnp.bfloat16).astype(jnp.float32)
    return first, second, third


def lane_row(entries):
    lane = iota((1, LANES), 1)
    row = jnp.zeros((1, LANES), jnp.float32)
    for place, entry in enumerate(entries):
        row = jnp.where(lane == place, entry, row)
    return row


def pack_kernel(counts, points, normals, density, geometry, initial):
    slots, dims, width = points.shape
    used = jnp.where(iota((slots, width), 0) < counts[0], density[...], 0.0)
    initial[...] = used
    geometry[:, 0:dims, :] = points[...]
    geometry[:, dims : 2 * dims, :] = normals[...]
    geometry[:, 2 * dims, :] = used
    geometry[:, 2 * dims + 1, :] = jnp.zeros_like(used)


def write_moments(vector, sums, basis, transfer, message, start):
    slots, rank, _ = basis.shape
    lane = iota((rank, LANES), 1)
    columns = jnp.zeros((rank, LANES), jnp.float32)
    for leaf in range(slots):
        column = jnp.sum(basis[leaf] * vector[leaf : leaf + 1, :], axis=1, keepdims=True)
        columns = jnp.where(lane == leaf, column, columns)
    moments = columns.T
    end = start + slots
    message[start:end, :] = jnp.zeros((slots, LANES), jnp.float32)
    message[start:end, 0:rank] = moments[0:slots]
    box = jnp.zeros((rank, rank), jnp.float32)
    for leaf in range(slots):
        box = box + transfer[leaf] * message[start + leaf : start + leaf + 1, 0:rank]
    message[end : end + TILE_ROWS, :] = jnp.zeros((TILE_ROWS, LANES), jnp.float32)
    column = jnp.broadcast_to(jnp.sum(box, axis=1, keepdims=True), (rank, LANES))
    message[end : end + 1, 0:rank] = column.T[0:1]
    message[end + 1 : end + 2, :] = sums


def first_moments_kernel(counts, initial, basis, transfer, message):
    vector = initial[...]
    square_sum = jnp.sum(vector * vector, keepdims=True)
    in_use = jnp.full((1, 1), counts[0], jnp.int32).astype(jnp.float32)
    write_moments(initial, lane_row([square_sum, in_use]), basis, transfer, message, 0)


def leaf_part(moments, picks, coupling):
    count, rank, _ = coupling.shape
    slots = picks.shape[0] // count
    chosen = jnp.zeros((picks.shape[0], rank), jnp.float32)
    for part in split_three(jnp.concatenate(moments, axis=0)):
        chosen = chosen + jnp.dot(
            picks[...], part.astype(jnp.bfloat16), preferred_element_type=jnp.float32
        )
    local = jnp.zeros((slots, rank), jnp.float32)
    for place in range(count):
        local = local + lax.dot_general(
            chosen[place * slots : (place + 1) * slots],
            coupling[place],
            (((1,), (1,)), ((), ())),
            precision=HIGH_PRECISION,
            preferred_element_type=jnp.float32,
        )
    return local


def first_near_kernel(subs, near_rows, *refs):
    geometry, messages = refs[:subs], refs[subs : 2 * subs]
    picks, coupling, near, local, values, features, squares, fields = refs[2 * subs :]
    slots, height, width = geometry[0].shape
    neighbours = near_rows.shape[1]
    rank = coupling.shape[1]
    row = iota((height, width), 0)
    scale_square = jnp.where(row < 3, -2.0, 0.0)
    ones = jnp.where(row == 7, 1.0, 0.0)
    scale_normal = jnp.where((row >= 3) & (row < 6), -KERNEL_SCALE, 0.0)

    for sub in range(subs):
        rows = geometry[sub]
        at = [rows[:, component, :] for component in range(7)]
        squares[sub * slots : (sub + 1) * slots, :] = at[0] * at[0] + at[1] * at[1] + at[2] * at[2]
        fields[sub * slots : (sub + 1) * slots, :] = at[6]
        inner = (at[0] * at[3] + at[1] * at[4] + at[2] * at[5]) * KERNEL_SCALE
        local[...] = inner

        def source(leaf, carry, rows=rows, sub=sub):
            place = sub * slots + leaf
            plain = rows[leaf]
            square = squares[pl.ds(place, 1), :] + SOFTEN
            distance = jnp.where(row == 6, square, plain * scale_square + ones)
            numerator = jnp.where(row == 6, local[pl.ds(leaf, 1), :], plain * scale_normal)
            for part, value in enumerate((distance, numerator)):
                one, two, three = split_three(value)
                lanes = slice(part * width, (part + 1) * width)
                features[place, 0:16, lanes] = jnp.concatenate([one, two]).astype(jnp.bfloat16)
                features[place, 16:32, lanes] = jnp.concatenate([one, three]).astype(jnp.bfloat16)
            return carry

        lax.fori_loop(0, slots, source, 0, unroll=4)

    own = geometry[0]

    def target(leaf, carry):
        plain = own[leaf]
        shifted = pltpu.roll(plain, 3, 0)
        square = squares[pl.ds(leaf, 1), :]
        value = jnp.where(row < 3, plain, jnp.where(row < 6, shifted, jnp.where(row == 6, 1.0, square)))
        one, two, three = split_three(value)
        left = jnp.concatenate([one, one, two, two, three, one]).T.astype(jnp.bfloat16)
        total = jnp.zeros((width, width), jnp.float32)
        for column in range(neighbours):
            place = near_rows[leaf, column]
            upper, lower = features[place, 0:16, :], features[place, 16:32, :]
            right = jnp.concatenate([upper, upper, lower], axis=0)
            both = jnp.dot(left, right, preferred_element_type=jnp.float32)
            inverse = lax.rsqrt(both[:, 0:width])
            tile = both[:, width : 2 * width] * (inverse * inverse * inverse)
            values[leaf * neighbours + column] = tile
            total = total + tile * fields[pl.ds(place, 1), :]
        near[pl.ds(leaf, 1), :] = jnp.sum(total.T, axis=0, keepdims=True)
        return carry

    lax.fori_loop(0, slots, target, 0)
    local[...] = jnp.zeros_like(local)
    local[:, 0:rank] = leaf_part([ref[0:slots, 0:rank] for ref in messages], picks, coupling)


def second_near_kernel(subs, near_rows, *refs):
    messages = refs[:subs]
    picks, coupling, values, near, local, fields = refs[subs:]
    slots, width = near.shape
    neighbours = near_rows.shape[1]
    rank = coupling.shape[1]
    for sub in range(subs):
        fields[sub * slots : (sub + 1) * slots, :] = messages[sub][0:slots, :]

    def target(leaf, carry):
        total = jnp.zeros((width, width), jnp.float32)
        for column in range(neighbours):
            place = near_rows[leaf, column]
            total = total + values[leaf * neighbours + column] * fields[pl.ds(place, 1), :]
        near[pl.ds(leaf, 1), :] = jnp.sum(total.T, axis=0, keepdims=True)
        return carry

    lax.fori_loop(0, slots, target, 0)
    local[...] = jnp.zeros_like(local)
    local[:, 0:rank] = leaf_part(
        [ref[slots : 2 * slots, 0:rank] for ref in messages], picks, coupling
    )


def surface_sums(boxes):
    return tree_sum(
        [
            tree_sum([ref[at + 1 : at + 2, :] for at in range(0, ref.shape[0], TILE_ROWS)])
            for ref in boxes
        ]
    )


def add_far(counts, box_rows, boxes, near, local, basis, transfer, box_coupling, gather, image):
    slots, rank, width = basis.shape
    height = boxes[0].shape[0]
    for place, ref in enumerate(boxes):
        gather[place * height : (place + 1) * height, :] = ref[...]
    coupled = jnp.zeros((rank, rank), jnp.float32)
    for place in range(box_coupling.shape[0]):
        coupled = coupled + box_coupling[place] * gather[pl.ds(box_rows[place], 1), 0:rank]
    box_local = jnp.broadcast_to(jnp.sum(coupled, axis=1, keepdims=True), (rank, rank))
    for leaf in range(slots):
        local[leaf : leaf + 1, 0:rank] += jnp.sum(
            transfer[leaf] * box_local, axis=0, keepdims=True
        )
    columns = local[...].T
    for leaf in range(slots):
        far = jnp.sum(basis[leaf] * columns[0:rank, leaf : leaf + 1], axis=0, keepdims=True)
        image[leaf : leaf + 1, :] = jnp.where(
            leaf < counts[0], near[leaf : leaf + 1, :] + far, 0.0
        )


def first_image_kernel(patches, counts, box_rows, *refs):
    boxes = refs[:patches]
    near, leaf_local, initial, basis, transfer, box_coupling = refs[patches : patches + 6]
    message, basis_one, numbers, gather, image, local = refs[patches + 6 :]
    slots, _, width = basis.shape
    local[...] = leaf_local[...]
    add_far(
        counts, box_rows, boxes, near, local, basis, transfer, box_coupling, gather, image
    )
    sums = surface_sums(boxes)
    square_sum, unknowns = sums[:, 0:1], width * sums[:, 1:2]
    start_scale = jnp.sqrt(square_sum / unknowns + EPSILON)
    one_one = square_sum / (start_scale * start_scale)
    one = initial[...] / start_scale
    scaled = image[...] / start_scale
    basis_one[...] = one
    message[0:slots, :] = scaled
    numbers[...] = jnp.broadcast_to(lane_row([one_one, unknowns]), numbers.shape)
    partial = lane_row(
        [jnp.sum(one * scaled, keepdims=True), jnp.sum(scaled * scaled, keepdims=True)]
    )
    write_moments(message, partial, basis, transfer, message, slots)


def second_image_kernel(patches, counts, box_rows, *refs):
    boxes = refs[:patches]
    near, leaf_local, message, basis_one, numbers = refs[patches : patches + 5]
    basis, transfer, box_coupling = refs[patches + 5 : patches + 8]
    basis_two, image_two, partial, numbers_out, gather, image, local = refs[patches + 8 :]
    slots = basis.shape[0]
    local[...] = leaf_local[...]
    add_far(
        counts, box_rows, boxes, near, local, basis, transfer, box_coupling, gather, image
    )
    one_one, unknowns = numbers[0:1, 0:1], numbers[0:1, 1:2]
    sums = surface_sums(boxes)
    along, image_sq = sums[:, 0:1], sums[:, 1:2]
    upper_first = (0.5 * one_one + along) / unknowns
    shift = upper_first - 0.5
    residual_sq = image_sq - 2.0 * shift * along + shift * shift * one_one
    lower_first = jnp.sqrt(residual_sq / unknowns + EPSILON)
    one = basis_one[...]
    first = message[0:slots, :]
    two = (first - shift * one) / lower_first
    mapped = (image[...] - shift * first) / lower_first
    basis_two[...] = two
    image_two[...] = mapped
    one_two = (along - shift * one_one) / lower_first
    two_two = residual_sq / (lower_first * lower_first)
    numbers_out[...] = jnp.broadcast_to(
        lane_row([one_one, unknowns, upper_first, lower_first, one_two, two_two]),
        numbers_out.shape,
    )
    partial[...] = jnp.broadcast_to(
        lane_row(
            [
                jnp.sum(one * mapped, keepdims=True),
                jnp.sum(two * mapped, keepdims=True),
                jnp.sum(mapped * mapped, keepdims=True),
            ]
        ),
        partial.shape,
    )


def last_kernel(patches, *refs):
    parts = refs[:patches]
    basis_one, basis_two, image_two, numbers, basis_three, hessenberg = refs[patches:]
    sums = tree_sum([ref[0:1, :] for ref in parts])
    k_one, k_two, k_sq = sums[:, 0:1], sums[:, 1:2], sums[:, 2:3]
    one_one, unknowns, upper_first, lower_first, one_two, two_two = [
        numbers[0:1, place : place + 1] for place in range(6)
    ]
    upper_second = (0.5 * one_two + k_one) / unknowns
    middle_second = (0.5 * two_two + k_two - upper_second * one_two) / unknowns
    shift = middle_second - 0.5
    final_sq = (
        k_sq
        - 2.0 * upper_second * k_one
        - 2.0 * shift * k_two
        + upper_second * upper_second * one_one
        + 2.0 * upper_second * shift * one_two
        + shift * shift * two_two
    )
    lower_second = jnp.sqrt(final_sq / unknowns + EPSILON)
    basis_three[...] = (
        image_two[...] - upper_second * basis_one[...] - shift * basis_two[...]
    ) / lower_second
    row, column = iota(hessenberg.shape, 0), iota(hessenberg.shape, 1)
    matrix = jnp.where(column == 0, upper_first, upper_second)
    matrix = jnp.where(row == 1, jnp.where(column == 0, lower_first, middle_second), matrix)
    hessenberg[...] = jnp.where(row == 2, jnp.where(column == 0, 0.0, lower_second), matrix)


def shards(
    points,
    normals,
    density,
    counts,
    near_list,
    leaf_far,
    leaf_basis,
    leaf_to_box_transfer,
    leaf_coupling,
    box_far,
    box_coupling,
):
    slots, _, width = points.shape
    rank = leaf_basis.shape[1]
    neighbours = near_list.shape[1]
    far_count = leaf_far.shape[1]
    subs, patches = lax.axis_size("sub"), lax.axis_size("patch")
    sources = subs * slots
    patch_start = lax.axis_index("patch") * sources
    rows = f32(slots, width)

    def row_of(leaf):
        leaf = leaf - patch_start
        return place_of(leaf // slots, "sub") * slots + leaf % slots

    near_rows = row_of(near_list)
    picks = (
        row_of(leaf_far).T.reshape(far_count * slots, 1) == jnp.arange(sources)[None, :]
    ).astype(jnp.bfloat16)
    box_rows = TILE_ROWS * (
        place_of(box_far[0] // subs, "patch") * subs + place_of(box_far[0] % subs, "sub")
    )

    def box_parts(parts, start):
        return from_peers(
            jnp.concatenate([part[start : start + TILE_ROWS] for part in parts], axis=0), "patch"
        )

    geometry, initial = device_call(
        pack_kernel, [f32(slots, 8, width), rows], [counts], [points, normals, density]
    )
    geometry = from_peers(geometry, "sub")
    (message,) = device_call(
        first_moments_kernel,
        [f32(slots + TILE_ROWS, LANES)],
        [counts],
        [initial, leaf_basis, leaf_to_box_transfer],
    )
    messages = from_peers(message, "sub")
    boxes = box_parts(messages, slots)
    near, local, values = device_call(
        functools.partial(first_near_kernel, subs),
        [rows, f32(slots, LANES), pltpu.VMEM((slots * neighbours, width, width), jnp.float32)],
        [near_rows],
        [*geometry, *messages, picks, leaf_coupling],
        [
            pltpu.VMEM((sources, 32, 2 * width), jnp.bfloat16),
            pltpu.VMEM((sources, width), jnp.float32),
            pltpu.VMEM((sources, width), jnp.float32),
        ],
    )
    far_scratch = [
        pltpu.VMEM((patches * subs * TILE_ROWS, LANES), jnp.float32),
        pltpu.VMEM((slots, width), jnp.float32),
        pltpu.VMEM((slots, LANES), jnp.float32),
    ]
    message, basis_one, numbers = device_call(
        functools.partial(first_image_kernel, patches),
        [f32(2 * slots + TILE_ROWS, LANES), rows, f32(TILE_ROWS, LANES)],
        [counts, box_rows],
        [*boxes, near, local, initial, leaf_basis, leaf_to_box_transfer, box_coupling],
        far_scratch,
    )
    messages = from_peers(message, "sub")
    boxes = box_parts(messages, 2 * slots)
    near, local = device_call(
        functools.partial(second_near_kernel, subs),
        [rows, f32(slots, LANES)],
        [near_rows],
        [*messages, picks, leaf_coupling, values],
        [pltpu.VMEM((sources, width), jnp.float32)],
    )
    basis_two, image_two, partial, numbers = device_call(
        functools.partial(second_image_kernel, patches),
        [rows, rows, f32(TILE_ROWS, LANES), f32(TILE_ROWS, LANES)],
        [counts, box_rows],
        [
            *boxes,
            near,
            local,
            message,
            basis_one,
            numbers,
            leaf_basis,
            leaf_to_box_transfer,
            box_coupling,
        ],
        far_scratch,
    )
    parts = from_peers(tree_sum(from_peers(partial, "sub")), "patch")
    return device_call(
        functools.partial(last_kernel, patches),
        [rows, f32(3, 2)],
        [],
        [*parts, basis_one, basis_two, image_two, numbers],
    )


def solution(mesh):
    spread = ("groups", "patch", "sub")
    in_specs = (
        P(spread, None, None),
        P(spread, None, None),
        P(spread, None),
        P(spread),
        P(spread, None),
        P(spread, None),
        P(spread, None, None),
        P(spread, None, None),
        P(),
        P(spread, None),
        P(),
    )
    out_specs = (P(spread, None), P("groups", None))
    return jax.shard_map(shards, mesh=mesh, in_specs=in_specs, out_specs=out_specs, check_vma=False)
```

```python
import functools
import math

import jax
import jax.numpy as jnp
from jax import lax
from jax.experimental import pallas as pl
from jax.experimental.pallas import tpu as pltpu
from jax.sharding import PartitionSpec as P

SOFTEN = 0.05
EPSILON = 1e-06
KERNEL_SCALE = 0.25 / math.pi
HIGH_PRECISION = lax.Precision.HIGHEST
LANES = 128
TILE_ROWS = 8
VMEM_LIMIT = 16 << 20


def from_peers(value, axis):
    size = lax.axis_size(axis)
    arrived = [
        lax.ppermute(value, axis, [(i, i ^ turn) for i in range(size)]) for turn in range(1, size)
    ]
    return [value] + arrived


def place_of(owner, axis):
    return lax.axis_index(axis) ^ owner


def tree_sum(parts):
    while len(parts) > 1:
        parts = [parts[i] + parts[i + 1] for i in range(0, len(parts), 2)]
    return parts[0]


def device_call(kernel, outputs, scalars, arrays, scratch=(), remote=()):
    smem = pl.BlockSpec(memory_space=pltpu.SMEM)
    vmem = pl.BlockSpec(memory_space=pltpu.VMEM)
    hbm = pl.BlockSpec(memory_space=pltpu.HBM)
    return pl.pallas_call(
        kernel,
        out_shape=tuple(outputs),
        in_specs=[smem] * len(scalars) + [vmem] * len(arrays) + [hbm] * len(remote),
        out_specs=tuple([vmem] * len(outputs)),
        scratch_shapes=tuple(scratch),
        compiler_params=pltpu.CompilerParams(vmem_limit_bytes=VMEM_LIMIT),
    )(*scalars, *arrays, *remote)


def kept(array):
    return pltpu.VMEM(array.shape, array.dtype)


def f32(*shape):
    return jax.ShapeDtypeStruct(shape, jnp.float32)


def iota(shape, dimension):
    return lax.broadcasted_iota(jnp.int32, shape, dimension)


def split_three(value):
    first = value.astype(jnp.bfloat16).astype(jnp.float32)
    rest = value - first
    second = rest.astype(jnp.bfloat16).astype(jnp.float32)
    third = (rest - second).astype(jnp.bfloat16).astype(jnp.float32)
    return first, second, third


def lane_row(entries):
    lane = iota((1, LANES), 1)
    row = jnp.zeros((1, LANES), jnp.float32)
    for place, entry in enumerate(entries):
        row = jnp.where(lane == place, entry, row)
    return row


def pack_kernel(counts, points, normals, density, geometry, initial, at, arrived):
    dims, slots, width = points.shape
    copies = [
        pltpu.make_async_copy(points, at.at[0:dims], arrived.at[0]),
        pltpu.make_async_copy(normals, at.at[dims : 2 * dims], arrived.at[1]),
        pltpu.make_async_copy(density, at.at[2 * dims], arrived.at[2]),
    ]
    for copy in copies:
        copy.start()
    for copy in copies:
        copy.wait()
    for row in range(2 * dims):
        geometry[:, row, :] = at[row]
    used = jnp.where(iota((slots, width), 0) < counts[0], at[2 * dims], 0.0)
    initial[...] = used
    geometry[:, 2 * dims, :] = used
    geometry[:, 2 * dims + 1, :] = jnp.zeros_like(used)


def write_moments(vector, sums, basis, transfer, message, start):
    slots, rank, _ = basis.shape
    lane = iota((rank, LANES), 1)
    columns = jnp.zeros((rank, LANES), jnp.float32)
    for leaf in range(slots):
        column = jnp.sum(basis[leaf] * vector[leaf : leaf + 1, :], axis=1, keepdims=True)
        columns = jnp.where(lane == leaf, column, columns)
    moments = columns.T
    end = start + slots
    message[start:end, :] = jnp.zeros((slots, LANES), jnp.float32)
    message[start:end, 0:rank] = moments[0:slots]
    box = jnp.zeros((rank, rank), jnp.float32)
    for leaf in range(slots):
        box = box + transfer[leaf] * message[start + leaf : start + leaf + 1, 0:rank]
    message[end : end + TILE_ROWS, :] = jnp.zeros((TILE_ROWS, LANES), jnp.float32)
    column = jnp.broadcast_to(jnp.sum(box, axis=1, keepdims=True), (rank, LANES))
    message[end : end + 1, 0:rank] = column.T[0:1]
    message[end + 1 : end + 2, :] = sums


def first_moments_kernel(counts, initial, *refs):
    sources, message, held, arrived = refs[:4], refs[4], refs[5:9], refs[9]
    copies = [
        pltpu.make_async_copy(source, target, arrived.at[place])
        for place, (source, target) in enumerate(zip(sources, held))
    ]
    for copy in copies:
        copy.start()
    for copy in copies:
        copy.wait()
    vector = initial[...]
    square_sum = jnp.sum(vector * vector, keepdims=True)
    in_use = jnp.full((1, 1), counts[0], jnp.int32).astype(jnp.float32)
    write_moments(initial, lane_row([square_sum, in_use]), held[0], held[1], message, 0)


def leaf_part(moments, picks, coupling):
    count, rank, _ = coupling.shape
    slots = picks.shape[0] // count
    chosen = jnp.zeros((picks.shape[0], rank), jnp.float32)
    for part in split_three(jnp.concatenate(moments, axis=0)):
        chosen = chosen + jnp.dot(
            picks[...], part.astype(jnp.bfloat16), preferred_element_type=jnp.float32
        )
    local = jnp.zeros((slots, rank), jnp.float32)
    for place in range(count):
        local = local + lax.dot_general(
            chosen[place * slots : (place + 1) * slots],
            coupling[place],
            (((1,), (1,)), ((), ())),
            precision=HIGH_PRECISION,
            preferred_element_type=jnp.float32,
        )
    return local


def first_near_kernel(subs, offset, near_list, *refs):
    geometry, messages = refs[:subs], refs[subs : 2 * subs]
    picks, coupling, near, local, values, features, squares, fields = refs[2 * subs :]
    slots, height, width = geometry[0].shape
    neighbours = near_list.shape[0]
    rank = coupling.shape[1]
    row = iota((height, width), 0)
    scale_square = jnp.where(row < 3, -2.0, 0.0)
    ones = jnp.where(row == 7, 1.0, 0.0)
    scale_normal = jnp.where((row >= 3) & (row < 6), -KERNEL_SCALE, 0.0)

    for sub in range(subs):
        rows = geometry[sub]
        at = [rows[:, component, :] for component in range(7)]
        squares[sub * slots : (sub + 1) * slots, :] = at[0] * at[0] + at[1] * at[1] + at[2] * at[2]
        fields[sub * slots : (sub + 1) * slots, :] = at[6]
        inner = (at[0] * at[3] + at[1] * at[4] + at[2] * at[5]) * KERNEL_SCALE
        local[...] = inner

        def source(leaf, carry, rows=rows, sub=sub):
            place = sub * slots + leaf
            plain = rows[leaf]
            square = squares[pl.ds(place, 1), :] + SOFTEN
            distance = jnp.where(row == 6, square, plain * scale_square + ones)
            numerator = jnp.where(row == 6, local[pl.ds(leaf, 1), :], plain * scale_normal)
            for part, value in enumerate((distance, numerator)):
                one, two, three = split_three(value)
                lanes = slice(part * width, (part + 1) * width)
                features[place, 0:16, lanes] = jnp.concatenate([one, two]).astype(jnp.bfloat16)
                features[place, 16:32, lanes] = jnp.concatenate([one, three]).astype(jnp.bfloat16)
            return carry

        lax.fori_loop(0, slots, source, 0, unroll=4)

    own = geometry[0]

    def target(leaf, carry):
        plain = own[leaf]
        shifted = pltpu.roll(plain, 3, 0)
        square = squares[pl.ds(leaf, 1), :]
        value = jnp.where(row < 3, plain, jnp.where(row < 6, shifted, jnp.where(row == 6, 1.0, square)))
        one, two, three = split_three(value)
        left = jnp.concatenate([one, one, two, two, three, one]).T.astype(jnp.bfloat16)
        total = jnp.zeros((width, width), jnp.float32)
        for column in range(neighbours):
            place = near_list[column, leaf] ^ offset[0]
            upper, lower = features[place, 0:16, :], features[place, 16:32, :]
            right = jnp.concatenate([upper, upper, lower], axis=0)
            both = jnp.dot(left, right, preferred_element_type=jnp.float32)
            inverse = lax.rsqrt(both[:, 0:width])
            tile = both[:, width : 2 * width] * (inverse * inverse * inverse)
            values[leaf * neighbours + column] = tile
            total = total + tile * fields[pl.ds(place, 1), :]
        near[pl.ds(leaf, 1), :] = jnp.sum(total.T, axis=0, keepdims=True)
        return carry

    lax.fori_loop(0, slots, target, 0, unroll=True)
    local[...] = jnp.zeros_like(local)
    local[:, 0:rank] = leaf_part([ref[0:slots, 0:rank] for ref in messages], picks, coupling)


def second_near_kernel(subs, offset, near_list, *refs):
    messages = refs[:subs]
    picks, coupling, values, near, local, fields = refs[subs:]
    slots, width = near.shape
    neighbours = near_list.shape[0]
    rank = coupling.shape[1]
    for sub in range(subs):
        fields[sub * slots : (sub + 1) * slots, :] = messages[sub][0:slots, :]

    def target(leaf, carry):
        total = jnp.zeros((width, width), jnp.float32)
        for column in range(neighbours):
            place = near_list[column, leaf] ^ offset[0]
            total = total + values[leaf * neighbours + column] * fields[pl.ds(place, 1), :]
        near[pl.ds(leaf, 1), :] = jnp.sum(total.T, axis=0, keepdims=True)
        return carry

    lax.fori_loop(0, slots, target, 0, unroll=True)
    local[...] = jnp.zeros_like(local)
    local[:, 0:rank] = leaf_part(
        [ref[slots : 2 * slots, 0:rank] for ref in messages], picks, coupling
    )


def surface_sums(boxes):
    return tree_sum(
        [
            tree_sum([ref[at + 1 : at + 2, :] for at in range(0, ref.shape[0], TILE_ROWS)])
            for ref in boxes
        ]
    )


def add_far(counts, box_rows, boxes, near, local, basis, transfer, box_coupling, gather, image):
    slots, rank, width = basis.shape
    height = boxes[0].shape[0]
    for place, ref in enumerate(boxes):
        gather[place * height : (place + 1) * height, :] = ref[...]
    coupled = jnp.zeros((rank, rank), jnp.float32)
    for place in range(box_coupling.shape[0]):
        coupled = coupled + box_coupling[place] * gather[pl.ds(box_rows[place], 1), 0:rank]
    box_local = jnp.broadcast_to(jnp.sum(coupled, axis=1, keepdims=True), (rank, rank))
    for leaf in range(slots):
        local[leaf : leaf + 1, 0:rank] += jnp.sum(
            transfer[leaf] * box_local, axis=0, keepdims=True
        )
    columns = local[...].T
    for leaf in range(slots):
        far = jnp.sum(basis[leaf] * columns[0:rank, leaf : leaf + 1], axis=0, keepdims=True)
        image[leaf : leaf + 1, :] = jnp.where(
            leaf < counts[0], near[leaf : leaf + 1, :] + far, 0.0
        )


def first_image_kernel(patches, counts, box_rows, *refs):
    boxes = refs[:patches]
    near, leaf_local, initial, basis, transfer, box_coupling = refs[patches : patches + 6]
    message, basis_one, numbers, gather, image, local = refs[patches + 6 :]
    slots, _, width = basis.shape
    local[...] = leaf_local[...]
    add_far(
        counts, box_rows, boxes, near, local, basis, transfer, box_coupling, gather, image
    )
    sums = surface_sums(boxes)
    square_sum, unknowns = sums[:, 0:1], width * sums[:, 1:2]
    start_scale = jnp.sqrt(square_sum / unknowns + EPSILON)
    one_one = square_sum / (start_scale * start_scale)
    one = initial[...] / start_scale
    scaled = image[...] / start_scale
    basis_one[...] = one
    message[0:slots, :] = scaled
    numbers[...] = jnp.broadcast_to(lane_row([one_one, unknowns]), numbers.shape)
    partial = lane_row(
        [jnp.sum(one * scaled, keepdims=True), jnp.sum(scaled * scaled, keepdims=True)]
    )
    write_moments(message, partial, basis, transfer, message, slots)


def second_image_kernel(patches, counts, box_rows, *refs):
    boxes = refs[:patches]
    near, leaf_local, message, basis_one, numbers = refs[patches : patches + 5]
    basis, transfer, box_coupling = refs[patches + 5 : patches + 8]
    basis_two, image_two, partial, numbers_out, gather, image, local = refs[patches + 8 :]
    slots = basis.shape[0]
    local[...] = leaf_local[...]
    add_far(
        counts, box_rows, boxes, near, local, basis, transfer, box_coupling, gather, image
    )
    one_one, unknowns = numbers[0:1, 0:1], numbers[0:1, 1:2]
    sums = surface_sums(boxes)
    along, image_sq = sums[:, 0:1], sums[:, 1:2]
    upper_first = (0.5 * one_one + along) / unknowns
    shift = upper_first - 0.5
    residual_sq = image_sq - 2.0 * shift * along + shift * shift * one_one
    lower_first = jnp.sqrt(residual_sq / unknowns + EPSILON)
    one = basis_one[...]
    first = message[0:slots, :]
    two = (first - shift * one) / lower_first
    mapped = (image[...] - shift * first) / lower_first
    basis_two[...] = two
    image_two[...] = mapped
    one_two = (along - shift * one_one) / lower_first
    two_two = residual_sq / (lower_first * lower_first)
    numbers_out[...] = jnp.broadcast_to(
        lane_row([one_one, unknowns, upper_first, lower_first, one_two, two_two]),
        numbers_out.shape,
    )
    partial[...] = jnp.broadcast_to(
        lane_row(
            [
                jnp.sum(one * mapped, keepdims=True),
                jnp.sum(two * mapped, keepdims=True),
                jnp.sum(mapped * mapped, keepdims=True),
            ]
        ),
        partial.shape,
    )


def last_kernel(parts, basis_one, basis_two, image_two, numbers, basis_three, hessenberg):
    sums = jnp.sum(parts[...], axis=0, keepdims=True)
    k_one, k_two, k_sq = sums[:, 0:1], sums[:, 1:2], sums[:, 2:3]
    one_one, unknowns, upper_first, lower_first, one_two, two_two = [
        numbers[0:1, place : place + 1] for place in range(6)
    ]
    upper_second = (0.5 * one_two + k_one) / unknowns
    middle_second = (0.5 * two_two + k_two - upper_second * one_two) / unknowns
    shift = middle_second - 0.5
    final_sq = (
        k_sq
        - 2.0 * upper_second * k_one
        - 2.0 * shift * k_two
        + upper_second * upper_second * one_one
        + 2.0 * upper_second * shift * one_two
        + shift * shift * two_two
    )
    lower_second = jnp.sqrt(final_sq / unknowns + EPSILON)
    basis_three[...] = (
        image_two[...] - upper_second * basis_one[...] - shift * basis_two[...]
    ) / lower_second
    column, row = iota(hessenberg.shape, 0), iota(hessenberg.shape, 1)
    matrix = jnp.where(column == 0, upper_first, upper_second)
    matrix = jnp.where(row == 1, jnp.where(column == 0, lower_first, middle_second), matrix)
    hessenberg[...] = jnp.where(row == 2, jnp.where(column == 0, 0.0, lower_second), matrix)


def shards(
    points,
    normals,
    density,
    counts,
    near_list,
    leaf_far,
    leaf_basis,
    leaf_to_box_transfer,
    leaf_coupling,
    box_far,
    box_coupling,
):
    slots, _, width = points.shape
    rank = leaf_basis.shape[1]
    neighbours = near_list.shape[1]
    far_count = leaf_far.shape[1]
    subs, patches = lax.axis_size("sub"), lax.axis_size("patch")
    sources = subs * slots
    patch_start = lax.axis_index("patch") * sources
    rows = f32(slots, width)

    offset = patch_start + lax.axis_index("sub") * slots
    offsets = offset.reshape(1).astype(jnp.int32)
    near_list = near_list.T
    picks = (
        leaf_far.T.reshape(far_count * slots, 1) == (jnp.arange(sources) ^ offset)[None, :]
    ).astype(jnp.bfloat16)
    box_rows = TILE_ROWS * (
        place_of(box_far[0] // subs, "patch") * subs + place_of(box_far[0] % subs, "sub")
    )

    def box_parts(parts, start):
        return from_peers(
            jnp.concatenate([part[start : start + TILE_ROWS] for part in parts], axis=0), "patch"
        )

    geometry, initial = device_call(
        pack_kernel,
        [f32(slots, 8, width), rows],
        [counts],
        [],
        [pltpu.VMEM((7, slots, width), jnp.float32), pltpu.SemaphoreType.DMA((3,))],
        [points.transpose(1, 0, 2), normals.transpose(1, 0, 2), density],
    )
    geometry = from_peers(geometry, "sub")
    matrices = [leaf_basis, leaf_to_box_transfer, leaf_coupling, box_coupling]
    message, leaf_basis, leaf_to_box_transfer, leaf_coupling, box_coupling = device_call(
        first_moments_kernel,
        [f32(slots + TILE_ROWS, LANES), *[kept(matrix) for matrix in matrices]],
        [counts],
        [initial],
        [pltpu.SemaphoreType.DMA((4,))],
        matrices,
    )
    messages = from_peers(message, "sub")
    boxes = box_parts(messages, slots)
    near, local, values = device_call(
        functools.partial(first_near_kernel, subs),
        [rows, f32(slots, LANES), pltpu.VMEM((slots * neighbours, width, width), jnp.float32)],
        [offsets, near_list],
        [*geometry, *messages, picks, leaf_coupling],
        [
            pltpu.VMEM((sources, 32, 2 * width), jnp.bfloat16),
            pltpu.VMEM((sources, width), jnp.float32),
            pltpu.VMEM((sources, width), jnp.float32),
        ],
    )
    far_scratch = [
        pltpu.VMEM((patches * subs * TILE_ROWS, LANES), jnp.float32),
        pltpu.VMEM((slots, width), jnp.float32),
        pltpu.VMEM((slots, LANES), jnp.float32),
    ]
    message, basis_one, numbers = device_call(
        functools.partial(first_image_kernel, patches),
        [f32(2 * slots + TILE_ROWS, LANES), rows, f32(TILE_ROWS, LANES)],
        [counts, box_rows],
        [*boxes, near, local, initial, leaf_basis, leaf_to_box_transfer, box_coupling],
        far_scratch,
    )
    messages = from_peers(message, "sub")
    boxes = box_parts(messages, 2 * slots)
    near, local = device_call(
        functools.partial(second_near_kernel, subs),
        [rows, f32(slots, LANES)],
        [offsets, near_list],
        [*messages, picks, leaf_coupling, values],
        [pltpu.VMEM((sources, width), jnp.float32)],
    )
    basis_two, image_two, partial, numbers = device_call(
        functools.partial(second_image_kernel, patches),
        [rows, rows, f32(patches * subs, LANES), f32(TILE_ROWS, LANES)],
        [counts, box_rows],
        [
            *boxes,
            near,
            local,
            message,
            basis_one,
            numbers,
            leaf_basis,
            leaf_to_box_transfer,
            box_coupling,
        ],
        far_scratch,
    )
    parts = lax.all_to_all(partial, ("patch", "sub"), 0, 0, tiled=True)
    basis_three, hessenberg = device_call(
        last_kernel, [rows, f32(2, 3)], [], [parts, basis_one, basis_two, image_two, numbers]
    )
    return basis_three, hessenberg.T


def solution(mesh):
    spread = ("groups", "patch", "sub")
    in_specs = (
        P(spread, None, None),
        P(spread, None, None),
        P(spread, None),
        P(spread),
        P(spread, None),
        P(spread, None),
        P(spread, None, None),
        P(spread, None, None),
        P(),
        P(spread, None),
        P(),
    )
    out_specs = (P(spread, None), P("groups", None))
    return jax.shard_map(shards, mesh=mesh, in_specs=in_specs, out_specs=out_specs, check_vma=False)
```

```python
import functools
import math

import jax
import jax.numpy as jnp
from jax import lax
from jax.experimental import pallas as pl
from jax.experimental.pallas import tpu as pltpu
from jax.sharding import PartitionSpec as P

SOFTEN = 0.05
EPSILON = 1e-06
KERNEL_SCALE = 0.25 / math.pi
HIGH_PRECISION = lax.Precision.HIGHEST
LANES = 128
TILE_ROWS = 8
VMEM_LIMIT = 16 << 20


def from_peers(value, axis):
    size = lax.axis_size(axis)
    arrived = [
        lax.ppermute(value, axis, [(i, i ^ turn) for i in range(size)]) for turn in range(1, size)
    ]
    return [value] + arrived


def tree_sum(parts):
    while len(parts) > 1:
        parts = [parts[i] + parts[i + 1] for i in range(0, len(parts), 2)]
    return parts[0]


def device_call(kernel, outputs, scalars, arrays, scratch=(), remote=()):
    smem = pl.BlockSpec(memory_space=pltpu.SMEM)
    vmem = pl.BlockSpec(memory_space=pltpu.VMEM)
    hbm = pl.BlockSpec(memory_space=pltpu.HBM)
    return pl.pallas_call(
        kernel,
        out_shape=tuple(outputs),
        in_specs=[smem] * len(scalars) + [vmem] * len(arrays) + [hbm] * len(remote),
        out_specs=tuple([vmem] * len(outputs)),
        scratch_shapes=tuple(scratch),
        compiler_params=pltpu.CompilerParams(vmem_limit_bytes=VMEM_LIMIT),
    )(
        *scalars,
        *arrays,
        *[pltpu.with_memory_space_constraint(array, pltpu.HBM) for array in remote],
    )


def kept(array):
    return pltpu.VMEM(array.shape, array.dtype)


def f32(*shape):
    return jax.ShapeDtypeStruct(shape, jnp.float32)


def iota(shape, dimension):
    return lax.broadcasted_iota(jnp.int32, shape, dimension)


def split_three(value):
    first = value.astype(jnp.bfloat16).astype(jnp.float32)
    rest = value - first
    second = rest.astype(jnp.bfloat16).astype(jnp.float32)
    third = (rest - second).astype(jnp.bfloat16).astype(jnp.float32)
    return first, second, third


def lane_row(entries):
    lane = iota((1, LANES), 1)
    row = jnp.zeros((1, LANES), jnp.float32)
    for place, entry in enumerate(entries):
        row = jnp.where(lane == place, entry, row)
    return row


def write_moments(vector, sums, basis, transfer, message, start):
    slots, rank, _ = basis.shape
    lane = iota((rank, LANES), 1)
    columns = jnp.zeros((rank, LANES), jnp.float32)
    for leaf in range(slots):
        column = jnp.sum(basis[leaf] * vector[leaf : leaf + 1, :], axis=1, keepdims=True)
        columns = jnp.where(lane == leaf, column, columns)
    moments = columns.T
    end = start + slots
    message[start:end, :] = jnp.zeros((slots, LANES), jnp.float32)
    message[start:end, 0:rank] = moments[0:slots]
    box = jnp.zeros((rank, rank), jnp.float32)
    for leaf in range(slots):
        box = box + transfer[leaf] * message[start + leaf : start + leaf + 1, 0:rank]
    message[end : end + TILE_ROWS, :] = jnp.zeros((TILE_ROWS, LANES), jnp.float32)
    column = jnp.broadcast_to(jnp.sum(box, axis=1, keepdims=True), (rank, LANES))
    message[end : end + 1, 0:rank] = column.T[0:1]
    message[end + 1 : end + 2, :] = sums


def start_kernel(counts, *refs):
    sources, (geometry, initial, message), held = refs[:7], refs[7:10], refs[10:14]
    at, arrived = refs[14:]
    dims, slots, width = sources[0].shape
    targets = [at.at[0:dims], at.at[dims : 2 * dims], at.at[2 * dims], *held]
    copies = [
        pltpu.make_async_copy(source, target, arrived.at[place])
        for place, (source, target) in enumerate(zip(sources, targets))
    ]
    for copy in copies:
        copy.start()
    for copy in copies[:3]:
        copy.wait()
    for row in range(2 * dims):
        geometry[:, row, :] = at[row]
    vector = jnp.where(iota((slots, width), 0) < counts[0], at[2 * dims], 0.0)
    initial[...] = vector
    geometry[:, 2 * dims, :] = vector
    geometry[:, 2 * dims + 1, :] = jnp.zeros_like(vector)
    square_sum = jnp.sum(vector * vector, keepdims=True)
    in_use = jnp.full((1, 1), counts[0], jnp.int32).astype(jnp.float32)
    for copy in copies[3:]:
        copy.wait()
    write_moments(initial, lane_row([square_sum, in_use]), held[0], held[1], message, 0)


def leaf_part(moments, picks, coupling):
    count, rank, _ = coupling.shape
    slots = picks.shape[0] // count
    chosen = jnp.zeros((picks.shape[0], rank), jnp.float32)
    for part in split_three(jnp.concatenate(moments, axis=0)):
        chosen = chosen + jnp.dot(
            picks[...], part.astype(jnp.bfloat16), preferred_element_type=jnp.float32
        )
    local = jnp.zeros((slots, rank), jnp.float32)
    for place in range(count):
        local = local + lax.dot_general(
            chosen[place * slots : (place + 1) * slots],
            coupling[place],
            (((1,), (1,)), ((), ())),
            precision=HIGH_PRECISION,
            preferred_element_type=jnp.float32,
        )
    return local


def first_near_kernel(subs, box, *refs):
    geometry, messages = refs[:subs], refs[subs : 2 * subs]
    picks, coupling, near_source, near, local, values = refs[2 * subs : 2 * subs + 6]
    features, squares, fields, near_list, arrived = refs[2 * subs + 6 :]
    copy = pltpu.make_async_copy(near_source, near_list, arrived)
    copy.start()
    slots, height, width = geometry[0].shape
    neighbours = near_list.shape[0]
    rank = coupling.shape[1]
    row = iota((height, width), 0)
    scale_square = jnp.where(row < 3, -2.0, 0.0)
    ones = jnp.where(row == 7, 1.0, 0.0)
    scale_normal = jnp.where((row >= 3) & (row < 6), -KERNEL_SCALE, 0.0)

    for sub in range(subs):
        rows = geometry[sub]
        at = [rows[:, component, :] for component in range(7)]
        squares[sub * slots : (sub + 1) * slots, :] = at[0] * at[0] + at[1] * at[1] + at[2] * at[2]
        fields[sub * slots : (sub + 1) * slots, :] = at[6]
        inner = (at[0] * at[3] + at[1] * at[4] + at[2] * at[5]) * KERNEL_SCALE
        local[...] = inner

        def source(leaf, carry, rows=rows, sub=sub):
            place = sub * slots + leaf
            plain = rows[leaf]
            square = squares[pl.ds(place, 1), :] + SOFTEN
            distance = jnp.where(row == 6, square, plain * scale_square + ones)
            numerator = jnp.where(row == 6, local[pl.ds(leaf, 1), :], plain * scale_normal)
            for part, value in enumerate((distance, numerator)):
                one, two, three = split_three(value)
                lanes = slice(part * width, (part + 1) * width)
                features[place, 0:16, lanes] = jnp.concatenate([one, two]).astype(jnp.bfloat16)
                features[place, 16:32, lanes] = jnp.concatenate([one, three]).astype(jnp.bfloat16)
            return carry

        lax.fori_loop(0, slots, source, 0, unroll=4)

    own = geometry[0]

    def target(leaf, carry):
        plain = own[leaf]
        shifted = pltpu.roll(plain, 3, 0)
        square = squares[pl.ds(leaf, 1), :]
        value = jnp.where(row < 3, plain, jnp.where(row < 6, shifted, jnp.where(row == 6, 1.0, square)))
        one, two, three = split_three(value)
        left = jnp.concatenate([one, one, two, two, three, one]).T.astype(jnp.bfloat16)
        total = jnp.zeros((width, width), jnp.float32)
        for column in range(neighbours):
            place = near_list[column, leaf] ^ (box[0] * slots)
            upper, lower = features[place, 0:16, :], features[place, 16:32, :]
            right = jnp.concatenate([upper, upper, lower], axis=0)
            both = jnp.dot(left, right, preferred_element_type=jnp.float32)
            inverse = lax.rsqrt(both[:, 0:width])
            tile = both[:, width : 2 * width] * (inverse * inverse * inverse)
            values[leaf * neighbours + column] = tile
            total = total + tile * fields[pl.ds(place, 1), :]
        near[pl.ds(leaf, 1), :] = jnp.sum(total.T, axis=0, keepdims=True)
        return carry

    copy.wait()
    lax.fori_loop(0, slots, target, 0, unroll=True)
    local[...] = jnp.zeros_like(local)
    local[:, 0:rank] = leaf_part([ref[0:slots, 0:rank] for ref in messages], picks, coupling)


def second_near_kernel(subs, box, *refs):
    messages = refs[:subs]
    picks, coupling, values, near_source, near, local, fields, near_list, arrived = refs[subs:]
    copy = pltpu.make_async_copy(near_source, near_list, arrived)
    copy.start()
    slots, width = near.shape
    neighbours = near_list.shape[0]
    rank = coupling.shape[1]
    for sub in range(subs):
        fields[sub * slots : (sub + 1) * slots, :] = messages[sub][0:slots, :]

    def target(leaf, carry):
        total = jnp.zeros((width, width), jnp.float32)
        for column in range(neighbours):
            place = near_list[column, leaf] ^ (box[0] * slots)
            total = total + values[leaf * neighbours + column] * fields[pl.ds(place, 1), :]
        near[pl.ds(leaf, 1), :] = jnp.sum(total.T, axis=0, keepdims=True)
        return carry

    local[...] = jnp.zeros_like(local)
    local[:, 0:rank] = leaf_part(
        [ref[slots : 2 * slots, 0:rank] for ref in messages], picks, coupling
    )
    copy.wait()
    lax.fori_loop(0, slots, target, 0, unroll=True)


def surface_sums(boxes):
    return tree_sum(
        [
            tree_sum([ref[at + 1 : at + 2, :] for at in range(0, ref.shape[0], TILE_ROWS)])
            for ref in boxes
        ]
    )


def add_far(counts, box, box_far, boxes, near, local, basis, transfer, box_coupling, gather, image):
    slots, rank, width = basis.shape
    height = boxes[0].shape[0]
    for place, ref in enumerate(boxes):
        gather[place * height : (place + 1) * height, :] = ref[...]
    coupled = jnp.zeros((rank, rank), jnp.float32)
    for place in range(box_coupling.shape[0]):
        row = (box_far[0, place] ^ box[0]) * TILE_ROWS
        coupled = coupled + box_coupling[place] * gather[pl.ds(row, 1), 0:rank]
    box_local = jnp.broadcast_to(jnp.sum(coupled, axis=1, keepdims=True), (rank, rank))
    for leaf in range(slots):
        local[leaf : leaf + 1, 0:rank] += jnp.sum(
            transfer[leaf] * box_local, axis=0, keepdims=True
        )
    columns = local[...].T
    for leaf in range(slots):
        far = jnp.sum(basis[leaf] * columns[0:rank, leaf : leaf + 1], axis=0, keepdims=True)
        image[leaf : leaf + 1, :] = jnp.where(
            leaf < counts[0], near[leaf : leaf + 1, :] + far, 0.0
        )


def first_image_kernel(patches, counts, box, box_far, *refs):
    boxes = refs[:patches]
    near, leaf_local, initial, basis, transfer, box_coupling = refs[patches : patches + 6]
    message, basis_one, numbers, gather, image, local = refs[patches + 6 :]
    slots, _, width = basis.shape
    local[...] = leaf_local[...]
    add_far(
        counts, box, box_far, boxes, near, local, basis, transfer, box_coupling, gather, image
    )
    sums = surface_sums(boxes)
    square_sum, unknowns = sums[:, 0:1], width * sums[:, 1:2]
    start_scale = jnp.sqrt(square_sum / unknowns + EPSILON)
    one_one = square_sum / (start_scale * start_scale)
    one = initial[...] / start_scale
    scaled = image[...] / start_scale
    basis_one[...] = one
    message[0:slots, :] = scaled
    numbers[...] = jnp.broadcast_to(lane_row([one_one, unknowns]), numbers.shape)
    partial = lane_row(
        [jnp.sum(one * scaled, keepdims=True), jnp.sum(scaled * scaled, keepdims=True)]
    )
    write_moments(message, partial, basis, transfer, message, slots)


def second_image_kernel(patches, counts, box, box_far, *refs):
    boxes = refs[:patches]
    near, leaf_local, message, basis_one, numbers = refs[patches : patches + 5]
    basis, transfer, box_coupling = refs[patches + 5 : patches + 8]
    basis_two, image_two, partial, numbers_out, gather, image, local = refs[patches + 8 :]
    slots = basis.shape[0]
    local[...] = leaf_local[...]
    add_far(
        counts, box, box_far, boxes, near, local, basis, transfer, box_coupling, gather, image
    )
    one_one, unknowns = numbers[0:1, 0:1], numbers[0:1, 1:2]
    sums = surface_sums(boxes)
    along, image_sq = sums[:, 0:1], sums[:, 1:2]
    upper_first = (0.5 * one_one + along) / unknowns
    shift = upper_first - 0.5
    residual_sq = image_sq - 2.0 * shift * along + shift * shift * one_one
    lower_first = jnp.sqrt(residual_sq / unknowns + EPSILON)
    one = basis_one[...]
    first = message[0:slots, :]
    two = (first - shift * one) / lower_first
    mapped = (image[...] - shift * first) / lower_first
    basis_two[...] = two
    image_two[...] = mapped
    one_two = (along - shift * one_one) / lower_first
    two_two = residual_sq / (lower_first * lower_first)
    numbers_out[...] = jnp.broadcast_to(
        lane_row([one_one, unknowns, upper_first, lower_first, one_two, two_two]),
        numbers_out.shape,
    )
    partial[...] = jnp.broadcast_to(
        lane_row(
            [
                jnp.sum(one * mapped, keepdims=True),
                jnp.sum(two * mapped, keepdims=True),
                jnp.sum(mapped * mapped, keepdims=True),
            ]
        ),
        partial.shape,
    )


def last_kernel(parts, basis_one, basis_two, image_two, numbers, basis_three, hessenberg):
    sums = jnp.sum(parts[...], axis=0, keepdims=True)
    k_one, k_two, k_sq = sums[:, 0:1], sums[:, 1:2], sums[:, 2:3]
    one_one, unknowns, upper_first, lower_first, one_two, two_two = [
        numbers[0:1, place : place + 1] for place in range(6)
    ]
    upper_second = (0.5 * one_two + k_one) / unknowns
    middle_second = (0.5 * two_two + k_two - upper_second * one_two) / unknowns
    shift = middle_second - 0.5
    final_sq = (
        k_sq
        - 2.0 * upper_second * k_one
        - 2.0 * shift * k_two
        + upper_second * upper_second * one_one
        + 2.0 * upper_second * shift * one_two
        + shift * shift * two_two
    )
    lower_second = jnp.sqrt(final_sq / unknowns + EPSILON)
    basis_three[...] = (
        image_two[...] - upper_second * basis_one[...] - shift * basis_two[...]
    ) / lower_second
    column, row = iota(hessenberg.shape, 0), iota(hessenberg.shape, 1)
    matrix = jnp.where(column == 0, upper_first, upper_second)
    matrix = jnp.where(row == 1, jnp.where(column == 0, lower_first, middle_second), matrix)
    hessenberg[...] = jnp.where(row == 2, jnp.where(column == 0, 0.0, lower_second), matrix)


def shards(
    points,
    normals,
    density,
    counts,
    near_list,
    leaf_far,
    leaf_basis,
    leaf_to_box_transfer,
    leaf_coupling,
    box_far,
    box_coupling,
):
    slots, _, width = points.shape
    neighbours = near_list.shape[1]
    far_count = leaf_far.shape[1]
    subs, patches = lax.axis_size("sub"), lax.axis_size("patch")
    sources = subs * slots
    rows = f32(slots, width)
    this_box = lax.axis_index("patch") * subs + lax.axis_index("sub")
    box = this_box.astype(jnp.int32).reshape(1)
    patch_start = lax.axis_index("patch") * sources
    leaves = (jnp.arange(sources) + patch_start) ^ (lax.axis_index("sub") * slots)
    picks = (leaf_far.T.reshape(far_count * slots, 1) == leaves[None, :]).astype(jnp.bfloat16)

    def box_parts(parts, start):
        return from_peers(
            jnp.concatenate([part[start : start + TILE_ROWS] for part in parts], axis=0), "patch"
        )

    matrices = [leaf_basis, leaf_to_box_transfer, leaf_coupling, box_coupling]
    geometry, initial, message, *matrices = device_call(
        start_kernel,
        [
            f32(slots, 8, width),
            rows,
            f32(slots + TILE_ROWS, LANES),
            *[kept(matrix) for matrix in matrices],
        ],
        [counts],
        [],
        [pltpu.VMEM((7, slots, width), jnp.float32), pltpu.SemaphoreType.DMA((7,))],
        [points.transpose(1, 0, 2), normals.transpose(1, 0, 2), density, *matrices],
    )
    leaf_basis, leaf_to_box_transfer, leaf_coupling, box_coupling = matrices
    near_list = near_list.T
    list_scratch = [
        pltpu.SMEM(near_list.shape, jnp.int32),
        pltpu.SemaphoreType.DMA,
    ]
    geometry = from_peers(geometry, "sub")
    messages = from_peers(message, "sub")
    boxes = box_parts(messages, slots)
    near, local, values = device_call(
        functools.partial(first_near_kernel, subs),
        [rows, f32(slots, LANES), pltpu.VMEM((slots * neighbours, width, width), jnp.float32)],
        [box],
        [*geometry, *messages, picks, leaf_coupling],
        [
            pltpu.VMEM((sources, 32, 2 * width), jnp.bfloat16),
            pltpu.VMEM((sources, width), jnp.float32),
            pltpu.VMEM((sources, width), jnp.float32),
            *list_scratch,
        ],
        [near_list],
    )
    far_scratch = [
        pltpu.VMEM((patches * subs * TILE_ROWS, LANES), jnp.float32),
        pltpu.VMEM((slots, width), jnp.float32),
        pltpu.VMEM((slots, LANES), jnp.float32),
    ]
    message, basis_one, numbers = device_call(
        functools.partial(first_image_kernel, patches),
        [f32(2 * slots + TILE_ROWS, LANES), rows, f32(TILE_ROWS, LANES)],
        [counts, box, box_far],
        [*boxes, near, local, initial, leaf_basis, leaf_to_box_transfer, box_coupling],
        far_scratch,
    )
    messages = from_peers(message, "sub")
    boxes = box_parts(messages, 2 * slots)
    near, local = device_call(
        functools.partial(second_near_kernel, subs),
        [rows, f32(slots, LANES)],
        [box],
        [*messages, picks, leaf_coupling, values],
        [pltpu.VMEM((sources, width), jnp.float32), *list_scratch],
        [near_list],
    )
    basis_two, image_two, partial, numbers = device_call(
        functools.partial(second_image_kernel, patches),
        [rows, rows, f32(patches * subs, LANES), f32(TILE_ROWS, LANES)],
        [counts, box, box_far],
        [
            *boxes,
            near,
            local,
            message,
            basis_one,
            numbers,
            leaf_basis,
            leaf_to_box_transfer,
            box_coupling,
        ],
        far_scratch,
    )
    parts = lax.all_to_all(partial, ("patch", "sub"), 0, 0, tiled=True)
    basis_three, hessenberg = device_call(
        last_kernel, [rows, f32(2, 3)], [], [parts, basis_one, basis_two, image_two, numbers]
    )
    return basis_three, hessenberg.T


def solution(mesh):
    spread = ("groups", "patch", "sub")
    in_specs = (
        P(spread, None, None),
        P(spread, None, None),
        P(spread, None),
        P(spread),
        P(spread, None),
        P(spread, None),
        P(spread, None, None),
        P(spread, None, None),
        P(),
        P(spread, None),
        P(),
    )
    out_specs = (P(spread, None), P("groups", None))
    return jax.shard_map(shards, mesh=mesh, in_specs=in_specs, out_specs=out_specs, check_vma=False)
```

```python
import functools
import math

import jax
import jax.numpy as jnp
from jax import lax
from jax.experimental import pallas as pl
from jax.experimental.pallas import tpu as pltpu
from jax.sharding import PartitionSpec as P

SOFTEN = 0.05
EPSILON = 1e-06
KERNEL_SCALE = 0.25 / math.pi
HIGH_PRECISION = lax.Precision.HIGHEST
LANES = 128
TILE_ROWS = 8
VMEM_LIMIT = 16 << 20


def from_peers(value, axis):
    size = lax.axis_size(axis)
    arrived = [
        lax.ppermute(value, axis, [(i, i ^ turn) for i in range(size)]) for turn in range(1, size)
    ]
    return [value] + arrived


def tree_sum(parts):
    while len(parts) > 1:
        parts = [parts[i] + parts[i + 1] for i in range(0, len(parts), 2)]
    return parts[0]


def device_call(kernel, outputs, scalars, arrays, scratch=(), remote=()):
    smem = pl.BlockSpec(memory_space=pltpu.SMEM)
    vmem = pl.BlockSpec(memory_space=pltpu.VMEM)
    hbm = pl.BlockSpec(memory_space=pltpu.HBM)
    return pl.pallas_call(
        kernel,
        out_shape=tuple(outputs),
        in_specs=[smem] * len(scalars) + [vmem] * len(arrays) + [hbm] * len(remote),
        out_specs=tuple([vmem] * len(outputs)),
        scratch_shapes=tuple(scratch),
        compiler_params=pltpu.CompilerParams(vmem_limit_bytes=VMEM_LIMIT),
    )(
        *scalars,
        *arrays,
        *[pltpu.with_memory_space_constraint(array, pltpu.HBM) for array in remote],
    )


def kept(array):
    return pltpu.VMEM(array.shape, array.dtype)


def f32(*shape):
    return jax.ShapeDtypeStruct(shape, jnp.float32)


def iota(shape, dimension):
    return lax.broadcasted_iota(jnp.int32, shape, dimension)


def split_three(value):
    first = value.astype(jnp.bfloat16).astype(jnp.float32)
    rest = value - first
    second = rest.astype(jnp.bfloat16).astype(jnp.float32)
    third = (rest - second).astype(jnp.bfloat16).astype(jnp.float32)
    return first, second, third


def lane_row(entries):
    lane = iota((1, LANES), 1)
    row = jnp.zeros((1, LANES), jnp.float32)
    for place, entry in enumerate(entries):
        row = jnp.where(lane == place, entry, row)
    return row


def copy_all(pairs, arrived):
    copies = [
        pltpu.make_async_copy(source, target, arrived.at[place])
        for place, (source, target) in enumerate(pairs)
    ]
    for copy in copies:
        copy.start()
    return copies


def start_kernel(counts, points, normals, density, geometry, initial, at, arrived):
    dims, slots, width = points.shape
    targets = [at.at[0:dims], at.at[dims : 2 * dims], at.at[2 * dims]]
    for copy in copy_all(zip((points, normals, density), targets), arrived):
        copy.wait()
    for row in range(2 * dims):
        geometry[:, row, :] = at[row]
    vector = jnp.where(iota((slots, width), 0) < counts[0], at[2 * dims], 0.0)
    initial[...] = vector
    geometry[:, 2 * dims, :] = vector
    geometry[:, 2 * dims + 1, :] = jnp.zeros_like(vector)


def write_moments(vector, basis, message, start):
    slots, rank, _ = basis.shape
    lane = iota((rank, LANES), 1)
    columns = jnp.zeros((rank, LANES), jnp.float32)
    for leaf in range(slots):
        column = jnp.sum(basis[leaf] * vector[leaf : leaf + 1, :], axis=1, keepdims=True)
        columns = jnp.where(lane == leaf, column, columns)
    message[start : start + slots, :] = jnp.zeros((slots, LANES), jnp.float32)
    message[start : start + slots, 0:rank] = columns.T[0:slots]


def box_moments(vector, box_basis):
    slots, rank, width = box_basis.shape
    total = jnp.zeros((rank, width), jnp.float32)
    for leaf in range(slots):
        total = total + box_basis[leaf] * vector[leaf : leaf + 1, :]
    column = jnp.sum(total, axis=1, keepdims=True)
    diagonal = iota((rank, LANES), 0) == iota((rank, LANES), 1)
    return jnp.sum(jnp.where(diagonal, column, 0.0), axis=0, keepdims=True)


def six_products(left, right, contract):
    one, two, three = [part.astype(jnp.bfloat16) for part in split_three(right)]
    parts = jnp.concatenate(split_three(left)).astype(jnp.bfloat16)
    rows = left.shape[0]

    def product(count, other):
        return lax.dot_general(
            parts[0 : count * rows],
            other,
            (contract, ((), ())),
            preferred_element_type=jnp.float32,
        )

    first, second, third = product(3, one), product(2, two), product(1, three)
    return first[0:rows] + (
        (first[rows : 2 * rows] + second[0:rows])
        + (first[2 * rows : 3 * rows] + second[rows : 2 * rows] + third)
    )


def basis_kernel(counts, box_far, initial, *refs):
    sources, message, box_basis, (basis, leaf_coupling, box_coupling) = (
        refs[:4],
        refs[4],
        refs[5],
        refs[6:9],
    )
    transfer, arrived = refs[9:]
    slots, rank, _ = basis.shape
    targets = (basis, transfer, leaf_coupling, box_coupling)
    copies = copy_all(zip(sources, targets), arrived)
    for copy in copies:
        copy.wait()
    gram = jnp.zeros((rank, rank), jnp.float32)
    for leaf in range(slots):
        product = jnp.dot(
            transfer[leaf],
            basis[leaf],
            precision=HIGH_PRECISION,
            preferred_element_type=jnp.float32,
        )
        product = jnp.where(leaf < counts[0], product, 0.0)
        box_basis[leaf] = product
        gram = gram + six_products(product, product, ((1,), (1,)))
    write_moments(initial, basis, message, 0)
    vector = initial[...]
    entries = [jnp.sum(vector * vector, keepdims=True)] + [
        jnp.full((1, 1), value, jnp.int32).astype(jnp.float32)
        for value in [counts[0]] + [box_far[0, place] for place in range(box_far.shape[1])]
    ]
    message[slots : slots + TILE_ROWS, :] = jnp.zeros((TILE_ROWS, LANES), jnp.float32)
    message[slots : slots + 1, :] = box_moments(initial, box_basis)
    message[slots + 1 : slots + 2, :] = lane_row(entries)
    start, half = slots + TILE_ROWS, rank // 2
    message[start : start + half, 0:rank] = gram[0:half]
    message[start : start + half, rank : 2 * rank] = gram[half:rank]


def leaf_part(moments, picks, coupling):
    count, rank, _ = coupling.shape
    slots = picks.shape[0] // count
    chosen = jnp.zeros((picks.shape[0], rank), jnp.float32)
    for part in split_three(jnp.concatenate(moments, axis=0)):
        chosen = chosen + jnp.dot(
            picks[...], part.astype(jnp.bfloat16), preferred_element_type=jnp.float32
        )
    local = jnp.zeros((slots, rank), jnp.float32)
    for place in range(count):
        local = local + lax.dot_general(
            chosen[place * slots : (place + 1) * slots],
            coupling[place],
            (((1,), (1,)), ((), ())),
            precision=HIGH_PRECISION,
            preferred_element_type=jnp.float32,
        )
    return local


def add_leaf_far(counts, moments, picks, coupling, basis, near):
    slots, rank, width = basis.shape
    local = leaf_part(moments, picks, coupling)
    columns = jnp.concatenate([local, jnp.zeros((slots, LANES - rank), jnp.float32)], axis=1).T
    for leaf in range(slots):
        far = jnp.sum(basis[leaf] * columns[0:rank, leaf : leaf + 1], axis=0, keepdims=True)
        near[leaf : leaf + 1, :] = jnp.where(
            leaf < counts[0], near[leaf : leaf + 1, :] + far, 0.0
        )


def first_near_kernel(subs, box, counts, *refs):
    geometry, messages = refs[:subs], refs[subs : 2 * subs]
    picks, coupling, basis, near_source, near, values = refs[2 * subs : 2 * subs + 6]
    features, squares, fields, inner, near_list, arrived = refs[2 * subs + 6 :]
    copy = pltpu.make_async_copy(near_source, near_list, arrived)
    copy.start()
    slots, height, width = geometry[0].shape
    neighbours = near_list.shape[0]
    rank = coupling.shape[1]
    row = iota((height, width), 0)
    scale_square = jnp.where(row < 3, -2.0, 0.0)
    ones = jnp.where(row == 7, 1.0, 0.0)
    scale_normal = jnp.where((row >= 3) & (row < 6), -KERNEL_SCALE, 0.0)

    for sub in range(subs):
        rows = geometry[sub]
        at = [rows[:, component, :] for component in range(7)]
        squares[sub * slots : (sub + 1) * slots, :] = at[0] * at[0] + at[1] * at[1] + at[2] * at[2]
        fields[sub * slots : (sub + 1) * slots, :] = at[6]
        inner[...] = (at[0] * at[3] + at[1] * at[4] + at[2] * at[5]) * KERNEL_SCALE

        def source(leaf, carry, rows=rows, sub=sub):
            place = sub * slots + leaf
            plain = rows[leaf]
            square = squares[pl.ds(place, 1), :] + SOFTEN
            distance = jnp.where(row == 6, square, plain * scale_square + ones)
            numerator = jnp.where(row == 6, inner[pl.ds(leaf, 1), :], plain * scale_normal)
            for part, value in enumerate((distance, numerator)):
                one, two, three = split_three(value)
                lanes = slice(part * width, (part + 1) * width)
                features[place, 0:16, lanes] = jnp.concatenate([one, two]).astype(jnp.bfloat16)
                features[place, 16:32, lanes] = jnp.concatenate([one, three]).astype(jnp.bfloat16)
            return carry

        lax.fori_loop(0, slots, source, 0, unroll=4)

    own = geometry[0]

    def target(leaf, carry):
        plain = own[leaf]
        shifted = pltpu.roll(plain, 3, 0)
        square = squares[pl.ds(leaf, 1), :]
        value = jnp.where(row < 3, plain, jnp.where(row < 6, shifted, jnp.where(row == 6, 1.0, square)))
        one, two, three = split_three(value)
        left = jnp.concatenate([one, one, two, two, three, one]).T.astype(jnp.bfloat16)
        total = jnp.zeros((width, width), jnp.float32)
        for column in range(neighbours):
            place = near_list[column, leaf] ^ (box[0] * slots)
            upper, lower = features[place, 0:16, :], features[place, 16:32, :]
            right = jnp.concatenate([upper, upper, lower], axis=0)
            both = jnp.dot(left, right, preferred_element_type=jnp.float32)
            inverse = lax.rsqrt(both[:, 0:width])
            tile = both[:, width : 2 * width] * (inverse * inverse * inverse)
            values[leaf * neighbours + column] = tile
            total = total + tile * fields[pl.ds(place, 1), :]
        near[pl.ds(leaf, 1), :] = jnp.sum(total.T, axis=0, keepdims=True)
        return carry

    copy.wait()
    lax.fori_loop(0, slots, target, 0, unroll=True)
    moments = [ref[0:slots, 0:rank] for ref in messages]
    add_leaf_far(counts, moments, picks, coupling, basis, near)


def box_images(box_basis, coefficients, image):
    slots, rank, width = box_basis.shape
    spread = jnp.broadcast_to(coefficients, (rank, width))
    for leaf in range(slots):
        image[leaf : leaf + 1, :] += jnp.sum(box_basis[leaf] * spread, axis=0, keepdims=True)


def first_image_kernel(patches, span, box, box_far, *refs):
    boxes = refs[:patches]
    part, initial, basis, box_basis, box_coupling = refs[patches : patches + 5]
    message, basis_one, numbers, gather, image = refs[patches + 5 :]
    slots, rank, width = basis.shape
    height = boxes[0].shape[0]
    for place, ref in enumerate(boxes):
        gather[place * height : (place + 1) * height, :] = ref[...]
    coupled = jnp.zeros((rank, rank), jnp.float32)
    for place in range(box_coupling.shape[0]):
        row = (box_far[0, place] ^ box[0]) * span
        coupled = coupled + box_coupling[place] * gather[pl.ds(row, 1), 0:rank]
    image[...] = part[...]
    box_images(box_basis, jnp.sum(coupled, axis=1, keepdims=True), image)
    sums = tree_sum(
        [
            tree_sum([ref[at + 1 : at + 2, :] for at in range(0, height, span)])
            for ref in boxes
        ]
    )
    square_sum, unknowns = sums[:, 0:1], width * sums[:, 1:2]
    start_scale = jnp.sqrt(square_sum / unknowns + EPSILON)
    one_one = square_sum / (start_scale * start_scale)
    basis_one[...] = initial[...] / start_scale
    message[0:slots, :] = image[...] / start_scale
    numbers[...] = jnp.broadcast_to(lane_row([one_one, unknowns, start_scale]), numbers.shape)
    write_moments(message, basis, message, slots)


def second_near_kernel(subs, box, counts, *refs):
    messages = refs[:subs]
    picks, coupling, basis, box_basis, basis_one, values, near_source = refs[subs : subs + 7]
    part, shares, fields, near_list, arrived = refs[subs + 7 :]
    copy = pltpu.make_async_copy(near_source, near_list, arrived)
    copy.start()
    slots, width = part.shape
    neighbours = near_list.shape[0]
    rank = coupling.shape[1]
    for sub in range(subs):
        fields[sub * slots : (sub + 1) * slots, :] = messages[sub][0:slots, :]

    def target(leaf, carry):
        total = jnp.zeros((width, width), jnp.float32)
        for column in range(neighbours):
            place = near_list[column, leaf] ^ (box[0] * slots)
            total = total + values[leaf * neighbours + column] * fields[pl.ds(place, 1), :]
        part[pl.ds(leaf, 1), :] = jnp.sum(total.T, axis=0, keepdims=True)
        return carry

    copy.wait()
    lax.fori_loop(0, slots, target, 0, unroll=True)
    moments = [ref[slots : 2 * slots, 0:rank] for ref in messages]
    add_leaf_far(counts, moments, picks, coupling, basis, part)
    first, one, second = messages[0][0:slots, :], basis_one[...], part[...]
    products = [one * first, first * first, one * second, first * second, second * second]
    sums = lane_row([jnp.sum(product, keepdims=True) for product in products])
    lane = iota((1, LANES), 1)
    both = jnp.where(
        lane < rank,
        box_moments(messages[0], box_basis),
        pltpu.roll(box_moments(part, box_basis), rank, 1),
    )
    shares[...] = jnp.where(iota(shares.shape, 0) % 2 == 0, both, sums)


def last_kernel(patches, span, box, *refs):
    boxes, (shares, message, basis_one, part, numbers) = refs[:patches], refs[patches : patches + 5]
    box_basis, box_coupling = refs[patches + 5 : patches + 7]
    basis_three, hessenberg, gather, starts, lists, pairs, image = refs[patches + 7 :]
    slots, rank, width = box_basis.shape
    height = boxes[0].shape[0]
    count = patches * (height // span)
    for place, ref in enumerate(boxes):
        gather[place * height : (place + 1) * height, :] = ref[...]
    for other in range(count):
        row = (box[0] ^ other) * span
        starts[other : other + 1, :] = gather[pl.ds(row, 1), :]
        lists[other : other + 1, :] = gather[pl.ds(row + 1, 1), :]
        pairs[other : other + 1, :] = shares[2 * other : 2 * other + 1, :]
        pairs[count + other : count + other + 1, :] = shares[2 * other + 1 : 2 * other + 2, :]
    first_box, second_box = pairs[0:count, 0:rank], pairs[0:count, rank : 2 * rank]
    parts = [part.astype(jnp.bfloat16) for part in split_three(first_box)]
    lane = iota((count, count), 1).astype(jnp.float32)
    box_local = jnp.zeros((count, rank), jnp.float32)
    for place in range(box_coupling.shape[0]):
        pick = jnp.where(lists[:, 2 + place : 3 + place] == lane, 1.0, 0.0).astype(jnp.bfloat16)
        chosen = jnp.zeros((count, rank), jnp.float32)
        for split in parts:
            chosen = chosen + jnp.dot(pick, split, preferred_element_type=jnp.float32)
        box_local = box_local + lax.dot_general(
            chosen,
            box_coupling[place],
            (((1,), (1,)), ((), ())),
            precision=HIGH_PRECISION,
            preferred_element_type=jnp.float32,
        )
    twice = jnp.concatenate([box_local, box_local], axis=1)
    columns = twice.T
    half = rank // 2
    low = iota((half, 2 * rank), 1) < rank
    quadratic = jnp.zeros((half, 2 * rank), jnp.float32)
    for other in range(count):
        row = (box[0] ^ other) * span + TILE_ROWS
        column = jnp.where(
            low, columns[0:half, other : other + 1], columns[half:rank, other : other + 1]
        )
        quadratic = quadratic + gather[pl.ds(row, half), :] * twice[other : other + 1, :] * column
    one_one, unknowns, start_scale = [numbers[0:1, place : place + 1] for place in range(3)]
    sums = jnp.sum(pairs[count : 2 * count, :], axis=0, keepdims=True)
    along, image_sq, one_part, first_part, part_sq = [
        sums[:, place : place + 1] for place in range(5)
    ]
    one_second = (
        one_part + jnp.sum(starts[:, 0:rank] * box_local, keepdims=True) / start_scale
    )
    first_second = first_part + jnp.sum(first_box * box_local, keepdims=True)
    second_sq = (
        part_sq
        + 2.0 * jnp.sum(second_box * box_local, keepdims=True)
        + jnp.sum(quadratic, keepdims=True)
    )
    upper_first = (0.5 * one_one + along) / unknowns
    shift = upper_first - 0.5
    residual_sq = image_sq - 2.0 * shift * along + shift * shift * one_one
    lower_first = jnp.sqrt(residual_sq / unknowns + EPSILON)
    one_two = (along - shift * one_one) / lower_first
    two_two = residual_sq / (lower_first * lower_first)
    k_one = (one_second - shift * along) / lower_first
    k_two = (
        (first_second - shift * image_sq) - shift * (one_second - shift * along)
    ) / (lower_first * lower_first)
    k_sq = (second_sq - 2.0 * shift * first_second + shift * shift * image_sq) / (
        lower_first * lower_first
    )
    upper_second = (0.5 * one_two + k_one) / unknowns
    middle_second = (0.5 * two_two + k_two - upper_second * one_two) / unknowns
    turn = middle_second - 0.5
    final_sq = (
        k_sq
        - 2.0 * upper_second * k_one
        - 2.0 * turn * k_two
        + upper_second * upper_second * one_one
        + 2.0 * upper_second * turn * one_two
        + turn * turn * two_two
    )
    lower_second = jnp.sqrt(final_sq / unknowns + EPSILON)
    image[...] = part[...]
    own = jnp.where(iota((rank, count), 1) == box[0], columns[0:rank], 0.0)
    box_images(box_basis, jnp.sum(own, axis=1, keepdims=True), image)
    one, first = basis_one[...], message[0:slots, :]
    two = (first - shift * one) / lower_first
    mapped = (image[...] - shift * first) / lower_first
    basis_three[...] = (mapped - upper_second * one - turn * two) / lower_second
    column, row = iota(hessenberg.shape, 0), iota(hessenberg.shape, 1)
    matrix = jnp.where(column == 0, upper_first, upper_second)
    matrix = jnp.where(row == 1, jnp.where(column == 0, lower_first, middle_second), matrix)
    hessenberg[...] = jnp.where(row == 2, jnp.where(column == 0, 0.0, lower_second), matrix)


def shards(
    points,
    normals,
    density,
    counts,
    near_list,
    leaf_far,
    leaf_basis,
    leaf_to_box_transfer,
    leaf_coupling,
    box_far,
    box_coupling,
):
    slots, _, width = points.shape
    neighbours = near_list.shape[1]
    far_count = leaf_far.shape[1]
    subs, patches = lax.axis_size("sub"), lax.axis_size("patch")
    sources = subs * slots
    rows = f32(slots, width)
    this_box = lax.axis_index("patch") * subs + lax.axis_index("sub")
    box = this_box.astype(jnp.int32).reshape(1)
    patch_start = lax.axis_index("patch") * sources
    leaves = (jnp.arange(sources) + patch_start) ^ (lax.axis_index("sub") * slots)
    picks = (leaf_far.T.reshape(far_count * slots, 1) == leaves[None, :]).astype(jnp.bfloat16)

    rank = leaf_basis.shape[1]
    span = TILE_ROWS + rank // 2
    near_list = near_list.T
    list_scratch = [pltpu.SMEM(near_list.shape, jnp.int32), pltpu.SemaphoreType.DMA]
    block = pltpu.VMEM((sources, width), jnp.float32)

    geometry, initial = device_call(
        start_kernel,
        [f32(slots, 8, width), rows],
        [counts],
        [],
        [pltpu.VMEM((7, slots, width), jnp.float32), pltpu.SemaphoreType.DMA((3,))],
        [points.transpose(1, 0, 2), normals.transpose(1, 0, 2), density],
    )
    geometry = from_peers(geometry, "sub")
    message, box_basis, leaf_basis, leaf_coupling, box_coupling = device_call(
        basis_kernel,
        [
            f32(slots + span, LANES),
            kept(leaf_basis),
            kept(leaf_basis),
            kept(leaf_coupling),
            kept(box_coupling),
        ],
        [counts, box_far],
        [initial],
        [
            pltpu.VMEM(leaf_to_box_transfer.shape, jnp.float32),
            pltpu.SemaphoreType.DMA((4,)),
        ],
        [leaf_basis, leaf_to_box_transfer, leaf_coupling, box_coupling],
    )
    messages = from_peers(message, "sub")
    boxes = from_peers(
        jnp.concatenate([part[slots : slots + span] for part in messages], axis=0), "patch"
    )
    gather = pltpu.VMEM((patches * subs * span, LANES), jnp.float32)
    part, values = device_call(
        functools.partial(first_near_kernel, subs),
        [rows, pltpu.VMEM((slots * neighbours, width, width), jnp.float32)],
        [box, counts],
        [*geometry, *messages, picks, leaf_coupling, leaf_basis],
        [
            pltpu.VMEM((sources, 32, 2 * width), jnp.bfloat16),
            block,
            block,
            pltpu.VMEM((slots, width), jnp.float32),
            *list_scratch,
        ],
        [near_list],
    )
    message, basis_one, numbers = device_call(
        functools.partial(first_image_kernel, patches, span),
        [f32(2 * slots, LANES), rows, f32(TILE_ROWS, LANES)],
        [box, box_far],
        [*boxes, part, initial, leaf_basis, box_basis, box_coupling],
        [gather, pltpu.VMEM((slots, width), jnp.float32)],
    )
    messages = from_peers(message, "sub")
    part, shares = device_call(
        functools.partial(second_near_kernel, subs),
        [rows, f32(2 * patches * subs, LANES)],
        [box, counts],
        [*messages, picks, leaf_coupling, leaf_basis, box_basis, basis_one, values],
        [block, *list_scratch],
        [near_list],
    )
    shares = lax.all_to_all(shares, ("patch", "sub"), 0, 0, tiled=True)
    basis_three, hessenberg = device_call(
        functools.partial(last_kernel, patches, span),
        [rows, f32(2, 3)],
        [box],
        [*boxes, shares, message, basis_one, part, numbers, box_basis, box_coupling],
        [
            gather,
            pltpu.VMEM((patches * subs, LANES), jnp.float32),
            pltpu.VMEM((patches * subs, LANES), jnp.float32),
            pltpu.VMEM((2 * patches * subs, LANES), jnp.float32),
            pltpu.VMEM((slots, width), jnp.float32),
        ],
    )
    return basis_three, hessenberg.T


def solution(mesh):
    spread = ("groups", "patch", "sub")
    in_specs = (
        P(spread, None, None),
        P(spread, None, None),
        P(spread, None),
        P(spread),
        P(spread, None),
        P(spread, None),
        P(spread, None, None),
        P(spread, None, None),
        P(),
        P(spread, None),
        P(),
    )
    out_specs = (P(spread, None), P("groups", None))
    return jax.shard_map(shards, mesh=mesh, in_specs=in_specs, out_specs=out_specs, check_vma=False)
```

```python
import functools
import math

import jax
import jax.numpy as jnp
from jax import lax
from jax.experimental import pallas as pl
from jax.experimental.pallas import tpu as pltpu
from jax.sharding import PartitionSpec as P

SOFTEN = 0.05
EPSILON = 1e-06
KERNEL_SCALE = 0.25 / math.pi
HIGH_PRECISION = lax.Precision.HIGHEST
LANES = 128
TILE_ROWS = 8
VMEM_LIMIT = 16 << 20


def from_peers(value, axis):
    size = lax.axis_size(axis)
    arrived = [
        lax.ppermute(value, axis, [(i, i ^ turn) for i in range(size)]) for turn in range(1, size)
    ]
    return [value] + arrived


def tree_sum(parts):
    while len(parts) > 1:
        parts = [parts[i] + parts[i + 1] for i in range(0, len(parts), 2)]
    return parts[0]


def device_call(kernel, outputs, scalars, arrays, scratch=(), remote=()):
    smem = pl.BlockSpec(memory_space=pltpu.SMEM)
    vmem = pl.BlockSpec(memory_space=pltpu.VMEM)
    hbm = pl.BlockSpec(memory_space=pltpu.HBM)
    return pl.pallas_call(
        kernel,
        out_shape=tuple(outputs),
        in_specs=[smem] * len(scalars) + [vmem] * len(arrays) + [hbm] * len(remote),
        out_specs=tuple([vmem] * len(outputs)),
        scratch_shapes=tuple(scratch),
        compiler_params=pltpu.CompilerParams(vmem_limit_bytes=VMEM_LIMIT),
    )(
        *scalars,
        *arrays,
        *[pltpu.with_memory_space_constraint(array, pltpu.HBM) for array in remote],
    )


def kept(array):
    return pltpu.VMEM(array.shape, array.dtype)


def f32(*shape):
    return jax.ShapeDtypeStruct(shape, jnp.float32)


def iota(shape, dimension):
    return lax.broadcasted_iota(jnp.int32, shape, dimension)


def split_three(value):
    first = value.astype(jnp.bfloat16).astype(jnp.float32)
    rest = value - first
    second = rest.astype(jnp.bfloat16).astype(jnp.float32)
    third = (rest - second).astype(jnp.bfloat16).astype(jnp.float32)
    return first, second, third


def lane_row(entries):
    lane = iota((1, LANES), 1)
    row = jnp.zeros((1, LANES), jnp.float32)
    for place, entry in enumerate(entries):
        row = jnp.where(lane == place, entry, row)
    return row


def copy_all(pairs, arrived):
    copies = [
        pltpu.make_async_copy(source, target, arrived.at[place])
        for place, (source, target) in enumerate(pairs)
    ]
    for copy in copies:
        copy.start()
    return copies


def write_moments(vector, basis, message, start):
    slots, rank, _ = basis.shape
    lane = iota((rank, LANES), 1)
    columns = jnp.zeros((rank, LANES), jnp.float32)
    for leaf in range(slots):
        column = jnp.sum(basis[leaf] * vector[leaf : leaf + 1, :], axis=1, keepdims=True)
        columns = jnp.where(lane == leaf, column, columns)
    message[start : start + slots, :] = jnp.zeros((slots, LANES), jnp.float32)
    message[start : start + slots, 0:rank] = columns.T[0:slots]


def box_moments(vector, box_basis):
    slots, rank, width = box_basis.shape
    total = jnp.zeros((rank, width), jnp.float32)
    for leaf in range(slots):
        total = total + box_basis[leaf] * vector[leaf : leaf + 1, :]
    column = jnp.sum(total, axis=1, keepdims=True)
    diagonal = iota((rank, LANES), 0) == iota((rank, LANES), 1)
    return jnp.sum(jnp.where(diagonal, column, 0.0), axis=0, keepdims=True)


def six_products(left, right, contract):
    one, two, three = [part.astype(jnp.bfloat16) for part in split_three(right)]
    parts = jnp.concatenate(split_three(left)).astype(jnp.bfloat16)
    rows = left.shape[0]

    def product(count, other):
        return lax.dot_general(
            parts[0 : count * rows],
            other,
            (contract, ((), ())),
            preferred_element_type=jnp.float32,
        )

    first, second, third = product(3, one), product(2, two), product(1, three)
    return first[0:rows] + (
        (first[rows : 2 * rows] + second[0:rows])
        + (first[2 * rows : 3 * rows] + second[rows : 2 * rows] + third)
    )


def start_kernel(counts, box_far, *refs):
    sources, (geometry, initial, message, box_basis) = refs[:7], refs[7:11]
    basis, leaf_coupling, box_coupling = refs[11:14]
    at, transfer, arrived = refs[14:]
    dims, slots, width = sources[0].shape
    rank = basis.shape[1]
    targets = [at.at[0:dims], at.at[dims : 2 * dims], at.at[2 * dims]]
    targets += [transfer, basis, leaf_coupling, box_coupling]
    copies = copy_all(zip(sources, targets), arrived)
    for copy in copies[:3]:
        copy.wait()
    for row in range(2 * dims):
        geometry[:, row, :] = at[row]
    vector = jnp.where(iota((slots, width), 0) < counts[0], at[2 * dims], 0.0)
    initial[...] = vector
    geometry[:, 2 * dims, :] = vector
    geometry[:, 2 * dims + 1, :] = jnp.zeros_like(vector)
    entries = [jnp.sum(vector * vector, keepdims=True)] + [
        jnp.full((1, 1), value, jnp.int32).astype(jnp.float32)
        for value in [counts[0]] + [box_far[place] for place in range(box_far.shape[0])]
    ]
    message[slots : slots + TILE_ROWS, :] = jnp.zeros((TILE_ROWS, LANES), jnp.float32)
    message[slots + 1 : slots + 2, :] = lane_row(entries)
    for copy in copies[3:]:
        copy.wait()
    gram = jnp.zeros((rank, rank), jnp.float32)
    for leaf in range(slots):
        product = jnp.dot(
            transfer[leaf],
            basis[leaf],
            precision=HIGH_PRECISION,
            preferred_element_type=jnp.float32,
        )
        product = jnp.where(leaf < counts[0], product, 0.0)
        box_basis[leaf] = product
        gram = gram + six_products(product, product, ((1,), (1,)))
    write_moments(initial, basis, message, 0)
    message[slots : slots + 1, :] = box_moments(initial, box_basis)
    start, half = slots + TILE_ROWS, rank // 2
    message[start : start + half, 0:rank] = gram[0:half]
    message[start : start + half, rank : 2 * rank] = gram[half:rank]


def leaf_part(moments, picks, coupling):
    count, rank, _ = coupling.shape
    slots = picks.shape[0] // count
    chosen = jnp.zeros((picks.shape[0], rank), jnp.float32)
    for part in split_three(jnp.concatenate(moments, axis=0)):
        chosen = chosen + jnp.dot(
            picks[...], part.astype(jnp.bfloat16), preferred_element_type=jnp.float32
        )
    local = jnp.zeros((slots, rank), jnp.float32)
    for place in range(count):
        local = local + lax.dot_general(
            chosen[place * slots : (place + 1) * slots],
            coupling[place],
            (((1,), (1,)), ((), ())),
            precision=HIGH_PRECISION,
            preferred_element_type=jnp.float32,
        )
    return local


def add_leaf_far(counts, moments, picks, coupling, basis, near):
    slots, rank, width = basis.shape
    local = leaf_part(moments, picks, coupling)
    columns = jnp.concatenate([local, jnp.zeros((slots, LANES - rank), jnp.float32)], axis=1).T
    for leaf in range(slots):
        far = jnp.sum(basis[leaf] * columns[0:rank, leaf : leaf + 1], axis=0, keepdims=True)
        near[leaf : leaf + 1, :] = jnp.where(
            leaf < counts[0], near[leaf : leaf + 1, :] + far, 0.0
        )


def first_near_kernel(subs, box, counts, *refs):
    geometry, messages = refs[:subs], refs[subs : 2 * subs]
    coupling, basis, near_source, far_source, near, values, picks = refs[2 * subs : 2 * subs + 7]
    features, squares, fields, inner, near_list, far_list, arrived = refs[2 * subs + 7 :]
    copies = copy_all([(near_source, near_list), (far_source, far_list)], arrived)
    slots, height, width = geometry[0].shape
    neighbours = near_list.shape[0]
    rank = coupling.shape[1]
    row = iota((height, width), 0)
    scale_square = jnp.where(row < 3, -2.0, 0.0)
    ones = jnp.where(row == 7, 1.0, 0.0)
    scale_normal = jnp.where((row >= 3) & (row < 6), -KERNEL_SCALE, 0.0)

    for sub in range(subs):
        rows = geometry[sub]
        at = [rows[:, component, :] for component in range(7)]
        squares[sub * slots : (sub + 1) * slots, :] = at[0] * at[0] + at[1] * at[1] + at[2] * at[2]
        fields[sub * slots : (sub + 1) * slots, :] = at[6]
        inner[...] = (at[0] * at[3] + at[1] * at[4] + at[2] * at[5]) * KERNEL_SCALE

        def source(leaf, carry, rows=rows, sub=sub):
            place = sub * slots + leaf
            plain = rows[leaf]
            square = squares[pl.ds(place, 1), :] + SOFTEN
            distance = jnp.where(row == 6, square, plain * scale_square + ones)
            numerator = jnp.where(row == 6, inner[pl.ds(leaf, 1), :], plain * scale_normal)
            for part, value in enumerate((distance, numerator)):
                one, two, three = split_three(value)
                lanes = slice(part * width, (part + 1) * width)
                features[place, 0:16, lanes] = jnp.concatenate([one, two]).astype(jnp.bfloat16)
                features[place, 16:32, lanes] = jnp.concatenate([one, three]).astype(jnp.bfloat16)
            return carry

        lax.fori_loop(0, slots, source, 0, unroll=4)

    own = geometry[0]

    def target(leaf, carry):
        plain = own[leaf]
        shifted = pltpu.roll(plain, 3, 0)
        square = squares[pl.ds(leaf, 1), :]
        value = jnp.where(row < 3, plain, jnp.where(row < 6, shifted, jnp.where(row == 6, 1.0, square)))
        one, two, three = split_three(value)
        left = jnp.concatenate([one, one, two, two, three, one]).T.astype(jnp.bfloat16)
        total = jnp.zeros((width, width), jnp.float32)
        for column in range(neighbours):
            place = near_list[column, leaf] ^ (box[0] * slots)
            upper, lower = features[place, 0:16, :], features[place, 16:32, :]
            right = jnp.concatenate([upper, upper, lower], axis=0)
            both = jnp.dot(left, right, preferred_element_type=jnp.float32)
            inverse = lax.rsqrt(both[:, 0:width])
            tile = both[:, width : 2 * width] * (inverse * inverse * inverse)
            values[leaf * neighbours + column] = tile
            total = total + tile * fields[pl.ds(place, 1), :]
        near[pl.ds(leaf, 1), :] = jnp.sum(total.T, axis=0, keepdims=True)
        return carry

    for copy in copies:
        copy.wait()
    far_count, sources = far_list.shape[0], subs * slots
    far_rows = far_list[...].astype(jnp.float32)
    far_rows = jnp.concatenate(
        [far_rows, jnp.zeros((far_count, LANES - slots), jnp.float32)], axis=1
    ).T
    leaves = (iota((slots, sources), 1) ^ (box[0] * slots)).astype(jnp.float32)
    for place in range(far_count):
        chosen = jnp.where(far_rows[0:slots, place : place + 1] == leaves, 1.0, 0.0)
        picks[place * slots : (place + 1) * slots, :] = chosen.astype(jnp.bfloat16)
    lax.fori_loop(0, slots, target, 0, unroll=True)
    moments = [ref[0:slots, 0:rank] for ref in messages]
    add_leaf_far(counts, moments, picks, coupling, basis, near)


def box_images(box_basis, coefficients, image):
    slots, rank, width = box_basis.shape
    spread = jnp.broadcast_to(coefficients, (rank, width))
    for leaf in range(slots):
        image[leaf : leaf + 1, :] += jnp.sum(box_basis[leaf] * spread, axis=0, keepdims=True)


def first_image_kernel(patches, span, box, box_far, *refs):
    boxes = refs[:patches]
    part, initial, basis, box_basis, box_coupling = refs[patches : patches + 5]
    message, basis_one, numbers, gather, image = refs[patches + 5 :]
    slots, rank, width = basis.shape
    height = boxes[0].shape[0]
    for place, ref in enumerate(boxes):
        gather[place * height : (place + 1) * height, :] = ref[...]
    coupled = jnp.zeros((rank, rank), jnp.float32)
    for place in range(box_coupling.shape[0]):
        row = (box_far[place] ^ box[0]) * span
        coupled = coupled + box_coupling[place] * gather[pl.ds(row, 1), 0:rank]
    image[...] = part[...]
    box_images(box_basis, jnp.sum(coupled, axis=1, keepdims=True), image)
    sums = tree_sum(
        [
            tree_sum([ref[at + 1 : at + 2, :] for at in range(0, height, span)])
            for ref in boxes
        ]
    )
    square_sum, unknowns = sums[:, 0:1], width * sums[:, 1:2]
    start_scale = jnp.sqrt(square_sum / unknowns + EPSILON)
    one_one = square_sum / (start_scale * start_scale)
    basis_one[...] = initial[...] / start_scale
    message[0:slots, :] = image[...] / start_scale
    numbers[...] = jnp.broadcast_to(lane_row([one_one, unknowns, start_scale]), numbers.shape)
    write_moments(message, basis, message, slots)


def second_near_kernel(subs, box, counts, *refs):
    messages = refs[:subs]
    picks, coupling, basis, box_basis, basis_one, values, near_source = refs[subs : subs + 7]
    part, shares, fields, near_list, arrived = refs[subs + 7 :]
    copy = pltpu.make_async_copy(near_source, near_list, arrived)
    copy.start()
    slots, width = part.shape
    neighbours = near_list.shape[0]
    rank = coupling.shape[1]
    for sub in range(subs):
        fields[sub * slots : (sub + 1) * slots, :] = messages[sub][0:slots, :]

    def target(leaf, carry):
        total = jnp.zeros((width, width), jnp.float32)
        for column in range(neighbours):
            place = near_list[column, leaf] ^ (box[0] * slots)
            total = total + values[leaf * neighbours + column] * fields[pl.ds(place, 1), :]
        part[pl.ds(leaf, 1), :] = jnp.sum(total.T, axis=0, keepdims=True)
        return carry

    copy.wait()
    lax.fori_loop(0, slots, target, 0, unroll=True)
    moments = [ref[slots : 2 * slots, 0:rank] for ref in messages]
    add_leaf_far(counts, moments, picks, coupling, basis, part)
    first, one, second = messages[0][0:slots, :], basis_one[...], part[...]
    products = [one * first, first * first, one * second, first * second, second * second]
    sums = lane_row([jnp.sum(product, keepdims=True) for product in products])
    lane = iota((1, LANES), 1)
    both = jnp.where(
        lane < rank,
        box_moments(messages[0], box_basis),
        pltpu.roll(box_moments(part, box_basis), rank, 1),
    )
    shares[...] = jnp.where(iota(shares.shape, 0) % 2 == 0, both, sums)


def last_kernel(patches, span, box, *refs):
    boxes, (shares, message, basis_one, part, numbers) = refs[:patches], refs[patches : patches + 5]
    box_basis, box_coupling = refs[patches + 5 : patches + 7]
    basis_three, hessenberg, gather, starts, lists, pairs, image = refs[patches + 7 :]
    slots, rank, width = box_basis.shape
    height = boxes[0].shape[0]
    count = patches * (height // span)
    for place, ref in enumerate(boxes):
        gather[place * height : (place + 1) * height, :] = ref[...]
    for other in range(count):
        row = (box[0] ^ other) * span
        starts[other : other + 1, :] = gather[pl.ds(row, 1), :]
        lists[other : other + 1, :] = gather[pl.ds(row + 1, 1), :]
        pairs[other : other + 1, :] = shares[2 * other : 2 * other + 1, :]
        pairs[count + other : count + other + 1, :] = shares[2 * other + 1 : 2 * other + 2, :]
    first_box, second_box = pairs[0:count, 0:rank], pairs[0:count, rank : 2 * rank]
    parts = [part.astype(jnp.bfloat16) for part in split_three(first_box)]
    lane = iota((count, count), 1).astype(jnp.float32)
    box_local = jnp.zeros((count, rank), jnp.float32)
    for place in range(box_coupling.shape[0]):
        pick = jnp.where(lists[:, 2 + place : 3 + place] == lane, 1.0, 0.0).astype(jnp.bfloat16)
        chosen = jnp.zeros((count, rank), jnp.float32)
        for split in parts:
            chosen = chosen + jnp.dot(pick, split, preferred_element_type=jnp.float32)
        box_local = box_local + lax.dot_general(
            chosen,
            box_coupling[place],
            (((1,), (1,)), ((), ())),
            precision=HIGH_PRECISION,
            preferred_element_type=jnp.float32,
        )
    twice = jnp.concatenate([box_local, box_local], axis=1)
    columns = twice.T
    half = rank // 2
    low = iota((half, 2 * rank), 1) < rank
    quadratic = jnp.zeros((half, 2 * rank), jnp.float32)
    for other in range(count):
        row = (box[0] ^ other) * span + TILE_ROWS
        column = jnp.where(
            low, columns[0:half, other : other + 1], columns[half:rank, other : other + 1]
        )
        quadratic = quadratic + gather[pl.ds(row, half), :] * twice[other : other + 1, :] * column
    one_one, unknowns, start_scale = [numbers[0:1, place : place + 1] for place in range(3)]
    sums = jnp.sum(pairs[count : 2 * count, :], axis=0, keepdims=True)
    along, image_sq, one_part, first_part, part_sq = [
        sums[:, place : place + 1] for place in range(5)
    ]
    one_second = (
        one_part + jnp.sum(starts[:, 0:rank] * box_local, keepdims=True) / start_scale
    )
    first_second = first_part + jnp.sum(first_box * box_local, keepdims=True)
    second_sq = (
        part_sq
        + 2.0 * jnp.sum(second_box * box_local, keepdims=True)
        + jnp.sum(quadratic, keepdims=True)
    )
    upper_first = (0.5 * one_one + along) / unknowns
    shift = upper_first - 0.5
    residual_sq = image_sq - 2.0 * shift * along + shift * shift * one_one
    lower_first = jnp.sqrt(residual_sq / unknowns + EPSILON)
    one_two = (along - shift * one_one) / lower_first
    two_two = residual_sq / (lower_first * lower_first)
    k_one = (one_second - shift * along) / lower_first
    k_two = (
        (first_second - shift * image_sq) - shift * (one_second - shift * along)
    ) / (lower_first * lower_first)
    k_sq = (second_sq - 2.0 * shift * first_second + shift * shift * image_sq) / (
        lower_first * lower_first
    )
    upper_second = (0.5 * one_two + k_one) / unknowns
    middle_second = (0.5 * two_two + k_two - upper_second * one_two) / unknowns
    turn = middle_second - 0.5
    final_sq = (
        k_sq
        - 2.0 * upper_second * k_one
        - 2.0 * turn * k_two
        + upper_second * upper_second * one_one
        + 2.0 * upper_second * turn * one_two
        + turn * turn * two_two
    )
    lower_second = jnp.sqrt(final_sq / unknowns + EPSILON)
    image[...] = part[...]
    own = jnp.where(iota((rank, count), 1) == box[0], columns[0:rank], 0.0)
    box_images(box_basis, jnp.sum(own, axis=1, keepdims=True), image)
    one, first = basis_one[...], message[0:slots, :]
    two = (first - shift * one) / lower_first
    mapped = (image[...] - shift * first) / lower_first
    basis_three[...] = (mapped - upper_second * one - turn * two) / lower_second
    column, row = iota(hessenberg.shape, 0), iota(hessenberg.shape, 1)
    matrix = jnp.where(column == 0, upper_first, upper_second)
    matrix = jnp.where(row == 1, jnp.where(column == 0, lower_first, middle_second), matrix)
    hessenberg[...] = jnp.where(row == 2, jnp.where(column == 0, 0.0, lower_second), matrix)


def shards(
    points,
    normals,
    density,
    counts,
    near_list,
    leaf_far,
    leaf_basis,
    leaf_to_box_transfer,
    leaf_coupling,
    box_far,
    box_coupling,
):
    slots, _, width = points.shape
    neighbours = near_list.shape[1]
    far_count = leaf_far.shape[1]
    subs, patches = lax.axis_size("sub"), lax.axis_size("patch")
    sources = subs * slots
    rows = f32(slots, width)
    this_box = lax.axis_index("patch") * subs + lax.axis_index("sub")
    box = this_box.astype(jnp.int32).reshape(1)
    box_far = box_far.reshape(-1)
    far_list = leaf_far.T
    rank = leaf_basis.shape[1]
    span = TILE_ROWS + rank // 2
    near_list = near_list.T
    list_scratch = [pltpu.SMEM(near_list.shape, jnp.int32), pltpu.SemaphoreType.DMA]
    block = pltpu.VMEM((sources, width), jnp.float32)

    geometry, initial, message, box_basis, *matrices = device_call(
        start_kernel,
        [
            f32(slots, 8, width),
            rows,
            f32(slots + span, LANES),
            kept(leaf_basis),
            kept(leaf_basis),
            kept(leaf_coupling),
            kept(box_coupling),
        ],
        [counts, box_far],
        [],
        [
            pltpu.VMEM((7, slots, width), jnp.float32),
            pltpu.VMEM(leaf_to_box_transfer.shape, jnp.float32),
            pltpu.SemaphoreType.DMA((7,)),
        ],
        [
            points.transpose(1, 0, 2),
            normals.transpose(1, 0, 2),
            density,
            leaf_to_box_transfer,
            leaf_basis,
            leaf_coupling,
            box_coupling,
        ],
    )
    leaf_basis, leaf_coupling, box_coupling = matrices
    geometry = from_peers(geometry, "sub")
    messages = from_peers(message, "sub")
    boxes = from_peers(
        jnp.concatenate([part[slots : slots + span] for part in messages], axis=0), "patch"
    )
    gather = pltpu.VMEM((patches * subs * span, LANES), jnp.float32)
    part, values, picks = device_call(
        functools.partial(first_near_kernel, subs),
        [
            rows,
            pltpu.VMEM((slots * neighbours, width, width), jnp.float32),
            pltpu.VMEM((far_count * slots, sources), jnp.bfloat16),
        ],
        [box, counts],
        [*geometry, *messages, leaf_coupling, leaf_basis],
        [
            pltpu.VMEM((sources, 32, 2 * width), jnp.bfloat16),
            block,
            block,
            pltpu.VMEM((slots, width), jnp.float32),
            pltpu.SMEM(near_list.shape, jnp.int32),
            pltpu.VMEM(far_list.shape, jnp.int32),
            pltpu.SemaphoreType.DMA((2,)),
        ],
        [near_list, far_list],
    )
    message, basis_one, numbers = device_call(
        functools.partial(first_image_kernel, patches, span),
        [f32(2 * slots, LANES), rows, f32(TILE_ROWS, LANES)],
        [box, box_far],
        [*boxes, part, initial, leaf_basis, box_basis, box_coupling],
        [gather, pltpu.VMEM((slots, width), jnp.float32)],
    )
    messages = from_peers(message, "sub")
    part, shares = device_call(
        functools.partial(second_near_kernel, subs),
        [rows, f32(2 * patches * subs, LANES)],
        [box, counts],
        [*messages, picks, leaf_coupling, leaf_basis, box_basis, basis_one, values],
        [block, *list_scratch],
        [near_list],
    )
    shares = lax.all_to_all(shares, ("patch", "sub"), 0, 0, tiled=True)
    basis_three, hessenberg = device_call(
        functools.partial(last_kernel, patches, span),
        [rows, f32(2, 3)],
        [box],
        [*boxes, shares, message, basis_one, part, numbers, box_basis, box_coupling],
        [
            gather,
            pltpu.VMEM((patches * subs, LANES), jnp.float32),
            pltpu.VMEM((patches * subs, LANES), jnp.float32),
            pltpu.VMEM((2 * patches * subs, LANES), jnp.float32),
            pltpu.VMEM((slots, width), jnp.float32),
        ],
    )
    return basis_three, hessenberg.T


def solution(mesh):
    spread = ("groups", "patch", "sub")
    in_specs = (
        P(spread, None, None),
        P(spread, None, None),
        P(spread, None),
        P(spread),
        P(spread, None),
        P(spread, None),
        P(spread, None, None),
        P(spread, None, None),
        P(),
        P(spread, None),
        P(),
    )
    out_specs = (P(spread, None), P("groups", None))
    return jax.shard_map(shards, mesh=mesh, in_specs=in_specs, out_specs=out_specs, check_vma=False)
```

```python
import functools
import math

import jax
import jax.numpy as jnp
from jax import lax
from jax.experimental import pallas as pl
from jax.experimental.pallas import tpu as pltpu
from jax.sharding import PartitionSpec as P

SOFTEN = 0.05
EPSILON = 1e-06
KERNEL_SCALE = 0.25 / math.pi
HIGH_PRECISION = lax.Precision.HIGHEST
LANES = 128
TILE_ROWS = 8
VMEM_LIMIT = 16 << 20


def from_peers(value, axis):
    size = lax.axis_size(axis)
    arrived = [
        lax.ppermute(value, axis, [(i, i ^ turn) for i in range(size)]) for turn in range(1, size)
    ]
    return [value] + arrived


def tree_sum(parts):
    while len(parts) > 1:
        parts = [parts[i] + parts[i + 1] for i in range(0, len(parts), 2)]
    return parts[0]


def device_call(kernel, outputs, scalars, arrays, scratch=(), remote=()):
    smem = pl.BlockSpec(memory_space=pltpu.SMEM)
    vmem = pl.BlockSpec(memory_space=pltpu.VMEM)
    hbm = pl.BlockSpec(memory_space=pltpu.HBM)
    return pl.pallas_call(
        kernel,
        out_shape=tuple(outputs),
        in_specs=[smem] * len(scalars) + [vmem] * len(arrays) + [hbm] * len(remote),
        out_specs=tuple([vmem] * len(outputs)),
        scratch_shapes=tuple(scratch),
        compiler_params=pltpu.CompilerParams(vmem_limit_bytes=VMEM_LIMIT),
    )(
        *scalars,
        *[pltpu.with_memory_space_constraint(array, pltpu.VMEM) for array in arrays],
        *[pltpu.with_memory_space_constraint(array, pltpu.HBM) for array in remote],
    )


def kept(*shape, dtype=jnp.float32):
    return pltpu.VMEM(shape, dtype)


def f32(*shape):
    return jax.ShapeDtypeStruct(shape, jnp.float32)


def iota(shape, dimension):
    return lax.broadcasted_iota(jnp.int32, shape, dimension)


def split_three(value):
    first = value.astype(jnp.bfloat16).astype(jnp.float32)
    rest = value - first
    second = rest.astype(jnp.bfloat16).astype(jnp.float32)
    third = (rest - second).astype(jnp.bfloat16).astype(jnp.float32)
    return first, second, third


def lane_row(entries):
    lane = iota((1, LANES), 1)
    row = jnp.zeros((1, LANES), jnp.float32)
    for place, entry in enumerate(entries):
        row = jnp.where(lane == place, entry, row)
    return row


def copy_all(pairs, arrived):
    copies = [
        pltpu.make_async_copy(source, target, arrived.at[place])
        for place, (source, target) in enumerate(pairs)
    ]
    for copy in copies:
        copy.start()
    return copies


def write_moments(vector, basis, message, start):
    slots, rank, _ = basis.shape
    lane = iota((rank, LANES), 1)
    columns = jnp.zeros((rank, LANES), jnp.float32)
    for leaf in range(slots):
        column = jnp.sum(basis[leaf] * vector[leaf : leaf + 1, :], axis=1, keepdims=True)
        columns = jnp.where(lane == leaf, column, columns)
    message[start : start + slots, :] = jnp.zeros((slots, LANES), jnp.float32)
    message[start : start + slots, 0:rank] = columns.T[0:slots]


def box_moments(vector, box_basis):
    slots, rank, width = box_basis.shape
    total = jnp.zeros((rank, width), jnp.float32)
    for leaf in range(slots):
        total = total + box_basis[leaf] * vector[leaf : leaf + 1, :]
    column = jnp.sum(total, axis=1, keepdims=True)
    diagonal = iota((rank, LANES), 0) == iota((rank, LANES), 1)
    return jnp.sum(jnp.where(diagonal, column, 0.0), axis=0, keepdims=True)


def start_kernel(counts, *refs):
    sources, (geometry, initial, message, box_basis) = refs[:8], refs[8:12]
    basis, leaf_coupling, box_coupling = refs[12:15]
    at, box_far, transfer, parts, arrived = refs[15:]
    dims, slots, width = sources[0].shape
    rank = basis.shape[1]
    targets = [at.at[0:dims], at.at[dims : 2 * dims], at.at[2 * dims], box_far]
    targets += [transfer, basis, leaf_coupling, box_coupling]
    copies = copy_all(zip(sources, targets), arrived)
    for copy in copies[:4]:
        copy.wait()
    for row in range(2 * dims):
        geometry[:, row, :] = at[row]
    vector = jnp.where(iota((slots, width), 0) < counts[0], at[2 * dims], 0.0)
    initial[...] = vector
    geometry[:, 2 * dims, :] = vector
    geometry[:, 2 * dims + 1, :] = jnp.zeros_like(vector)
    entries = [jnp.sum(vector * vector, keepdims=True)] + [
        jnp.full((1, 1), value, jnp.int32).astype(jnp.float32)
        for value in [counts[0]] + [box_far[0, place] for place in range(box_far.shape[1])]
    ]
    message[slots : slots + TILE_ROWS, :] = jnp.zeros((TILE_ROWS, LANES), jnp.float32)
    message[slots + 1 : slots + 2, :] = lane_row(entries)
    for copy in copies[4:6]:
        copy.wait()
    for leaf in range(slots):
        product = jnp.dot(
            transfer[leaf],
            basis[leaf],
            precision=HIGH_PRECISION,
            preferred_element_type=jnp.float32,
        )
        product = jnp.where(leaf < counts[0], product, 0.0)
        box_basis[leaf] = product
        split = jnp.concatenate(split_three(product)).astype(jnp.bfloat16)
        parts[:, leaf * width : (leaf + 1) * width] = split
    write_moments(initial, basis, message, 0)
    message[slots : slots + 1, :] = box_moments(initial, box_basis)
    products = lax.dot_general(
        parts[...], parts[...], (((1,), (1,)), ((), ())), preferred_element_type=jnp.float32
    )
    mixed = products[rank : 2 * rank, 0:rank] + products[2 * rank : 3 * rank, 0:rank]
    gram = products[0:rank, 0:rank] + (
        mixed + mixed.T + products[rank : 2 * rank, rank : 2 * rank]
    )
    start, half = slots + TILE_ROWS, rank // 2
    message[start : start + half, 0:rank] = gram[0:half]
    message[start : start + half, rank : 2 * rank] = gram[half:rank]
    for copy in copies[6:]:
        copy.wait()


def leaf_part(moments, picks, coupling):
    count, rank, _ = coupling.shape
    slots = picks.shape[0] // count
    chosen = jnp.zeros((picks.shape[0], rank), jnp.float32)
    for part in split_three(jnp.concatenate(moments, axis=0)):
        chosen = chosen + jnp.dot(
            picks[...], part.astype(jnp.bfloat16), preferred_element_type=jnp.float32
        )
    local = jnp.zeros((slots, rank), jnp.float32)
    for place in range(count):
        local = local + lax.dot_general(
            chosen[place * slots : (place + 1) * slots],
            coupling[place],
            (((1,), (1,)), ((), ())),
            precision=HIGH_PRECISION,
            preferred_element_type=jnp.float32,
        )
    return local


def wide_transpose(rows):
    count, lanes = rows.shape
    return jnp.concatenate([rows, jnp.zeros((count, LANES - lanes), rows.dtype)], axis=1).T


def add_leaf_far(counts, local, basis, near):
    slots, rank, width = basis.shape
    columns = wide_transpose(local)
    for leaf in range(slots):
        far = jnp.sum(basis[leaf] * columns[0:rank, leaf : leaf + 1], axis=0, keepdims=True)
        near[leaf : leaf + 1, :] = jnp.where(
            leaf < counts[0], near[leaf : leaf + 1, :] + far, 0.0
        )


def first_near_kernel(subs, box, counts, *refs):
    geometry, messages = refs[:subs], refs[subs : 2 * subs]
    coupling, basis, near_source, far_source, near, values, picks = refs[2 * subs : 2 * subs + 7]
    features, squares, fields, inner, near_list, far_list, arrived = refs[2 * subs + 7 :]
    copies = copy_all([(near_source, near_list), (far_source, far_list)], arrived)
    slots, height, width = geometry[0].shape
    neighbours = near_list.shape[0]
    rank = coupling.shape[1]
    row = iota((height, width), 0)
    scale_square = jnp.where(row < 3, -2.0, 0.0)
    ones = jnp.where(row == 7, 1.0, 0.0)
    scale_normal = jnp.where((row >= 3) & (row < 6), -KERNEL_SCALE, 0.0)

    for sub in range(subs):
        rows = geometry[sub]
        at = [rows[:, component, :] for component in range(7)]
        squares[sub * slots : (sub + 1) * slots, :] = at[0] * at[0] + at[1] * at[1] + at[2] * at[2]
        fields[sub * slots : (sub + 1) * slots, :] = at[6]
        inner[...] = (at[0] * at[3] + at[1] * at[4] + at[2] * at[5]) * KERNEL_SCALE

        def source(leaf, carry, rows=rows, sub=sub):
            place = sub * slots + leaf
            plain = rows[leaf]
            square = squares[pl.ds(place, 1), :] + SOFTEN
            distance = jnp.where(row == 6, square, plain * scale_square + ones)
            numerator = jnp.where(row == 6, inner[pl.ds(leaf, 1), :], plain * scale_normal)
            for part, value in enumerate((distance, numerator)):
                one, two, three = split_three(value)
                lanes = slice(part * width, (part + 1) * width)
                features[place, 0:16, lanes] = jnp.concatenate([one, two]).astype(jnp.bfloat16)
                features[place, 16:32, lanes] = jnp.concatenate([one, three]).astype(jnp.bfloat16)
            return carry

        lax.fori_loop(0, slots, source, 0, unroll=4)

    own = geometry[0]

    def target(leaf, carry):
        plain = own[leaf]
        shifted = pltpu.roll(plain, 3, 0)
        square = squares[pl.ds(leaf, 1), :]
        value = jnp.where(row < 3, plain, jnp.where(row < 6, shifted, jnp.where(row == 6, 1.0, square)))
        one, two, three = split_three(value)
        left = jnp.concatenate([one, one, two, two, three, one]).T.astype(jnp.bfloat16)
        total = jnp.zeros((width, width), jnp.float32)
        for column in range(neighbours):
            place = near_list[column, leaf] ^ (box[0] * slots)
            upper, lower = features[place, 0:16, :], features[place, 16:32, :]
            right = jnp.concatenate([upper, upper, lower], axis=0)
            both = jnp.dot(left, right, preferred_element_type=jnp.float32)
            inverse = lax.rsqrt(both[:, 0:width])
            tile = both[:, width : 2 * width] * (inverse * inverse * inverse)
            values[leaf * neighbours + column] = tile
            total = total + tile * fields[pl.ds(place, 1), :]
        near[pl.ds(leaf, 1), :] = jnp.sum(total.T, axis=0, keepdims=True)
        return carry

    for copy in copies:
        copy.wait()
    far_count, sources = far_list.shape[0], subs * slots
    far_rows = wide_transpose(far_list[...].astype(jnp.float32))
    leaves = (iota((slots, sources), 1) ^ (box[0] * slots)).astype(jnp.float32)
    for place in range(far_count):
        chosen = jnp.where(far_rows[0:slots, place : place + 1] == leaves, 1.0, 0.0)
        picks[place * slots : (place + 1) * slots, :] = chosen.astype(jnp.bfloat16)
    local = leaf_part([ref[0:slots, 0:rank] for ref in messages], picks, coupling)
    lax.fori_loop(0, slots, target, 0, unroll=True)
    add_leaf_far(counts, local, basis, near)


def box_images(box_basis, coefficients, image):
    slots, rank, width = box_basis.shape
    spread = jnp.broadcast_to(coefficients, (rank, width))
    for leaf in range(slots):
        image[leaf : leaf + 1, :] += jnp.sum(box_basis[leaf] * spread, axis=0, keepdims=True)


def first_image_kernel(patches, span, box, *refs):
    boxes = refs[:patches]
    part, initial, basis, box_basis, box_coupling = refs[patches : patches + 5]
    message, basis_one, numbers, starts, image = refs[patches + 5 :]
    slots, rank, width = basis.shape
    height = boxes[0].shape[0]
    row_starts = [(ref, at) for ref in boxes for at in range(0, height, span)]
    count = len(row_starts)
    for place, (ref, at) in enumerate(row_starts):
        starts[place : place + 1, :] = ref[at : at + 1, :]
    number = (iota((count, LANES), 0) ^ box[0]).astype(jnp.float32)
    coupled = jnp.zeros((rank, rank), jnp.float32)
    for place in range(box_coupling.shape[0]):
        wanted = boxes[0][1:2, 2 + place : 3 + place]
        row = jnp.sum(jnp.where(number == wanted, starts[...], 0.0), axis=0, keepdims=True)
        coupled = coupled + box_coupling[place] * row[:, 0:rank]
    image[...] = part[...]
    box_images(box_basis, jnp.sum(coupled, axis=1, keepdims=True), image)
    sums = tree_sum(
        [
            tree_sum([ref[at + 1 : at + 2, :] for at in range(0, height, span)])
            for ref in boxes
        ]
    )
    square_sum, unknowns = sums[:, 0:1], width * sums[:, 1:2]
    start_scale = jnp.sqrt(square_sum / unknowns + EPSILON)
    one_one = square_sum / (start_scale * start_scale)
    basis_one[...] = initial[...] / start_scale
    message[0:slots, :] = image[...] / start_scale
    numbers[...] = jnp.broadcast_to(lane_row([one_one, unknowns, start_scale]), numbers.shape)
    write_moments(message, basis, message, slots)


def second_near_kernel(subs, box, counts, *refs):
    messages = refs[:subs]
    picks, coupling, basis, box_basis, basis_one, values, near_source = refs[subs : subs + 7]
    part, shares, fields, near_list, arrived = refs[subs + 7 :]
    copy = pltpu.make_async_copy(near_source, near_list, arrived)
    copy.start()
    slots, width = part.shape
    neighbours = near_list.shape[0]
    rank = coupling.shape[1]
    for sub in range(subs):
        fields[sub * slots : (sub + 1) * slots, :] = messages[sub][0:slots, :]

    def target(leaf, carry):
        total = jnp.zeros((width, width), jnp.float32)
        for column in range(neighbours):
            place = near_list[column, leaf] ^ (box[0] * slots)
            total = total + values[leaf * neighbours + column] * fields[pl.ds(place, 1), :]
        part[pl.ds(leaf, 1), :] = jnp.sum(total.T, axis=0, keepdims=True)
        return carry

    local = leaf_part([ref[slots : 2 * slots, 0:rank] for ref in messages], picks, coupling)
    copy.wait()
    lax.fori_loop(0, slots, target, 0, unroll=True)
    add_leaf_far(counts, local, basis, part)
    first, one, second = messages[0][0:slots, :], basis_one[...], part[...]
    products = [one * first, first * first, one * second, first * second, second * second]
    sums = lane_row([jnp.sum(product, keepdims=True) for product in products])
    lane = iota((1, LANES), 1)
    both = jnp.where(
        lane < rank,
        box_moments(messages[0], box_basis),
        pltpu.roll(box_moments(part, box_basis), rank, 1),
    )
    shares[...] = jnp.where(iota(shares.shape, 0) % 2 == 0, both, sums)


def last_kernel(patches, span, box, *refs):
    boxes, (shares, message, basis_one, part, numbers) = refs[:patches], refs[patches : patches + 5]
    box_basis, box_coupling = refs[patches + 5 : patches + 7]
    basis_three, hessenberg, gather, starts, lists, pairs, image = refs[patches + 7 :]
    slots, rank, width = box_basis.shape
    height = boxes[0].shape[0]
    count = patches * (height // span)
    for place, ref in enumerate(boxes):
        gather[place * height : (place + 1) * height, :] = ref[...]
    for other in range(count):
        row = (box[0] ^ other) * span
        starts[other : other + 1, :] = gather[pl.ds(row, 1), :]
        lists[other : other + 1, :] = gather[pl.ds(row + 1, 1), :]
        pairs[other : other + 1, :] = shares[2 * other : 2 * other + 1, :]
        pairs[count + other : count + other + 1, :] = shares[2 * other + 1 : 2 * other + 2, :]
    first_box, second_box = pairs[0:count, 0:rank], pairs[0:count, rank : 2 * rank]
    parts = [part.astype(jnp.bfloat16) for part in split_three(first_box)]
    lane = iota((count, count), 1).astype(jnp.float32)
    box_local = jnp.zeros((count, rank), jnp.float32)
    for place in range(box_coupling.shape[0]):
        pick = jnp.where(lists[:, 2 + place : 3 + place] == lane, 1.0, 0.0).astype(jnp.bfloat16)
        chosen = jnp.zeros((count, rank), jnp.float32)
        for split in parts:
            chosen = chosen + jnp.dot(pick, split, preferred_element_type=jnp.float32)
        box_local = box_local + lax.dot_general(
            chosen,
            box_coupling[place],
            (((1,), (1,)), ((), ())),
            precision=HIGH_PRECISION,
            preferred_element_type=jnp.float32,
        )
    twice = jnp.concatenate([box_local, box_local], axis=1)
    columns = twice.T
    half = rank // 2
    low = iota((half, 2 * rank), 1) < rank
    quadratic = jnp.zeros((half, 2 * rank), jnp.float32)
    for other in range(count):
        row = (box[0] ^ other) * span + TILE_ROWS
        column = jnp.where(
            low, columns[0:half, other : other + 1], columns[half:rank, other : other + 1]
        )
        quadratic = quadratic + gather[pl.ds(row, half), :] * twice[other : other + 1, :] * column
    one_one, unknowns, start_scale = [numbers[0:1, place : place + 1] for place in range(3)]
    sums = jnp.sum(pairs[count : 2 * count, :], axis=0, keepdims=True)
    along, image_sq, one_part, first_part, part_sq = [
        sums[:, place : place + 1] for place in range(5)
    ]
    one_second = (
        one_part + jnp.sum(starts[:, 0:rank] * box_local, keepdims=True) / start_scale
    )
    first_second = first_part + jnp.sum(first_box * box_local, keepdims=True)
    second_sq = (
        part_sq
        + 2.0 * jnp.sum(second_box * box_local, keepdims=True)
        + jnp.sum(quadratic, keepdims=True)
    )
    upper_first = (0.5 * one_one + along) / unknowns
    shift = upper_first - 0.5
    residual_sq = image_sq - 2.0 * shift * along + shift * shift * one_one
    lower_first = jnp.sqrt(residual_sq / unknowns + EPSILON)
    one_two = (along - shift * one_one) / lower_first
    two_two = residual_sq / (lower_first * lower_first)
    k_one = (one_second - shift * along) / lower_first
    k_two = (
        (first_second - shift * image_sq) - shift * (one_second - shift * along)
    ) / (lower_first * lower_first)
    k_sq = (second_sq - 2.0 * shift * first_second + shift * shift * image_sq) / (
        lower_first * lower_first
    )
    upper_second = (0.5 * one_two + k_one) / unknowns
    middle_second = (0.5 * two_two + k_two - upper_second * one_two) / unknowns
    turn = middle_second - 0.5
    final_sq = (
        k_sq
        - 2.0 * upper_second * k_one
        - 2.0 * turn * k_two
        + upper_second * upper_second * one_one
        + 2.0 * upper_second * turn * one_two
        + turn * turn * two_two
    )
    lower_second = jnp.sqrt(final_sq / unknowns + EPSILON)
    image[...] = part[...]
    own = jnp.where(iota((rank, count), 1) == box[0], columns[0:rank], 0.0)
    box_images(box_basis, jnp.sum(own, axis=1, keepdims=True), image)
    one, first = basis_one[...], message[0:slots, :]
    two = (first - shift * one) / lower_first
    mapped = (image[...] - shift * first) / lower_first
    basis_three[...] = (mapped - upper_second * one - turn * two) / lower_second
    column, row = iota(hessenberg.shape, 0), iota(hessenberg.shape, 1)
    matrix = jnp.where(column == 0, upper_first, upper_second)
    matrix = jnp.where(row == 1, jnp.where(column == 0, lower_first, middle_second), matrix)
    hessenberg[...] = jnp.where(row == 2, jnp.where(column == 0, 0.0, lower_second), matrix)


def shards(
    points,
    normals,
    density,
    counts,
    near_list,
    leaf_far,
    leaf_basis,
    leaf_to_box_transfer,
    leaf_coupling,
    box_far,
    box_coupling,
):
    slots, _, width = points.shape
    neighbours = near_list.shape[1]
    far_count = leaf_far.shape[1]
    subs, patches = lax.axis_size("sub"), lax.axis_size("patch")
    sources = subs * slots
    rows = kept(slots, width)
    this_box = lax.axis_index("patch") * subs + lax.axis_index("sub")
    box = this_box.astype(jnp.int32).reshape(1)
    far_list = leaf_far.T
    rank = leaf_basis.shape[1]
    span = TILE_ROWS + rank // 2
    near_list = near_list.T
    list_scratch = [pltpu.SMEM(near_list.shape, jnp.int32), pltpu.SemaphoreType.DMA]
    block = pltpu.VMEM((sources, width), jnp.float32)

    matrices = [leaf_basis, leaf_coupling, box_coupling]
    geometry, initial, message, box_basis, *matrices = device_call(
        start_kernel,
        [
            kept(slots, 8, width),
            rows,
            kept(slots + span, LANES),
            kept(*leaf_basis.shape),
            *[kept(*matrix.shape) for matrix in matrices],
        ],
        [counts],
        [],
        [
            pltpu.VMEM((7, slots, width), jnp.float32),
            pltpu.SMEM(box_far.shape, jnp.int32),
            pltpu.VMEM(leaf_to_box_transfer.shape, jnp.float32),
            pltpu.VMEM((3 * rank, slots * width), jnp.bfloat16),
            pltpu.SemaphoreType.DMA((8,)),
        ],
        [
            points.transpose(1, 0, 2),
            normals.transpose(1, 0, 2),
            density,
            box_far,
            leaf_to_box_transfer,
            *matrices,
        ],
    )
    leaf_basis, leaf_coupling, box_coupling = matrices
    geometry = from_peers(geometry, "sub")
    messages = from_peers(message, "sub")
    boxes = from_peers(
        jnp.concatenate([part[slots : slots + span] for part in messages], axis=0), "patch"
    )
    gather = pltpu.VMEM((patches * subs * span, LANES), jnp.float32)
    part, values, picks = device_call(
        functools.partial(first_near_kernel, subs),
        [
            rows,
            kept(slots * neighbours, width, width),
            kept(far_count * slots, sources, dtype=jnp.bfloat16),
        ],
        [box, counts],
        [*geometry, *messages, leaf_coupling, leaf_basis],
        [
            pltpu.VMEM((sources, 32, 2 * width), jnp.bfloat16),
            block,
            block,
            pltpu.VMEM((slots, width), jnp.float32),
            pltpu.SMEM(near_list.shape, jnp.int32),
            pltpu.VMEM(far_list.shape, jnp.int32),
            pltpu.SemaphoreType.DMA((2,)),
        ],
        [near_list, far_list],
    )
    message, basis_one, numbers = device_call(
        functools.partial(first_image_kernel, patches, span),
        [kept(2 * slots, LANES), rows, kept(TILE_ROWS, LANES)],
        [box],
        [*boxes, part, initial, leaf_basis, box_basis, box_coupling],
        [
            pltpu.VMEM((patches * subs, LANES), jnp.float32),
            pltpu.VMEM((slots, width), jnp.float32),
        ],
    )
    messages = from_peers(message, "sub")
    part, shares = device_call(
        functools.partial(second_near_kernel, subs),
        [rows, kept(2 * patches * subs, LANES)],
        [box, counts],
        [*messages, picks, leaf_coupling, leaf_basis, box_basis, basis_one, values],
        [block, *list_scratch],
        [near_list],
    )
    shares = lax.all_to_all(shares, ("patch", "sub"), 0, 0, tiled=True)
    basis_three, hessenberg = device_call(
        functools.partial(last_kernel, patches, span),
        [f32(slots, width), f32(2, 3)],
        [box],
        [*boxes, shares, message, basis_one, part, numbers, box_basis, box_coupling],
        [
            gather,
            pltpu.VMEM((patches * subs, LANES), jnp.float32),
            pltpu.VMEM((patches * subs, LANES), jnp.float32),
            pltpu.VMEM((2 * patches * subs, LANES), jnp.float32),
            pltpu.VMEM((slots, width), jnp.float32),
        ],
    )
    return basis_three, hessenberg.T


def solution(mesh):
    spread = ("groups", "patch", "sub")
    in_specs = (
        P(spread, None, None),
        P(spread, None, None),
        P(spread, None),
        P(spread),
        P(spread, None),
        P(spread, None),
        P(spread, None, None),
        P(spread, None, None),
        P(),
        P(spread, None),
        P(),
    )
    out_specs = (P(spread, None), P("groups", None))
    return jax.shard_map(shards, mesh=mesh, in_specs=in_specs, out_specs=out_specs, check_vma=False)
```

```python
import functools
import math

import jax
import jax.numpy as jnp
from jax import lax
from jax.experimental import pallas as pl
from jax.experimental.pallas import tpu as pltpu
from jax.sharding import PartitionSpec as P

SOFTEN = 0.05
EPSILON = 1e-06
KERNEL_SCALE = 0.25 / math.pi
HIGH_PRECISION = lax.Precision.HIGHEST
LANES = 128
TILE_ROWS = 8
VMEM_LIMIT = 16 << 20


def from_peers(value, axis):
    size = lax.axis_size(axis)
    arrived = [
        lax.ppermute(value, axis, [(i, i ^ turn) for i in range(size)]) for turn in range(1, size)
    ]
    return [value] + arrived


def tree_sum(parts):
    while len(parts) > 1:
        parts = [parts[i] + parts[i + 1] for i in range(0, len(parts), 2)]
    return parts[0]


def device_call(kernel, outputs, scalars, arrays, scratch=(), remote=()):
    smem = pl.BlockSpec(memory_space=pltpu.SMEM)
    vmem = pl.BlockSpec(memory_space=pltpu.VMEM)
    hbm = pl.BlockSpec(memory_space=pltpu.HBM)
    return pl.pallas_call(
        kernel,
        out_shape=tuple(outputs),
        in_specs=[smem] * len(scalars) + [vmem] * len(arrays) + [hbm] * len(remote),
        out_specs=tuple([vmem] * len(outputs)),
        scratch_shapes=tuple(scratch),
        compiler_params=pltpu.CompilerParams(vmem_limit_bytes=VMEM_LIMIT),
    )(
        *scalars,
        *[pltpu.with_memory_space_constraint(array, pltpu.VMEM) for array in arrays],
        *[pltpu.with_memory_space_constraint(array, pltpu.HBM) for array in remote],
    )


def kept(*shape, dtype=jnp.float32):
    return pltpu.VMEM(shape, dtype)


def f32(*shape):
    return jax.ShapeDtypeStruct(shape, jnp.float32)


def iota(shape, dimension):
    return lax.broadcasted_iota(jnp.int32, shape, dimension)


def split_three(value):
    first = value.astype(jnp.bfloat16).astype(jnp.float32)
    rest = value - first
    second = rest.astype(jnp.bfloat16).astype(jnp.float32)
    third = (rest - second).astype(jnp.bfloat16).astype(jnp.float32)
    return first, second, third


def lane_row(entries):
    lane = iota((1, LANES), 1)
    row = jnp.zeros((1, LANES), jnp.float32)
    for place, entry in enumerate(entries):
        row = jnp.where(lane == place, entry, row)
    return row


def copy_all(pairs, arrived):
    copies = [
        pltpu.make_async_copy(source, target, arrived.at[place])
        for place, (source, target) in enumerate(pairs)
    ]
    for copy in copies:
        copy.start()
    return copies


def write_moments(vector, basis, message, start):
    slots, rank, _ = basis.shape
    lane = iota((rank, LANES), 1)
    columns = jnp.zeros((rank, LANES), jnp.float32)
    for leaf in range(slots):
        column = jnp.sum(basis[leaf] * vector[leaf : leaf + 1, :], axis=1, keepdims=True)
        columns = jnp.where(lane == leaf, column, columns)
    message[start : start + slots, :] = jnp.zeros((slots, LANES), jnp.float32)
    message[start : start + slots, 0:rank] = columns.T[0:slots]


def box_moments(vector, box_basis):
    slots, rank, width = box_basis.shape
    total = jnp.zeros((rank, width), jnp.float32)
    for leaf in range(slots):
        total = total + box_basis[leaf] * vector[leaf : leaf + 1, :]
    column = jnp.sum(total, axis=1, keepdims=True)
    diagonal = iota((rank, LANES), 0) == iota((rank, LANES), 1)
    return jnp.sum(jnp.where(diagonal, column, 0.0), axis=0, keepdims=True)


def start_kernel(counts, *refs):
    sources, (geometry, message, box_basis) = refs[:8], refs[8:11]
    basis, leaf_coupling, box_coupling = refs[11:14]
    at, initial, box_far, transfer, parts, arrived = refs[14:]
    dims, slots, width = sources[0].shape
    rank = basis.shape[1]
    targets = [at.at[0:dims], at.at[dims : 2 * dims], at.at[2 * dims], box_far]
    targets += [transfer, basis, leaf_coupling, box_coupling]
    copies = copy_all(zip(sources, targets), arrived)
    for copy in copies[:4]:
        copy.wait()
    for row in range(2 * dims):
        geometry[:, row, :] = at[row]
    vector = jnp.where(iota((slots, width), 0) < counts[0], at[2 * dims], 0.0)
    initial[...] = vector
    geometry[:, 2 * dims, :] = vector
    geometry[:, 2 * dims + 1, :] = jnp.zeros_like(vector)
    entries = [jnp.sum(vector * vector, keepdims=True)] + [
        jnp.full((1, 1), value, jnp.int32).astype(jnp.float32)
        for value in [counts[0]] + [box_far[0, place] for place in range(box_far.shape[1])]
    ]
    message[slots : slots + TILE_ROWS, :] = jnp.zeros((TILE_ROWS, LANES), jnp.float32)
    message[slots + 1 : slots + 2, :] = lane_row(entries)
    for copy in copies[4:6]:
        copy.wait()
    for leaf in range(slots):
        product = jnp.dot(
            transfer[leaf],
            basis[leaf],
            precision=HIGH_PRECISION,
            preferred_element_type=jnp.float32,
        )
        product = jnp.where(leaf < counts[0], product, 0.0)
        box_basis[leaf] = product
        split = jnp.concatenate(split_three(product)).astype(jnp.bfloat16)
        parts[:, leaf * width : (leaf + 1) * width] = split
    write_moments(initial, basis, message, 0)
    message[slots : slots + 1, :] = box_moments(initial, box_basis)
    products = lax.dot_general(
        parts[...], parts[...], (((1,), (1,)), ((), ())), preferred_element_type=jnp.float32
    )
    mixed = products[rank : 2 * rank, 0:rank] + products[2 * rank : 3 * rank, 0:rank]
    gram = products[0:rank, 0:rank] + (
        mixed + mixed.T + products[rank : 2 * rank, rank : 2 * rank]
    )
    start, half = slots + TILE_ROWS, rank // 2
    message[start : start + half, 0:rank] = gram[0:half]
    message[start : start + half, rank : 2 * rank] = gram[half:rank]
    for copy in copies[6:]:
        copy.wait()


def join_kernel(subs, *refs):
    messages, (moments, blocks) = refs[:subs], refs[subs:]
    slots, span = moments.shape[0] // subs, blocks.shape[0] // subs
    for sub, message in enumerate(messages):
        moments[sub * slots : (sub + 1) * slots, :] = message[0:slots, :]
        blocks[sub * span : (sub + 1) * span, :] = message[slots : slots + span, :]


def leaf_part(moments, picks, coupling):
    count, rank, _ = coupling.shape
    slots = picks.shape[0] // count
    chosen = jnp.zeros((picks.shape[0], rank), jnp.float32)
    for part in split_three(moments):
        chosen = chosen + jnp.dot(
            picks[...], part.astype(jnp.bfloat16), preferred_element_type=jnp.float32
        )
    local = jnp.zeros((slots, rank), jnp.float32)
    for place in range(count):
        local = local + lax.dot_general(
            chosen[place * slots : (place + 1) * slots],
            coupling[place],
            (((1,), (1,)), ((), ())),
            precision=HIGH_PRECISION,
            preferred_element_type=jnp.float32,
        )
    return local


def wide_transpose(rows):
    count, lanes = rows.shape
    return jnp.concatenate([rows, jnp.zeros((count, LANES - lanes), rows.dtype)], axis=1).T


def add_leaf_far(counts, local, basis, near):
    slots, rank, width = basis.shape
    columns = wide_transpose(local)
    for leaf in range(slots):
        far = jnp.sum(basis[leaf] * columns[0:rank, leaf : leaf + 1], axis=0, keepdims=True)
        near[leaf : leaf + 1, :] = jnp.where(
            leaf < counts[0], near[leaf : leaf + 1, :] + far, 0.0
        )


def first_near_kernel(subs, box, counts, *refs):
    geometry, (moments, coupling, basis) = refs[:subs], refs[subs : subs + 3]
    near_source, far_source, near, initial, values, picks = refs[subs + 3 : subs + 9]
    features, squares, fields, inner, near_list, far_list, arrived = refs[subs + 9 :]
    copies = copy_all([(near_source, near_list), (far_source, far_list)], arrived)
    slots, height, width = geometry[0].shape
    neighbours = near_list.shape[0]
    rank = coupling.shape[1]
    row = iota((height, width), 0)
    scale_square = jnp.where(row < 3, -2.0, 0.0)
    ones = jnp.where(row == 7, 1.0, 0.0)
    scale_normal = jnp.where((row >= 3) & (row < 6), -KERNEL_SCALE, 0.0)

    for sub in range(subs):
        rows = geometry[sub]
        at = [rows[:, component, :] for component in range(7)]
        squares[sub * slots : (sub + 1) * slots, :] = at[0] * at[0] + at[1] * at[1] + at[2] * at[2]
        fields[sub * slots : (sub + 1) * slots, :] = at[6]
        inner[...] = (at[0] * at[3] + at[1] * at[4] + at[2] * at[5]) * KERNEL_SCALE

        def source(leaf, carry, rows=rows, sub=sub):
            place = sub * slots + leaf
            plain = rows[leaf]
            square = squares[pl.ds(place, 1), :] + SOFTEN
            distance = jnp.where(row == 6, square, plain * scale_square + ones)
            numerator = jnp.where(row == 6, inner[pl.ds(leaf, 1), :], plain * scale_normal)
            for part, value in enumerate((distance, numerator)):
                one, two, three = split_three(value)
                lanes = slice(part * width, (part + 1) * width)
                features[place, 0:16, lanes] = jnp.concatenate([one, two]).astype(jnp.bfloat16)
                features[place, 16:32, lanes] = jnp.concatenate([one, three]).astype(jnp.bfloat16)
            return carry

        lax.fori_loop(0, slots, source, 0, unroll=4)

    own = geometry[0]

    def target(leaf, carry):
        plain = own[leaf]
        shifted = pltpu.roll(plain, 3, 0)
        square = squares[pl.ds(leaf, 1), :]
        value = jnp.where(row < 3, plain, jnp.where(row < 6, shifted, jnp.where(row == 6, 1.0, square)))
        one, two, three = split_three(value)
        left = jnp.concatenate([one, one, two, two, three, one]).T.astype(jnp.bfloat16)
        total = jnp.zeros((width, width), jnp.float32)
        for column in range(neighbours):
            place = near_list[column, leaf] ^ (box[0] * slots)
            upper, lower = features[place, 0:16, :], features[place, 16:32, :]
            right = jnp.concatenate([upper, upper, lower], axis=0)
            both = jnp.dot(left, right, preferred_element_type=jnp.float32)
            inverse = lax.rsqrt(both[:, 0:width])
            tile = both[:, width : 2 * width] * (inverse * inverse * inverse)
            values[leaf * neighbours + column] = tile
            total = total + tile * fields[pl.ds(place, 1), :]
        near[pl.ds(leaf, 1), :] = jnp.sum(total.T, axis=0, keepdims=True)
        return carry

    for copy in copies:
        copy.wait()
    far_count, sources = far_list.shape[0], subs * slots
    far_rows = wide_transpose(far_list[...].astype(jnp.float32))
    leaves = (iota((slots, sources), 1) ^ (box[0] * slots)).astype(jnp.float32)
    for place in range(far_count):
        chosen = jnp.where(far_rows[0:slots, place : place + 1] == leaves, 1.0, 0.0)
        picks[place * slots : (place + 1) * slots, :] = chosen.astype(jnp.bfloat16)
    local = leaf_part(moments[:, 0:rank], picks, coupling)
    initial[...] = fields[0:slots, :]
    lax.fori_loop(0, slots, target, 0, unroll=True)
    add_leaf_far(counts, local, basis, near)


def box_images(box_basis, coefficients, image):
    slots, rank, width = box_basis.shape
    spread = jnp.broadcast_to(coefficients, (rank, width))
    for leaf in range(slots):
        image[leaf : leaf + 1, :] += jnp.sum(box_basis[leaf] * spread, axis=0, keepdims=True)


def first_image_kernel(patches, span, box, *refs):
    boxes = refs[:patches]
    part, initial, basis, box_basis, box_coupling = refs[patches : patches + 5]
    message, basis_one, numbers, starts, image = refs[patches + 5 :]
    slots, rank, width = basis.shape
    height = boxes[0].shape[0]
    row_starts = [(ref, at) for ref in boxes for at in range(0, height, span)]
    count = len(row_starts)
    for place, (ref, at) in enumerate(row_starts):
        starts[place : place + 1, :] = ref[at : at + 1, :]
    number = (iota((count, LANES), 0) ^ box[0]).astype(jnp.float32)
    coupled = jnp.zeros((rank, rank), jnp.float32)
    for place in range(box_coupling.shape[0]):
        wanted = boxes[0][1:2, 2 + place : 3 + place]
        row = jnp.sum(jnp.where(number == wanted, starts[...], 0.0), axis=0, keepdims=True)
        coupled = coupled + box_coupling[place] * row[:, 0:rank]
    image[...] = part[...]
    box_images(box_basis, jnp.sum(coupled, axis=1, keepdims=True), image)
    sums = tree_sum(
        [
            tree_sum([ref[at + 1 : at + 2, :] for at in range(0, height, span)])
            for ref in boxes
        ]
    )
    square_sum, unknowns = sums[:, 0:1], width * sums[:, 1:2]
    start_scale = jnp.sqrt(square_sum / unknowns + EPSILON)
    one_one = square_sum / (start_scale * start_scale)
    basis_one[...] = initial[...] / start_scale
    message[0:slots, :] = image[...] / start_scale
    numbers[...] = jnp.broadcast_to(lane_row([one_one, unknowns, start_scale]), numbers.shape)
    write_moments(message, basis, message, slots)


def second_near_kernel(subs, box, counts, *refs):
    messages = refs[:subs]
    picks, coupling, basis, box_basis, basis_one, values, near_source = refs[subs : subs + 7]
    part, shares, fields, near_list, arrived = refs[subs + 7 :]
    copy = pltpu.make_async_copy(near_source, near_list, arrived)
    copy.start()
    slots, width = part.shape
    neighbours = near_list.shape[0]
    rank = coupling.shape[1]
    for sub in range(subs):
        fields[sub * slots : (sub + 1) * slots, :] = messages[sub][0:slots, :]

    def target(leaf, carry):
        total = jnp.zeros((width, width), jnp.float32)
        for column in range(neighbours):
            place = near_list[column, leaf] ^ (box[0] * slots)
            total = total + values[leaf * neighbours + column] * fields[pl.ds(place, 1), :]
        part[pl.ds(leaf, 1), :] = jnp.sum(total.T, axis=0, keepdims=True)
        return carry

    moments = jnp.concatenate([ref[slots : 2 * slots, 0:rank] for ref in messages], axis=0)
    local = leaf_part(moments, picks, coupling)
    copy.wait()
    lax.fori_loop(0, slots, target, 0, unroll=True)
    add_leaf_far(counts, local, basis, part)
    first, one, second = messages[0][0:slots, :], basis_one[...], part[...]
    products = [one * first, first * first, one * second, first * second, second * second]
    sums = lane_row([jnp.sum(product, keepdims=True) for product in products])
    lane = iota((1, LANES), 1)
    both = jnp.where(
        lane < rank,
        box_moments(messages[0], box_basis),
        pltpu.roll(box_moments(part, box_basis), rank, 1),
    )
    shares[...] = jnp.where(iota(shares.shape, 0) % 2 == 0, both, sums)


def last_kernel(patches, span, box, *refs):
    boxes, (shares, message, basis_one, part, numbers) = refs[:patches], refs[patches : patches + 5]
    box_basis, box_coupling = refs[patches + 5 : patches + 7]
    basis_three, hessenberg, gather, starts, lists, pairs, image = refs[patches + 7 :]
    slots, rank, width = box_basis.shape
    height = boxes[0].shape[0]
    count = patches * (height // span)
    for place, ref in enumerate(boxes):
        gather[place * height : (place + 1) * height, :] = ref[...]
    for other in range(count):
        row = (box[0] ^ other) * span
        starts[other : other + 1, :] = gather[pl.ds(row, 1), :]
        lists[other : other + 1, :] = gather[pl.ds(row + 1, 1), :]
        pairs[other : other + 1, :] = shares[2 * other : 2 * other + 1, :]
        pairs[count + other : count + other + 1, :] = shares[2 * other + 1 : 2 * other + 2, :]
    first_box, second_box = pairs[0:count, 0:rank], pairs[0:count, rank : 2 * rank]
    parts = [part.astype(jnp.bfloat16) for part in split_three(first_box)]
    lane = iota((count, count), 1).astype(jnp.float32)
    box_local = jnp.zeros((count, rank), jnp.float32)
    for place in range(box_coupling.shape[0]):
        pick = jnp.where(lists[:, 2 + place : 3 + place] == lane, 1.0, 0.0).astype(jnp.bfloat16)
        chosen = jnp.zeros((count, rank), jnp.float32)
        for split in parts:
            chosen = chosen + jnp.dot(pick, split, preferred_element_type=jnp.float32)
        box_local = box_local + lax.dot_general(
            chosen,
            box_coupling[place],
            (((1,), (1,)), ((), ())),
            precision=HIGH_PRECISION,
            preferred_element_type=jnp.float32,
        )
    twice = jnp.concatenate([box_local, box_local], axis=1)
    columns = twice.T
    half = rank // 2
    low = iota((half, 2 * rank), 1) < rank
    quadratic = jnp.zeros((half, 2 * rank), jnp.float32)
    for other in range(count):
        row = (box[0] ^ other) * span + TILE_ROWS
        column = jnp.where(
            low, columns[0:half, other : other + 1], columns[half:rank, other : other + 1]
        )
        quadratic = quadratic + gather[pl.ds(row, half), :] * twice[other : other + 1, :] * column
    one_one, unknowns, start_scale = [numbers[0:1, place : place + 1] for place in range(3)]
    sums = jnp.sum(pairs[count : 2 * count, :], axis=0, keepdims=True)
    along, image_sq, one_part, first_part, part_sq = [
        sums[:, place : place + 1] for place in range(5)
    ]
    one_second = (
        one_part + jnp.sum(starts[:, 0:rank] * box_local, keepdims=True) / start_scale
    )
    first_second = first_part + jnp.sum(first_box * box_local, keepdims=True)
    second_sq = (
        part_sq
        + 2.0 * jnp.sum(second_box * box_local, keepdims=True)
        + jnp.sum(quadratic, keepdims=True)
    )
    upper_first = (0.5 * one_one + along) / unknowns
    shift = upper_first - 0.5
    residual_sq = image_sq - 2.0 * shift * along + shift * shift * one_one
    lower_first = jnp.sqrt(residual_sq / unknowns + EPSILON)
    one_two = (along - shift * one_one) / lower_first
    two_two = residual_sq / (lower_first * lower_first)
    k_one = (one_second - shift * along) / lower_first
    k_two = (
        (first_second - shift * image_sq) - shift * (one_second - shift * along)
    ) / (lower_first * lower_first)
    k_sq = (second_sq - 2.0 * shift * first_second + shift * shift * image_sq) / (
        lower_first * lower_first
    )
    upper_second = (0.5 * one_two + k_one) / unknowns
    middle_second = (0.5 * two_two + k_two - upper_second * one_two) / unknowns
    turn = middle_second - 0.5
    final_sq = (
        k_sq
        - 2.0 * upper_second * k_one
        - 2.0 * turn * k_two
        + upper_second * upper_second * one_one
        + 2.0 * upper_second * turn * one_two
        + turn * turn * two_two
    )
    lower_second = jnp.sqrt(final_sq / unknowns + EPSILON)
    image[...] = part[...]
    own = jnp.where(iota((rank, count), 1) == box[0], columns[0:rank], 0.0)
    box_images(box_basis, jnp.sum(own, axis=1, keepdims=True), image)
    one, first = basis_one[...], message[0:slots, :]
    two = (first - shift * one) / lower_first
    mapped = (image[...] - shift * first) / lower_first
    basis_three[...] = (mapped - upper_second * one - turn * two) / lower_second
    column, row = iota(hessenberg.shape, 0), iota(hessenberg.shape, 1)
    matrix = jnp.where(column == 0, upper_first, upper_second)
    matrix = jnp.where(row == 1, jnp.where(column == 0, lower_first, middle_second), matrix)
    hessenberg[...] = jnp.where(row == 2, jnp.where(column == 0, 0.0, lower_second), matrix)


def shards(
    points,
    normals,
    density,
    counts,
    near_list,
    leaf_far,
    leaf_basis,
    leaf_to_box_transfer,
    leaf_coupling,
    box_far,
    box_coupling,
):
    slots, _, width = points.shape
    neighbours = near_list.shape[1]
    far_count = leaf_far.shape[1]
    subs, patches = lax.axis_size("sub"), lax.axis_size("patch")
    sources = subs * slots
    rows = kept(slots, width)
    this_box = lax.axis_index("patch") * subs + lax.axis_index("sub")
    box = this_box.astype(jnp.int32).reshape(1)
    far_list = leaf_far.T
    rank = leaf_basis.shape[1]
    span = TILE_ROWS + rank // 2
    near_list = near_list.T
    list_scratch = [pltpu.SMEM(near_list.shape, jnp.int32), pltpu.SemaphoreType.DMA]
    block = pltpu.VMEM((sources, width), jnp.float32)

    matrices = [leaf_basis, leaf_coupling, box_coupling]
    geometry, message, box_basis, *matrices = device_call(
        start_kernel,
        [
            kept(slots, 8, width),
            kept(slots + span, LANES),
            kept(*leaf_basis.shape),
            *[kept(*matrix.shape) for matrix in matrices],
        ],
        [counts],
        [],
        [
            pltpu.VMEM((7, slots, width), jnp.float32),
            pltpu.VMEM((slots, width), jnp.float32),
            pltpu.SMEM(box_far.shape, jnp.int32),
            pltpu.VMEM(leaf_to_box_transfer.shape, jnp.float32),
            pltpu.VMEM((3 * rank, slots * width), jnp.bfloat16),
            pltpu.SemaphoreType.DMA((8,)),
        ],
        [
            points.transpose(1, 0, 2),
            normals.transpose(1, 0, 2),
            density,
            box_far,
            leaf_to_box_transfer,
            *matrices,
        ],
    )
    leaf_basis, leaf_coupling, box_coupling = matrices
    geometry = from_peers(geometry, "sub")
    messages = from_peers(message, "sub")
    moments, blocks = device_call(
        functools.partial(join_kernel, subs),
        [kept(sources, LANES), kept(subs * span, LANES)],
        [],
        messages,
    )
    boxes = from_peers(blocks, "patch")
    gather = pltpu.VMEM((patches * subs * span, LANES), jnp.float32)
    part, initial, values, picks = device_call(
        functools.partial(first_near_kernel, subs),
        [
            rows,
            rows,
            kept(slots * neighbours, width, width),
            kept(far_count * slots, sources, dtype=jnp.bfloat16),
        ],
        [box, counts],
        [*geometry, moments, leaf_coupling, leaf_basis],
        [
            pltpu.VMEM((sources, 32, 2 * width), jnp.bfloat16),
            block,
            block,
            pltpu.VMEM((slots, width), jnp.float32),
            pltpu.SMEM(near_list.shape, jnp.int32),
            pltpu.VMEM(far_list.shape, jnp.int32),
            pltpu.SemaphoreType.DMA((2,)),
        ],
        [near_list, far_list],
    )
    message, basis_one, numbers = device_call(
        functools.partial(first_image_kernel, patches, span),
        [kept(2 * slots, LANES), rows, kept(TILE_ROWS, LANES)],
        [box],
        [*boxes, part, initial, leaf_basis, box_basis, box_coupling],
        [
            pltpu.VMEM((patches * subs, LANES), jnp.float32),
            pltpu.VMEM((slots, width), jnp.float32),
        ],
    )
    messages = from_peers(message, "sub")
    part, shares = device_call(
        functools.partial(second_near_kernel, subs),
        [rows, kept(2 * patches * subs, LANES)],
        [box, counts],
        [*messages, picks, leaf_coupling, leaf_basis, box_basis, basis_one, values],
        [block, *list_scratch],
        [near_list],
    )
    shares = lax.all_to_all(shares, ("patch", "sub"), 0, 0, tiled=True)
    basis_three, hessenberg = device_call(
        functools.partial(last_kernel, patches, span),
        [f32(slots, width), f32(2, 3)],
        [box],
        [*boxes, shares, message, basis_one, part, numbers, box_basis, box_coupling],
        [
            gather,
            pltpu.VMEM((patches * subs, LANES), jnp.float32),
            pltpu.VMEM((patches * subs, LANES), jnp.float32),
            pltpu.VMEM((2 * patches * subs, LANES), jnp.float32),
            pltpu.VMEM((slots, width), jnp.float32),
        ],
    )
    return basis_three, hessenberg.T


def solution(mesh):
    spread = ("groups", "patch", "sub")
    in_specs = (
        P(spread, None, None),
        P(spread, None, None),
        P(spread, None),
        P(spread),
        P(spread, None),
        P(spread, None),
        P(spread, None, None),
        P(spread, None, None),
        P(),
        P(spread, None),
        P(),
    )
    out_specs = (P(spread, None), P("groups", None))
    return jax.shard_map(shards, mesh=mesh, in_specs=in_specs, out_specs=out_specs, check_vma=False)
```

```python
import functools
import math

import jax
import jax.numpy as jnp
from jax import lax
from jax.experimental import pallas as pl
from jax.experimental.pallas import tpu as pltpu
from jax.sharding import PartitionSpec as P

SOFTEN = 0.05
EPSILON = 1e-06
KERNEL_SCALE = 0.25 / math.pi
HIGH_PRECISION = lax.Precision.HIGHEST
LANES = 128
TILE_ROWS = 8
VMEM_LIMIT = 16 << 20


def from_peers(value, axis):
    size = lax.axis_size(axis)
    arrived = [
        lax.ppermute(value, axis, [(i, i ^ turn) for i in range(size)]) for turn in range(1, size)
    ]
    return [value] + arrived


def tree_sum(parts):
    while len(parts) > 1:
        parts = [parts[i] + parts[i + 1] for i in range(0, len(parts), 2)]
    return parts[0]


def device_call(kernel, outputs, scalars, arrays, scratch=(), remote=()):
    smem = pl.BlockSpec(memory_space=pltpu.SMEM)
    vmem = pl.BlockSpec(memory_space=pltpu.VMEM)
    hbm = pl.BlockSpec(memory_space=pltpu.HBM)
    return pl.pallas_call(
        kernel,
        out_shape=tuple(outputs),
        in_specs=[smem] * len(scalars) + [vmem] * len(arrays) + [hbm] * len(remote),
        out_specs=tuple([vmem] * len(outputs)),
        scratch_shapes=tuple(scratch),
        compiler_params=pltpu.CompilerParams(vmem_limit_bytes=VMEM_LIMIT),
    )(
        *scalars,
        *[pltpu.with_memory_space_constraint(array, pltpu.VMEM) for array in arrays],
        *[pltpu.with_memory_space_constraint(array, pltpu.HBM) for array in remote],
    )


def kept(*shape, dtype=jnp.float32):
    return pltpu.VMEM(shape, dtype)


def f32(*shape):
    return jax.ShapeDtypeStruct(shape, jnp.float32)


def iota(shape, dimension):
    return lax.broadcasted_iota(jnp.int32, shape, dimension)


def split_three(value):
    first = value.astype(jnp.bfloat16).astype(jnp.float32)
    rest = value - first
    second = rest.astype(jnp.bfloat16).astype(jnp.float32)
    third = (rest - second).astype(jnp.bfloat16).astype(jnp.float32)
    return first, second, third


def lane_row(entries):
    lane = iota((1, LANES), 1)
    row = jnp.zeros((1, LANES), jnp.float32)
    for place, entry in enumerate(entries):
        row = jnp.where(lane == place, entry, row)
    return row


def copy_all(pairs, arrived):
    copies = [
        pltpu.make_async_copy(source, target, arrived.at[place])
        for place, (source, target) in enumerate(pairs)
    ]
    for copy in copies:
        copy.start()
    return copies


def write_moments(vector, basis, message, start):
    slots, rank, _ = basis.shape
    lane = iota((rank, LANES), 1)
    columns = jnp.zeros((rank, LANES), jnp.float32)
    for leaf in range(slots):
        column = jnp.sum(basis[leaf] * vector[leaf : leaf + 1, :], axis=1, keepdims=True)
        columns = jnp.where(lane == leaf, column, columns)
    message[start : start + slots, :] = jnp.zeros((slots, LANES), jnp.float32)
    message[start : start + slots, 0:rank] = columns.T[0:slots]


def box_moments(vector, box_basis):
    slots, rank, width = box_basis.shape
    total = jnp.zeros((rank, width), jnp.float32)
    for leaf in range(slots):
        total = total + box_basis[leaf] * vector[leaf : leaf + 1, :]
    column = jnp.sum(total, axis=1, keepdims=True)
    diagonal = iota((rank, LANES), 0) == iota((rank, LANES), 1)
    return jnp.sum(jnp.where(diagonal, column, 0.0), axis=0, keepdims=True)


def start_kernel(counts, *refs):
    sources, (geometry, message, box_basis) = refs[:8], refs[8:11]
    basis, leaf_coupling, box_coupling = refs[11:14]
    at, initial, box_far, transfer, parts, arrived = refs[14:]
    dims, slots, width = sources[0].shape
    rank = basis.shape[1]
    targets = [at.at[0:dims], at.at[dims : 2 * dims], at.at[2 * dims], box_far]
    targets += [transfer, basis, leaf_coupling, box_coupling]
    copies = copy_all(zip(sources, targets), arrived)
    for copy in copies[:4]:
        copy.wait()
    for row in range(2 * dims):
        geometry[:, row, :] = at[row]
    vector = jnp.where(iota((slots, width), 0) < counts[0], at[2 * dims], 0.0)
    initial[...] = vector
    geometry[:, 2 * dims, :] = vector
    geometry[:, 2 * dims + 1, :] = jnp.zeros_like(vector)
    entries = [jnp.sum(vector * vector, keepdims=True)] + [
        jnp.full((1, 1), value, jnp.int32).astype(jnp.float32)
        for value in [counts[0]] + [box_far[0, place] for place in range(box_far.shape[1])]
    ]
    message[slots : slots + TILE_ROWS, :] = jnp.zeros((TILE_ROWS, LANES), jnp.float32)
    message[slots + 1 : slots + 2, :] = lane_row(entries)
    for copy in copies[4:6]:
        copy.wait()
    for leaf in range(slots):
        product = jnp.dot(
            transfer[leaf],
            basis[leaf],
            precision=HIGH_PRECISION,
            preferred_element_type=jnp.float32,
        )
        product = jnp.where(leaf < counts[0], product, 0.0)
        box_basis[leaf] = product
        split = jnp.concatenate(split_three(product)).astype(jnp.bfloat16)
        parts[:, leaf * width : (leaf + 1) * width] = split
    write_moments(initial, basis, message, 0)
    message[slots : slots + 1, :] = box_moments(initial, box_basis)
    products = lax.dot_general(
        parts[...], parts[...], (((1,), (1,)), ((), ())), preferred_element_type=jnp.float32
    )
    mixed = products[rank : 2 * rank, 0:rank] + products[2 * rank : 3 * rank, 0:rank]
    gram = products[0:rank, 0:rank] + (
        mixed + mixed.T + products[rank : 2 * rank, rank : 2 * rank]
    )
    start, half = slots + TILE_ROWS, rank // 2
    message[start : start + half, 0:rank] = gram[0:half]
    message[start : start + half, rank : 2 * rank] = gram[half:rank]
    for copy in copies[6:]:
        copy.wait()


def join_kernel(subs, *refs):
    messages, (moments, blocks) = refs[:subs], refs[subs:]
    slots, span = moments.shape[0] // subs, blocks.shape[0] // subs
    for sub, message in enumerate(messages):
        moments[sub * slots : (sub + 1) * slots, :] = message[0:slots, :]
        blocks[sub * span : (sub + 1) * span, :] = message[slots : slots + span, :]


def leaf_part(moments, picks, coupling):
    count, rank, _ = coupling.shape
    slots = picks.shape[0] // count
    chosen = jnp.zeros((picks.shape[0], rank), jnp.float32)
    for part in split_three(moments):
        chosen = chosen + jnp.dot(
            picks[...], part.astype(jnp.bfloat16), preferred_element_type=jnp.float32
        )
    local = jnp.zeros((slots, rank), jnp.float32)
    for place in range(count):
        local = local + lax.dot_general(
            chosen[place * slots : (place + 1) * slots],
            coupling[place],
            (((1,), (1,)), ((), ())),
            precision=HIGH_PRECISION,
            preferred_element_type=jnp.float32,
        )
    return local


def wide_transpose(rows):
    count, lanes = rows.shape
    return jnp.concatenate([rows, jnp.zeros((count, LANES - lanes), rows.dtype)], axis=1).T


def add_leaf_far(counts, local, basis, near):
    slots, rank, width = basis.shape
    columns = wide_transpose(local)
    for leaf in range(slots):
        far = jnp.sum(basis[leaf] * columns[0:rank, leaf : leaf + 1], axis=0, keepdims=True)
        near[leaf : leaf + 1, :] = jnp.where(
            leaf < counts[0], near[leaf : leaf + 1, :] + far, 0.0
        )


def first_near_kernel(subs, box, counts, *refs):
    geometry, (moments, coupling, basis) = refs[:subs], refs[subs : subs + 3]
    near_source, far_source, near, initial, values, picks = refs[subs + 3 : subs + 9]
    features, squares, fields, inner, near_list, far_list, arrived = refs[subs + 9 :]
    copies = copy_all([(near_source, near_list), (far_source, far_list)], arrived)
    slots, height, width = geometry[0].shape
    neighbours = near_list.shape[0]
    rank = coupling.shape[1]
    row = iota((height, width), 0)
    scale_square = jnp.where(row < 3, -2.0, 0.0)
    ones = jnp.where(row == 7, 1.0, 0.0)
    scale_normal = jnp.where((row >= 3) & (row < 6), -KERNEL_SCALE, 0.0)

    for sub in range(subs):
        rows = geometry[sub]
        at = [rows[:, component, :] for component in range(7)]
        squares[sub * slots : (sub + 1) * slots, :] = at[0] * at[0] + at[1] * at[1] + at[2] * at[2]
        fields[sub * slots : (sub + 1) * slots, :] = at[6]
        inner[...] = (at[0] * at[3] + at[1] * at[4] + at[2] * at[5]) * KERNEL_SCALE

        def source(leaf, carry, rows=rows, sub=sub):
            place = sub * slots + leaf
            plain = rows[leaf]
            square = squares[pl.ds(place, 1), :] + SOFTEN
            distance = jnp.where(row == 6, square, plain * scale_square + ones)
            numerator = jnp.where(row == 6, inner[pl.ds(leaf, 1), :], plain * scale_normal)
            for part, value in enumerate((distance, numerator)):
                one, two, three = split_three(value)
                lanes = slice(part * width, (part + 1) * width)
                features[place, 0:16, lanes] = jnp.concatenate([one, two]).astype(jnp.bfloat16)
                features[place, 16:32, lanes] = jnp.concatenate([one, three]).astype(jnp.bfloat16)
            return carry

        lax.fori_loop(0, slots, source, 0, unroll=4)

    own = geometry[0]

    def target(leaf, carry):
        plain = own[leaf]
        shifted = pltpu.roll(plain, 3, 0)
        square = squares[pl.ds(leaf, 1), :]
        value = jnp.where(row < 3, plain, jnp.where(row < 6, shifted, jnp.where(row == 6, 1.0, square)))
        one, two, three = split_three(value)
        left = jnp.concatenate([one, one, two, two, three, one]).T.astype(jnp.bfloat16)
        total = jnp.zeros((width, width), jnp.float32)
        for column in range(neighbours):
            place = near_list[column, leaf] ^ (box[0] * slots)
            upper, lower = features[place, 0:16, :], features[place, 16:32, :]
            right = jnp.concatenate([upper, upper, lower], axis=0)
            both = jnp.dot(left, right, preferred_element_type=jnp.float32)
            inverse = lax.rsqrt(both[:, 0:width])
            tile = both[:, width : 2 * width] * (inverse * inverse * inverse)
            values[leaf * neighbours + column] = tile
            total = total + tile * fields[pl.ds(place, 1), :]
        near[pl.ds(leaf, 1), :] = jnp.sum(total.T, axis=0, keepdims=True)
        return carry

    for copy in copies:
        copy.wait()
    far_count, sources = far_list.shape[0], subs * slots
    far_rows = wide_transpose(far_list[...].astype(jnp.float32))
    leaves = (iota((slots, sources), 1) ^ (box[0] * slots)).astype(jnp.float32)
    for place in range(far_count):
        chosen = jnp.where(far_rows[0:slots, place : place + 1] == leaves, 1.0, 0.0)
        picks[place * slots : (place + 1) * slots, :] = chosen.astype(jnp.bfloat16)
    local = leaf_part(moments[:, 0:rank], picks, coupling)
    initial[...] = fields[0:slots, :]
    lax.fori_loop(0, slots, target, 0, unroll=True)
    add_leaf_far(counts, local, basis, near)


def box_images(box_basis, coefficients, image):
    slots, rank, width = box_basis.shape
    spread = jnp.broadcast_to(coefficients, (rank, width))
    for leaf in range(slots):
        image[leaf : leaf + 1, :] += jnp.sum(box_basis[leaf] * spread, axis=0, keepdims=True)


def first_image_kernel(patches, span, box, *refs):
    boxes = refs[:patches]
    part, initial, basis, box_basis, box_coupling = refs[patches : patches + 5]
    message, basis_one, numbers, starts, image = refs[patches + 5 :]
    slots, rank, width = basis.shape
    height = boxes[0].shape[0]
    row_starts = [(ref, at) for ref in boxes for at in range(0, height, span)]
    count = len(row_starts)
    for place, (ref, at) in enumerate(row_starts):
        starts[place : place + 1, :] = ref[at : at + 1, :]
    number = (iota((count, LANES), 0) ^ box[0]).astype(jnp.float32)
    coupled = jnp.zeros((rank, rank), jnp.float32)
    for place in range(box_coupling.shape[0]):
        wanted = boxes[0][1:2, 2 + place : 3 + place]
        row = jnp.sum(jnp.where(number == wanted, starts[...], 0.0), axis=0, keepdims=True)
        coupled = coupled + box_coupling[place] * row[:, 0:rank]
    image[...] = part[...]
    box_images(box_basis, jnp.sum(coupled, axis=1, keepdims=True), image)
    sums = tree_sum(
        [
            tree_sum([ref[at + 1 : at + 2, :] for at in range(0, height, span)])
            for ref in boxes
        ]
    )
    square_sum, unknowns = sums[:, 0:1], width * sums[:, 1:2]
    start_scale = jnp.sqrt(square_sum / unknowns + EPSILON)
    one_one = square_sum / (start_scale * start_scale)
    basis_one[...] = initial[...] / start_scale
    message[0:slots, :] = image[...] / start_scale
    numbers[...] = jnp.broadcast_to(lane_row([one_one, unknowns, start_scale]), numbers.shape)
    write_moments(message, basis, message, slots)


def second_near_kernel(subs, box, counts, *refs):
    messages = refs[:subs]
    picks, coupling, basis, box_basis, basis_one, values, near_source = refs[subs : subs + 7]
    part, shares, fields, near_list, arrived = refs[subs + 7 :]
    copy = pltpu.make_async_copy(near_source, near_list, arrived)
    copy.start()
    slots, width = part.shape
    neighbours = near_list.shape[0]
    rank = coupling.shape[1]
    for sub in range(subs):
        fields[sub * slots : (sub + 1) * slots, :] = messages[sub][0:slots, :]

    def target(leaf, carry):
        total = jnp.zeros((width, width), jnp.float32)
        for column in range(neighbours):
            place = near_list[column, leaf] ^ (box[0] * slots)
            total = total + values[leaf * neighbours + column] * fields[pl.ds(place, 1), :]
        part[pl.ds(leaf, 1), :] = jnp.sum(total.T, axis=0, keepdims=True)
        return carry

    moments = jnp.concatenate([ref[slots : 2 * slots, 0:rank] for ref in messages], axis=0)
    local = leaf_part(moments, picks, coupling)
    copy.wait()
    lax.fori_loop(0, slots, target, 0, unroll=True)
    add_leaf_far(counts, local, basis, part)
    first, one, second = messages[0][0:slots, :], basis_one[...], part[...]
    products = [one * first, first * first, one * second, first * second, second * second]
    sums = lane_row([jnp.sum(product, keepdims=True) for product in products])
    lane = iota((1, LANES), 1)
    both = jnp.where(
        lane < rank,
        box_moments(messages[0], box_basis),
        pltpu.roll(box_moments(part, box_basis), rank, 1),
    )
    shares[...] = jnp.where(iota(shares.shape, 0) % 2 == 0, both, sums)


def last_kernel(patches, span, box, *refs):
    boxes, (shares, message, basis_one, part, numbers) = refs[:patches], refs[patches : patches + 5]
    box_basis, box_coupling = refs[patches + 5 : patches + 7]
    basis_three, hessenberg, gather, starts, lists, pairs, image = refs[patches + 7 :]
    slots, rank, width = box_basis.shape
    height = boxes[0].shape[0]
    count = patches * (height // span)
    for place, ref in enumerate(boxes):
        gather[place * height : (place + 1) * height, :] = ref[...]
    for other in range(count):
        row = (box[0] ^ other) * span
        starts[other : other + 1, :] = gather[pl.ds(row, 1), :]
        lists[other : other + 1, :] = gather[pl.ds(row + 1, 1), :]
        pairs[other : other + 1, :] = shares[2 * other : 2 * other + 1, :]
        pairs[count + other : count + other + 1, :] = shares[2 * other + 1 : 2 * other + 2, :]
    first_box, second_box = pairs[0:count, 0:rank], pairs[0:count, rank : 2 * rank]
    parts = [part.astype(jnp.bfloat16) for part in split_three(first_box)]
    lane = iota((count, count), 1).astype(jnp.float32)
    box_local = jnp.zeros((count, rank), jnp.float32)
    for place in range(box_coupling.shape[0]):
        pick = jnp.where(lists[:, 2 + place : 3 + place] == lane, 1.0, 0.0).astype(jnp.bfloat16)
        chosen = jnp.zeros((count, rank), jnp.float32)
        for split in parts:
            chosen = chosen + jnp.dot(pick, split, preferred_element_type=jnp.float32)
        box_local = box_local + lax.dot_general(
            chosen,
            box_coupling[place],
            (((1,), (1,)), ((), ())),
            precision=HIGH_PRECISION,
            preferred_element_type=jnp.float32,
        )
    twice = jnp.concatenate([box_local, box_local], axis=1)
    columns = twice.T
    half = rank // 2
    low = iota((half, 2 * rank), 1) < rank
    quadratic = jnp.zeros((half, 2 * rank), jnp.float32)
    for other in range(count):
        row = (box[0] ^ other) * span + TILE_ROWS
        column = jnp.where(
            low, columns[0:half, other : other + 1], columns[half:rank, other : other + 1]
        )
        quadratic = quadratic + gather[pl.ds(row, half), :] * twice[other : other + 1, :] * column
    one_one, unknowns, start_scale = [numbers[0:1, place : place + 1] for place in range(3)]
    sums = jnp.sum(pairs[count : 2 * count, :], axis=0, keepdims=True)
    along, image_sq, one_part, first_part, part_sq = [
        sums[:, place : place + 1] for place in range(5)
    ]
    one_second = (
        one_part + jnp.sum(starts[:, 0:rank] * box_local, keepdims=True) / start_scale
    )
    first_second = first_part + jnp.sum(first_box * box_local, keepdims=True)
    second_sq = (
        part_sq
        + 2.0 * jnp.sum(second_box * box_local, keepdims=True)
        + jnp.sum(quadratic, keepdims=True)
    )
    upper_first = (0.5 * one_one + along) / unknowns
    shift = upper_first - 0.5
    residual_sq = image_sq - 2.0 * shift * along + shift * shift * one_one
    lower_first = jnp.sqrt(residual_sq / unknowns + EPSILON)
    one_two = (along - shift * one_one) / lower_first
    two_two = residual_sq / (lower_first * lower_first)
    k_one = (one_second - shift * along) / lower_first
    k_two = (
        (first_second - shift * image_sq) - shift * (one_second - shift * along)
    ) / (lower_first * lower_first)
    k_sq = (second_sq - 2.0 * shift * first_second + shift * shift * image_sq) / (
        lower_first * lower_first
    )
    upper_second = (0.5 * one_two + k_one) / unknowns
    middle_second = (0.5 * two_two + k_two - upper_second * one_two) / unknowns
    turn = middle_second - 0.5
    final_sq = (
        k_sq
        - 2.0 * upper_second * k_one
        - 2.0 * turn * k_two
        + upper_second * upper_second * one_one
        + 2.0 * upper_second * turn * one_two
        + turn * turn * two_two
    )
    lower_second = jnp.sqrt(final_sq / unknowns + EPSILON)
    image[...] = part[...]
    own = jnp.where(iota((rank, count), 1) == box[0], columns[0:rank], 0.0)
    box_images(box_basis, jnp.sum(own, axis=1, keepdims=True), image)
    one, first = basis_one[...], message[0:slots, :]
    two = (first - shift * one) / lower_first
    mapped = (image[...] - shift * first) / lower_first
    basis_three[...] = (mapped - upper_second * one - turn * two) / lower_second
    column, row = iota(hessenberg.shape, 0), iota(hessenberg.shape, 1)
    matrix = jnp.where(column == 0, upper_first, upper_second)
    matrix = jnp.where(row == 1, jnp.where(column == 0, lower_first, middle_second), matrix)
    hessenberg[...] = jnp.where(row == 2, jnp.where(column == 0, 0.0, lower_second), matrix)


def shards(
    points,
    normals,
    density,
    counts,
    near_list,
    leaf_far,
    leaf_basis,
    leaf_to_box_transfer,
    leaf_coupling,
    box_far,
    box_coupling,
):
    slots, _, width = points.shape
    neighbours = near_list.shape[1]
    far_count = leaf_far.shape[1]
    subs, patches = lax.axis_size("sub"), lax.axis_size("patch")
    sources = subs * slots
    rows = kept(slots, width)
    this_box = lax.axis_index("patch") * subs + lax.axis_index("sub")
    box = this_box.astype(jnp.int32).reshape(1)
    far_list = leaf_far.T
    rank = leaf_basis.shape[1]
    span = TILE_ROWS + rank // 2
    near_list = near_list.T
    list_scratch = [pltpu.SMEM(near_list.shape, jnp.int32), pltpu.SemaphoreType.DMA]
    block = pltpu.VMEM((sources, width), jnp.float32)

    matrices = [leaf_basis, leaf_coupling, box_coupling]
    geometry, message, box_basis, *matrices = device_call(
        start_kernel,
        [
            kept(slots, 8, width),
            kept(slots + span, LANES),
            kept(*leaf_basis.shape),
            *[kept(*matrix.shape) for matrix in matrices],
        ],
        [counts],
        [],
        [
            pltpu.VMEM((7, slots, width), jnp.float32),
            pltpu.VMEM((slots, width), jnp.float32),
            pltpu.SMEM(box_far.shape, jnp.int32),
            pltpu.VMEM(leaf_to_box_transfer.shape, jnp.float32),
            pltpu.VMEM((3 * rank, slots * width), jnp.bfloat16),
            pltpu.SemaphoreType.DMA((8,)),
        ],
        [
            points.transpose(1, 0, 2),
            normals.transpose(1, 0, 2),
            density,
            box_far,
            leaf_to_box_transfer,
            *matrices,
        ],
    )
    leaf_basis, leaf_coupling, box_coupling = matrices
    messages = from_peers(message, "sub")
    geometry, messages = lax.optimization_barrier((geometry, messages))
    geometry = from_peers(geometry, "sub")
    moments, blocks = device_call(
        functools.partial(join_kernel, subs),
        [kept(sources, LANES), kept(subs * span, LANES)],
        [],
        messages,
    )
    boxes = from_peers(blocks, "patch")
    gather = pltpu.VMEM((patches * subs * span, LANES), jnp.float32)
    part, initial, values, picks = device_call(
        functools.partial(first_near_kernel, subs),
        [
            rows,
            rows,
            kept(slots * neighbours, width, width),
            kept(far_count * slots, sources, dtype=jnp.bfloat16),
        ],
        [box, counts],
        [*geometry, moments, leaf_coupling, leaf_basis],
        [
            pltpu.VMEM((sources, 32, 2 * width), jnp.bfloat16),
            block,
            block,
            pltpu.VMEM((slots, width), jnp.float32),
            pltpu.SMEM(near_list.shape, jnp.int32),
            pltpu.VMEM(far_list.shape, jnp.int32),
            pltpu.SemaphoreType.DMA((2,)),
        ],
        [near_list, far_list],
    )
    message, basis_one, numbers = device_call(
        functools.partial(first_image_kernel, patches, span),
        [kept(2 * slots, LANES), rows, kept(TILE_ROWS, LANES)],
        [box],
        [*boxes, part, initial, leaf_basis, box_basis, box_coupling],
        [
            pltpu.VMEM((patches * subs, LANES), jnp.float32),
            pltpu.VMEM((slots, width), jnp.float32),
        ],
    )
    messages = from_peers(message, "sub")
    part, shares = device_call(
        functools.partial(second_near_kernel, subs),
        [rows, kept(2 * patches * subs, LANES)],
        [box, counts],
        [*messages, picks, leaf_coupling, leaf_basis, box_basis, basis_one, values],
        [block, *list_scratch],
        [near_list],
    )
    shares = lax.all_to_all(shares, ("patch", "sub"), 0, 0, tiled=True)
    basis_three, hessenberg = device_call(
        functools.partial(last_kernel, patches, span),
        [f32(slots, width), f32(2, 3)],
        [box],
        [*boxes, shares, message, basis_one, part, numbers, box_basis, box_coupling],
        [
            gather,
            pltpu.VMEM((patches * subs, LANES), jnp.float32),
            pltpu.VMEM((patches * subs, LANES), jnp.float32),
            pltpu.VMEM((2 * patches * subs, LANES), jnp.float32),
            pltpu.VMEM((slots, width), jnp.float32),
        ],
    )
    return basis_three, hessenberg.T


def solution(mesh):
    spread = ("groups", "patch", "sub")
    in_specs = (
        P(spread, None, None),
        P(spread, None, None),
        P(spread, None),
        P(spread),
        P(spread, None),
        P(spread, None),
        P(spread, None, None),
        P(spread, None, None),
        P(),
        P(spread, None),
        P(),
    )
    out_specs = (P(spread, None), P("groups", None))
    return jax.shard_map(shards, mesh=mesh, in_specs=in_specs, out_specs=out_specs, check_vma=False)
```

```python
import functools
import math

import jax
import jax.numpy as jnp
from jax import lax
from jax.experimental import pallas as pl
from jax.experimental.pallas import tpu as pltpu
from jax.sharding import PartitionSpec as P

SOFTEN = 0.05
EPSILON = 1e-06
KERNEL_SCALE = 0.25 / math.pi
HIGH_PRECISION = lax.Precision.HIGHEST
LANES = 128
TILE_ROWS = 8
VMEM_LIMIT = 16 << 20
FIRST = pl.CostEstimate(flops=10**11, bytes_accessed=10**10, transcendentals=0)


def from_peers(value, axis):
    size = lax.axis_size(axis)
    arrived = [
        lax.ppermute(value, axis, [(i, i ^ turn) for i in range(size)]) for turn in range(1, size)
    ]
    return [value] + arrived


def tree_sum(parts):
    while len(parts) > 1:
        parts = [parts[i] + parts[i + 1] for i in range(0, len(parts), 2)]
    return parts[0]


def device_call(kernel, outputs, scalars, arrays, scratch=(), remote=(), cost=None):
    smem = pl.BlockSpec(memory_space=pltpu.SMEM)
    vmem = pl.BlockSpec(memory_space=pltpu.VMEM)
    hbm = pl.BlockSpec(memory_space=pltpu.HBM)
    return pl.pallas_call(
        kernel,
        out_shape=tuple(outputs),
        in_specs=[smem] * len(scalars) + [vmem] * len(arrays) + [hbm] * len(remote),
        out_specs=tuple([vmem] * len(outputs)),
        scratch_shapes=tuple(scratch),
        compiler_params=pltpu.CompilerParams(vmem_limit_bytes=VMEM_LIMIT),
        cost_estimate=cost,
    )(
        *scalars,
        *[pltpu.with_memory_space_constraint(array, pltpu.VMEM) for array in arrays],
        *[pltpu.with_memory_space_constraint(array, pltpu.HBM) for array in remote],
    )


def kept(*shape, dtype=jnp.float32):
    return pltpu.VMEM(shape, dtype)


def f32(*shape):
    return jax.ShapeDtypeStruct(shape, jnp.float32)


def iota(shape, dimension):
    return lax.broadcasted_iota(jnp.int32, shape, dimension)


def split_three(value):
    first = value.astype(jnp.bfloat16).astype(jnp.float32)
    rest = value - first
    second = rest.astype(jnp.bfloat16).astype(jnp.float32)
    third = (rest - second).astype(jnp.bfloat16).astype(jnp.float32)
    return first, second, third


def lane_row(entries):
    lane = iota((1, LANES), 1)
    row = jnp.zeros((1, LANES), jnp.float32)
    for place, entry in enumerate(entries):
        row = jnp.where(lane == place, entry, row)
    return row


def copy_all(pairs, arrived):
    copies = [
        pltpu.make_async_copy(source, target, arrived.at[place])
        for place, (source, target) in enumerate(pairs)
    ]
    for copy in copies:
        copy.start()
    return copies


def write_moments(vector, basis, message, start):
    slots, rank, _ = basis.shape
    lane = iota((rank, LANES), 1)
    columns = jnp.zeros((rank, LANES), jnp.float32)
    for leaf in range(slots):
        column = jnp.sum(basis[leaf] * vector[leaf : leaf + 1, :], axis=1, keepdims=True)
        columns = jnp.where(lane == leaf, column, columns)
    message[start : start + slots, :] = jnp.zeros((slots, LANES), jnp.float32)
    message[start : start + slots, 0:rank] = columns.T[0:slots]


def box_moments(vector, box_basis):
    slots, rank, width = box_basis.shape
    total = jnp.zeros((rank, width), jnp.float32)
    for leaf in range(slots):
        total = total + box_basis[leaf] * vector[leaf : leaf + 1, :]
    column = jnp.sum(total, axis=1, keepdims=True)
    diagonal = iota((rank, LANES), 0) == iota((rank, LANES), 1)
    return jnp.sum(jnp.where(diagonal, column, 0.0), axis=0, keepdims=True)


def start_kernel(counts, *refs):
    sources, (geometry, message, box_basis) = refs[:8], refs[8:11]
    basis, leaf_coupling, box_coupling = refs[11:14]
    at, initial, box_far, transfer, parts, arrived = refs[14:]
    dims, slots, width = sources[0].shape
    rank = basis.shape[1]
    targets = [at.at[0:dims], at.at[dims : 2 * dims], at.at[2 * dims], box_far]
    targets += [transfer, basis, leaf_coupling, box_coupling]
    copies = copy_all(zip(sources, targets), arrived)
    for copy in copies[:4]:
        copy.wait()
    for row in range(2 * dims):
        geometry[:, row, :] = at[row]
    vector = jnp.where(iota((slots, width), 0) < counts[0], at[2 * dims], 0.0)
    initial[...] = vector
    geometry[:, 2 * dims, :] = vector
    geometry[:, 2 * dims + 1, :] = jnp.zeros_like(vector)
    entries = [jnp.sum(vector * vector, keepdims=True)] + [
        jnp.full((1, 1), value, jnp.int32).astype(jnp.float32)
        for value in [counts[0]] + [box_far[0, place] for place in range(box_far.shape[1])]
    ]
    message[slots : slots + TILE_ROWS, :] = jnp.zeros((TILE_ROWS, LANES), jnp.float32)
    message[slots + 1 : slots + 2, :] = lane_row(entries)
    for copy in copies[4:6]:
        copy.wait()
    for leaf in range(slots):
        product = jnp.dot(
            transfer[leaf],
            basis[leaf],
            precision=HIGH_PRECISION,
            preferred_element_type=jnp.float32,
        )
        product = jnp.where(leaf < counts[0], product, 0.0)
        box_basis[leaf] = product
        split = jnp.concatenate(split_three(product)).astype(jnp.bfloat16)
        parts[:, leaf * width : (leaf + 1) * width] = split
    write_moments(initial, basis, message, 0)
    message[slots : slots + 1, :] = box_moments(initial, box_basis)
    products = lax.dot_general(
        parts[...], parts[...], (((1,), (1,)), ((), ())), preferred_element_type=jnp.float32
    )
    mixed = products[rank : 2 * rank, 0:rank] + products[2 * rank : 3 * rank, 0:rank]
    gram = products[0:rank, 0:rank] + (
        mixed + mixed.T + products[rank : 2 * rank, rank : 2 * rank]
    )
    start, half = slots + TILE_ROWS, rank // 2
    message[start : start + half, 0:rank] = gram[0:half]
    message[start : start + half, rank : 2 * rank] = gram[half:rank]
    for copy in copies[6:]:
        copy.wait()


def join_kernel(subs, *refs):
    messages, (moments, blocks) = refs[:subs], refs[subs:]
    slots, span = moments.shape[0] // subs, blocks.shape[0] // subs
    for sub, message in enumerate(messages):
        moments[sub * slots : (sub + 1) * slots, :] = message[0:slots, :]
        blocks[sub * span : (sub + 1) * span, :] = message[slots : slots + span, :]


def leaf_part(moments, picks, coupling):
    count, rank, _ = coupling.shape
    slots = picks.shape[0] // count
    chosen = jnp.zeros((picks.shape[0], rank), jnp.float32)
    for part in split_three(moments):
        chosen = chosen + jnp.dot(
            picks[...], part.astype(jnp.bfloat16), preferred_element_type=jnp.float32
        )
    local = jnp.zeros((slots, rank), jnp.float32)
    for place in range(count):
        local = local + lax.dot_general(
            chosen[place * slots : (place + 1) * slots],
            coupling[place],
            (((1,), (1,)), ((), ())),
            precision=HIGH_PRECISION,
            preferred_element_type=jnp.float32,
        )
    return local


def wide_transpose(rows):
    count, lanes = rows.shape
    return jnp.concatenate([rows, jnp.zeros((count, LANES - lanes), rows.dtype)], axis=1).T


def add_leaf_far(counts, local, basis, near):
    slots, rank, width = basis.shape
    columns = wide_transpose(local)
    for leaf in range(slots):
        far = jnp.sum(basis[leaf] * columns[0:rank, leaf : leaf + 1], axis=0, keepdims=True)
        near[leaf : leaf + 1, :] = jnp.where(
            leaf < counts[0], near[leaf : leaf + 1, :] + far, 0.0
        )


def first_near_kernel(subs, box, counts, *refs):
    geometry, (moments, coupling, basis) = refs[:subs], refs[subs : subs + 3]
    near_source, far_source, near, initial, values, picks = refs[subs + 3 : subs + 9]
    features, squares, fields, inner, near_list, far_list, arrived = refs[subs + 9 :]
    copies = copy_all([(near_source, near_list), (far_source, far_list)], arrived)
    slots, height, width = geometry[0].shape
    neighbours = near_list.shape[0]
    rank = coupling.shape[1]
    row = iota((height, width), 0)
    scale_square = jnp.where(row < 3, -2.0, 0.0)
    ones = jnp.where(row == 7, 1.0, 0.0)
    scale_normal = jnp.where((row >= 3) & (row < 6), -KERNEL_SCALE, 0.0)

    for sub in range(subs):
        rows = geometry[sub]
        at = [rows[:, component, :] for component in range(7)]
        squares[sub * slots : (sub + 1) * slots, :] = at[0] * at[0] + at[1] * at[1] + at[2] * at[2]
        fields[sub * slots : (sub + 1) * slots, :] = at[6]
        inner[...] = (at[0] * at[3] + at[1] * at[4] + at[2] * at[5]) * KERNEL_SCALE

        def source(leaf, carry, rows=rows, sub=sub):
            place = sub * slots + leaf
            plain = rows[leaf]
            square = squares[pl.ds(place, 1), :] + SOFTEN
            distance = jnp.where(row == 6, square, plain * scale_square + ones)
            numerator = jnp.where(row == 6, inner[pl.ds(leaf, 1), :], plain * scale_normal)
            for part, value in enumerate((distance, numerator)):
                one, two, three = split_three(value)
                lanes = slice(part * width, (part + 1) * width)
                features[place, 0:16, lanes] = jnp.concatenate([one, two]).astype(jnp.bfloat16)
                features[place, 16:32, lanes] = jnp.concatenate([one, three]).astype(jnp.bfloat16)
            return carry

        lax.fori_loop(0, slots, source, 0, unroll=4)

    own = geometry[0]

    def target(leaf, carry):
        plain = own[leaf]
        shifted = pltpu.roll(plain, 3, 0)
        square = squares[pl.ds(leaf, 1), :]
        value = jnp.where(row < 3, plain, jnp.where(row < 6, shifted, jnp.where(row == 6, 1.0, square)))
        one, two, three = split_three(value)
        left = jnp.concatenate([one, one, two, two, three, one]).T.astype(jnp.bfloat16)
        total = jnp.zeros((width, width), jnp.float32)
        for column in range(neighbours):
            place = near_list[column, leaf] ^ (box[0] * slots)
            upper, lower = features[place, 0:16, :], features[place, 16:32, :]
            right = jnp.concatenate([upper, upper, lower], axis=0)
            both = jnp.dot(left, right, preferred_element_type=jnp.float32)
            inverse = lax.rsqrt(both[:, 0:width])
            tile = both[:, width : 2 * width] * (inverse * inverse * inverse)
            values[leaf * neighbours + column] = tile
            total = total + tile * fields[pl.ds(place, 1), :]
        near[pl.ds(leaf, 1), :] = jnp.sum(total.T, axis=0, keepdims=True)
        return carry

    for copy in copies:
        copy.wait()
    far_count, sources = far_list.shape[0], subs * slots
    far_rows = wide_transpose(far_list[...].astype(jnp.float32))
    leaves = (iota((slots, sources), 1) ^ (box[0] * slots)).astype(jnp.float32)
    for place in range(far_count):
        chosen = jnp.where(far_rows[0:slots, place : place + 1] == leaves, 1.0, 0.0)
        picks[place * slots : (place + 1) * slots, :] = chosen.astype(jnp.bfloat16)
    local = leaf_part(moments[:, 0:rank], picks, coupling)
    initial[...] = fields[0:slots, :]
    lax.fori_loop(0, slots, target, 0, unroll=True)
    add_leaf_far(counts, local, basis, near)


def box_images(box_basis, coefficients, image):
    slots, rank, width = box_basis.shape
    spread = jnp.broadcast_to(coefficients, (rank, width))
    for leaf in range(slots):
        image[leaf : leaf + 1, :] += jnp.sum(box_basis[leaf] * spread, axis=0, keepdims=True)


def first_image_kernel(patches, span, box, *refs):
    boxes = refs[:patches]
    part, initial, basis, box_basis, box_coupling = refs[patches : patches + 5]
    message, basis_one, numbers, starts, image = refs[patches + 5 :]
    slots, rank, width = basis.shape
    height = boxes[0].shape[0]
    row_starts = [(ref, at) for ref in boxes for at in range(0, height, span)]
    count = len(row_starts)
    for place, (ref, at) in enumerate(row_starts):
        starts[place : place + 1, :] = ref[at : at + 1, :]
    number = (iota((count, LANES), 0) ^ box[0]).astype(jnp.float32)
    coupled = jnp.zeros((rank, rank), jnp.float32)
    for place in range(box_coupling.shape[0]):
        wanted = boxes[0][1:2, 2 + place : 3 + place]
        row = jnp.sum(jnp.where(number == wanted, starts[...], 0.0), axis=0, keepdims=True)
        coupled = coupled + box_coupling[place] * row[:, 0:rank]
    image[...] = part[...]
    box_images(box_basis, jnp.sum(coupled, axis=1, keepdims=True), image)
    sums = tree_sum(
        [
            tree_sum([ref[at + 1 : at + 2, :] for at in range(0, height, span)])
            for ref in boxes
        ]
    )
    square_sum, unknowns = sums[:, 0:1], width * sums[:, 1:2]
    start_scale = jnp.sqrt(square_sum / unknowns + EPSILON)
    one_one = square_sum / (start_scale * start_scale)
    basis_one[...] = initial[...] / start_scale
    message[0:slots, :] = image[...] / start_scale
    numbers[...] = jnp.broadcast_to(lane_row([one_one, unknowns, start_scale]), numbers.shape)
    write_moments(message, basis, message, slots)


def second_near_kernel(subs, box, counts, *refs):
    messages = refs[:subs]
    picks, coupling, basis, box_basis, basis_one, values, near_source = refs[subs : subs + 7]
    part, shares, fields, near_list, arrived = refs[subs + 7 :]
    copy = pltpu.make_async_copy(near_source, near_list, arrived)
    copy.start()
    slots, width = part.shape
    neighbours = near_list.shape[0]
    rank = coupling.shape[1]
    for sub in range(subs):
        fields[sub * slots : (sub + 1) * slots, :] = messages[sub][0:slots, :]

    def target(leaf, carry):
        total = jnp.zeros((width, width), jnp.float32)
        for column in range(neighbours):
            place = near_list[column, leaf] ^ (box[0] * slots)
            total = total + values[leaf * neighbours + column] * fields[pl.ds(place, 1), :]
        part[pl.ds(leaf, 1), :] = jnp.sum(total.T, axis=0, keepdims=True)
        return carry

    moments = jnp.concatenate([ref[slots : 2 * slots, 0:rank] for ref in messages], axis=0)
    local = leaf_part(moments, picks, coupling)
    copy.wait()
    lax.fori_loop(0, slots, target, 0, unroll=True)
    add_leaf_far(counts, local, basis, part)
    first, one, second = messages[0][0:slots, :], basis_one[...], part[...]
    products = [one * first, first * first, one * second, first * second, second * second]
    sums = lane_row([jnp.sum(product, keepdims=True) for product in products])
    lane = iota((1, LANES), 1)
    both = jnp.where(
        lane < rank,
        box_moments(messages[0], box_basis),
        pltpu.roll(box_moments(part, box_basis), rank, 1),
    )
    shares[...] = jnp.where(iota(shares.shape, 0) % 2 == 0, both, sums)


def last_kernel(patches, span, box, *refs):
    boxes, (shares, message, basis_one, part, numbers) = refs[:patches], refs[patches : patches + 5]
    box_basis, box_coupling = refs[patches + 5 : patches + 7]
    basis_three, hessenberg, gather, starts, lists, pairs, image = refs[patches + 7 :]
    slots, rank, width = box_basis.shape
    height = boxes[0].shape[0]
    count = patches * (height // span)
    for place, ref in enumerate(boxes):
        gather[place * height : (place + 1) * height, :] = ref[...]
    for other in range(count):
        row = (box[0] ^ other) * span
        starts[other : other + 1, :] = gather[pl.ds(row, 1), :]
        lists[other : other + 1, :] = gather[pl.ds(row + 1, 1), :]
        pairs[other : other + 1, :] = shares[2 * other : 2 * other + 1, :]
        pairs[count + other : count + other + 1, :] = shares[2 * other + 1 : 2 * other + 2, :]
    first_box, second_box = pairs[0:count, 0:rank], pairs[0:count, rank : 2 * rank]
    parts = [part.astype(jnp.bfloat16) for part in split_three(first_box)]
    lane = iota((count, count), 1).astype(jnp.float32)
    box_local = jnp.zeros((count, rank), jnp.float32)
    for place in range(box_coupling.shape[0]):
        pick = jnp.where(lists[:, 2 + place : 3 + place] == lane, 1.0, 0.0).astype(jnp.bfloat16)
        chosen = jnp.zeros((count, rank), jnp.float32)
        for split in parts:
            chosen = chosen + jnp.dot(pick, split, preferred_element_type=jnp.float32)
        box_local = box_local + lax.dot_general(
            chosen,
            box_coupling[place],
            (((1,), (1,)), ((), ())),
            precision=HIGH_PRECISION,
            preferred_element_type=jnp.float32,
        )
    twice = jnp.concatenate([box_local, box_local], axis=1)
    columns = twice.T
    half = rank // 2
    low = iota((half, 2 * rank), 1) < rank
    quadratic = jnp.zeros((half, 2 * rank), jnp.float32)
    for other in range(count):
        row = (box[0] ^ other) * span + TILE_ROWS
        column = jnp.where(
            low, columns[0:half, other : other + 1], columns[half:rank, other : other + 1]
        )
        quadratic = quadratic + gather[pl.ds(row, half), :] * twice[other : other + 1, :] * column
    one_one, unknowns, start_scale = [numbers[0:1, place : place + 1] for place in range(3)]
    sums = jnp.sum(pairs[count : 2 * count, :], axis=0, keepdims=True)
    along, image_sq, one_part, first_part, part_sq = [
        sums[:, place : place + 1] for place in range(5)
    ]
    one_second = (
        one_part + jnp.sum(starts[:, 0:rank] * box_local, keepdims=True) / start_scale
    )
    first_second = first_part + jnp.sum(first_box * box_local, keepdims=True)
    second_sq = (
        part_sq
        + 2.0 * jnp.sum(second_box * box_local, keepdims=True)
        + jnp.sum(quadratic, keepdims=True)
    )
    upper_first = (0.5 * one_one + along) / unknowns
    shift = upper_first - 0.5
    residual_sq = image_sq - 2.0 * shift * along + shift * shift * one_one
    lower_first = jnp.sqrt(residual_sq / unknowns + EPSILON)
    one_two = (along - shift * one_one) / lower_first
    two_two = residual_sq / (lower_first * lower_first)
    k_one = (one_second - shift * along) / lower_first
    k_two = (
        (first_second - shift * image_sq) - shift * (one_second - shift * along)
    ) / (lower_first * lower_first)
    k_sq = (second_sq - 2.0 * shift * first_second + shift * shift * image_sq) / (
        lower_first * lower_first
    )
    upper_second = (0.5 * one_two + k_one) / unknowns
    middle_second = (0.5 * two_two + k_two - upper_second * one_two) / unknowns
    turn = middle_second - 0.5
    final_sq = (
        k_sq
        - 2.0 * upper_second * k_one
        - 2.0 * turn * k_two
        + upper_second * upper_second * one_one
        + 2.0 * upper_second * turn * one_two
        + turn * turn * two_two
    )
    lower_second = jnp.sqrt(final_sq / unknowns + EPSILON)
    image[...] = part[...]
    own = jnp.where(iota((rank, count), 1) == box[0], columns[0:rank], 0.0)
    box_images(box_basis, jnp.sum(own, axis=1, keepdims=True), image)
    one, first = basis_one[...], message[0:slots, :]
    two = (first - shift * one) / lower_first
    mapped = (image[...] - shift * first) / lower_first
    basis_three[...] = (mapped - upper_second * one - turn * two) / lower_second
    column, row = iota(hessenberg.shape, 0), iota(hessenberg.shape, 1)
    matrix = jnp.where(column == 0, upper_first, upper_second)
    matrix = jnp.where(row == 1, jnp.where(column == 0, lower_first, middle_second), matrix)
    hessenberg[...] = jnp.where(row == 2, jnp.where(column == 0, 0.0, lower_second), matrix)


def shards(
    points,
    normals,
    density,
    counts,
    near_list,
    leaf_far,
    leaf_basis,
    leaf_to_box_transfer,
    leaf_coupling,
    box_far,
    box_coupling,
):
    slots, _, width = points.shape
    neighbours = near_list.shape[1]
    far_count = leaf_far.shape[1]
    subs, patches = lax.axis_size("sub"), lax.axis_size("patch")
    sources = subs * slots
    rows = kept(slots, width)
    this_box = lax.axis_index("patch") * subs + lax.axis_index("sub")
    box = this_box.astype(jnp.int32).reshape(1)
    far_list = leaf_far.T
    rank = leaf_basis.shape[1]
    span = TILE_ROWS + rank // 2
    near_list = near_list.T
    list_scratch = [pltpu.SMEM(near_list.shape, jnp.int32), pltpu.SemaphoreType.DMA]
    block = pltpu.VMEM((sources, width), jnp.float32)

    matrices = [leaf_basis, leaf_coupling, box_coupling]
    geometry, message, box_basis, *matrices = device_call(
        start_kernel,
        [
            kept(slots, 8, width),
            kept(slots + span, LANES),
            kept(*leaf_basis.shape),
            *[kept(*matrix.shape) for matrix in matrices],
        ],
        [counts],
        [],
        [
            pltpu.VMEM((7, slots, width), jnp.float32),
            pltpu.VMEM((slots, width), jnp.float32),
            pltpu.SMEM(box_far.shape, jnp.int32),
            pltpu.VMEM(leaf_to_box_transfer.shape, jnp.float32),
            pltpu.VMEM((3 * rank, slots * width), jnp.bfloat16),
            pltpu.SemaphoreType.DMA((8,)),
        ],
        [
            points.transpose(1, 0, 2),
            normals.transpose(1, 0, 2),
            density,
            box_far,
            leaf_to_box_transfer,
            *matrices,
        ],
    )
    leaf_basis, leaf_coupling, box_coupling = matrices
    messages = from_peers(message, "sub")
    geometry = from_peers(geometry, "sub")
    moments, blocks = device_call(
        functools.partial(join_kernel, subs),
        [kept(sources, LANES), kept(subs * span, LANES)],
        [],
        messages,
        cost=FIRST,
    )
    boxes = from_peers(blocks, "patch")
    gather = pltpu.VMEM((patches * subs * span, LANES), jnp.float32)
    part, initial, values, picks = device_call(
        functools.partial(first_near_kernel, subs),
        [
            rows,
            rows,
            kept(slots * neighbours, width, width),
            kept(far_count * slots, sources, dtype=jnp.bfloat16),
        ],
        [box, counts],
        [*geometry, moments, leaf_coupling, leaf_basis],
        [
            pltpu.VMEM((sources, 32, 2 * width), jnp.bfloat16),
            block,
            block,
            pltpu.VMEM((slots, width), jnp.float32),
            pltpu.SMEM(near_list.shape, jnp.int32),
            pltpu.VMEM(far_list.shape, jnp.int32),
            pltpu.SemaphoreType.DMA((2,)),
        ],
        [near_list, far_list],
    )
    message, basis_one, numbers = device_call(
        functools.partial(first_image_kernel, patches, span),
        [kept(2 * slots, LANES), rows, kept(TILE_ROWS, LANES)],
        [box],
        [*boxes, part, initial, leaf_basis, box_basis, box_coupling],
        [
            pltpu.VMEM((patches * subs, LANES), jnp.float32),
            pltpu.VMEM((slots, width), jnp.float32),
        ],
    )
    messages = from_peers(message, "sub")
    part, shares = device_call(
        functools.partial(second_near_kernel, subs),
        [rows, kept(2 * patches * subs, LANES)],
        [box, counts],
        [*messages, picks, leaf_coupling, leaf_basis, box_basis, basis_one, values],
        [block, *list_scratch],
        [near_list],
    )
    shares = lax.all_to_all(shares, ("patch", "sub"), 0, 0, tiled=True)
    basis_three, hessenberg = device_call(
        functools.partial(last_kernel, patches, span),
        [f32(slots, width), f32(2, 3)],
        [box],
        [*boxes, shares, message, basis_one, part, numbers, box_basis, box_coupling],
        [
            gather,
            pltpu.VMEM((patches * subs, LANES), jnp.float32),
            pltpu.VMEM((patches * subs, LANES), jnp.float32),
            pltpu.VMEM((2 * patches * subs, LANES), jnp.float32),
            pltpu.VMEM((slots, width), jnp.float32),
        ],
    )
    return basis_three, hessenberg.T


def solution(mesh):
    spread = ("groups", "patch", "sub")
    in_specs = (
        P(spread, None, None),
        P(spread, None, None),
        P(spread, None),
        P(spread),
        P(spread, None),
        P(spread, None),
        P(spread, None, None),
        P(spread, None, None),
        P(),
        P(spread, None),
        P(),
    )
    out_specs = (P(spread, None), P("groups", None))
    return jax.shard_map(shards, mesh=mesh, in_specs=in_specs, out_specs=out_specs, check_vma=False)
```

```python
import functools
import math

import jax
import jax.numpy as jnp
from jax import lax
from jax.experimental import pallas as pl
from jax.experimental.pallas import tpu as pltpu
from jax.sharding import PartitionSpec as P

SOFTEN = 0.05
EPSILON = 1e-06
KERNEL_SCALE = 0.25 / math.pi
HIGH_PRECISION = lax.Precision.HIGHEST
LANES = 128
TILE_ROWS = 8
VMEM_LIMIT = 16 << 20
CHUNKS = 4
FIRST = pl.CostEstimate(flops=10**11, bytes_accessed=10**10, transcendentals=0)


def from_peers(value, axis):
    size = lax.axis_size(axis)
    arrived = [
        lax.ppermute(value, axis, [(i, i ^ turn) for i in range(size)]) for turn in range(1, size)
    ]
    return [value] + arrived


def tree_sum(parts):
    while len(parts) > 1:
        parts = [parts[i] + parts[i + 1] for i in range(0, len(parts), 2)]
    return parts[0]


def device_call(kernel, outputs, scalars, arrays, scratch=(), remote=(), cost=None):
    smem = pl.BlockSpec(memory_space=pltpu.SMEM)
    vmem = pl.BlockSpec(memory_space=pltpu.VMEM)
    hbm = pl.BlockSpec(memory_space=pltpu.HBM)
    return pl.pallas_call(
        kernel,
        out_shape=tuple(outputs),
        in_specs=[smem] * len(scalars) + [vmem] * len(arrays) + [hbm] * len(remote),
        out_specs=tuple([vmem] * len(outputs)),
        scratch_shapes=tuple(scratch),
        compiler_params=pltpu.CompilerParams(vmem_limit_bytes=VMEM_LIMIT),
        cost_estimate=cost,
    )(
        *scalars,
        *[pltpu.with_memory_space_constraint(array, pltpu.VMEM) for array in arrays],
        *[pltpu.with_memory_space_constraint(array, pltpu.HBM) for array in remote],
    )


def kept(*shape, dtype=jnp.float32):
    return pltpu.VMEM(shape, dtype)


def f32(*shape):
    return jax.ShapeDtypeStruct(shape, jnp.float32)


def iota(shape, dimension):
    return lax.broadcasted_iota(jnp.int32, shape, dimension)


def split_three(value):
    first = value.astype(jnp.bfloat16).astype(jnp.float32)
    rest = value - first
    second = rest.astype(jnp.bfloat16).astype(jnp.float32)
    third = (rest - second).astype(jnp.bfloat16).astype(jnp.float32)
    return first, second, third


def lane_row(entries):
    lane = iota((1, LANES), 1)
    row = jnp.zeros((1, LANES), jnp.float32)
    for place, entry in enumerate(entries):
        row = jnp.where(lane == place, entry, row)
    return row


def copy_all(pairs, arrived):
    copies = [
        pltpu.make_async_copy(source, target, arrived.at[place])
        for place, (source, target) in enumerate(pairs)
    ]
    for copy in copies:
        copy.start()
    return copies


def write_moments(vector, basis, message, start):
    slots, rank, _ = basis.shape
    lane = iota((rank, LANES), 1)
    columns = jnp.zeros((rank, LANES), jnp.float32)
    for leaf in range(slots):
        column = jnp.sum(basis[leaf] * vector[leaf : leaf + 1, :], axis=1, keepdims=True)
        columns = jnp.where(lane == leaf, column, columns)
    message[start : start + slots, :] = jnp.zeros((slots, LANES), jnp.float32)
    message[start : start + slots, 0:rank] = columns.T[0:slots]


def box_moments(vector, box_basis):
    slots, rank, width = box_basis.shape
    total = jnp.zeros((rank, width), jnp.float32)
    for leaf in range(slots):
        total = total + box_basis[leaf] * vector[leaf : leaf + 1, :]
    column = jnp.sum(total, axis=1, keepdims=True)
    diagonal = iota((rank, LANES), 0) == iota((rank, LANES), 1)
    return jnp.sum(jnp.where(diagonal, column, 0.0), axis=0, keepdims=True)


def start_kernel(counts, *refs):
    sources, (geometry, message, box_basis) = refs[:8], refs[8:11]
    basis, leaf_coupling, box_coupling = refs[11:14]
    at, initial, box_far, transfer, parts, arrived = refs[14:]
    dims, slots, width = sources[0].shape
    rank = basis.shape[1]
    targets = [at.at[0:dims], at.at[dims : 2 * dims], at.at[2 * dims], box_far]
    pairs = list(zip(sources[:4], targets))
    step = slots // CHUNKS
    for first in range(0, slots, step):
        for source, target in zip(sources[4:6], (transfer, basis)):
            pairs.append((source.at[first : first + step], target.at[first : first + step]))
    pairs += zip(sources[6:], (leaf_coupling, box_coupling))
    copies = copy_all(pairs, arrived)
    for copy in copies[:4]:
        copy.wait()
    for row in range(2 * dims):
        geometry[:, row, :] = at[row]
    vector = jnp.where(iota((slots, width), 0) < counts[0], at[2 * dims], 0.0)
    initial[...] = vector
    geometry[:, 2 * dims, :] = vector
    geometry[:, 2 * dims + 1, :] = jnp.zeros_like(vector)
    entries = [jnp.sum(vector * vector, keepdims=True)] + [
        jnp.full((1, 1), value, jnp.int32).astype(jnp.float32)
        for value in [counts[0]] + [box_far[0, place] for place in range(box_far.shape[1])]
    ]
    message[slots : slots + TILE_ROWS, :] = jnp.zeros((TILE_ROWS, LANES), jnp.float32)
    message[slots + 1 : slots + 2, :] = lane_row(entries)
    for leaf in range(slots):
        if leaf % step == 0:
            for copy in copies[4 + 2 * (leaf // step) : 6 + 2 * (leaf // step)]:
                copy.wait()
        product = jnp.dot(
            transfer[leaf],
            basis[leaf],
            precision=HIGH_PRECISION,
            preferred_element_type=jnp.float32,
        )
        product = jnp.where(leaf < counts[0], product, 0.0)
        box_basis[leaf] = product
        parts[:, leaf * width : (leaf + 1) * width] = split_rows(product)
    write_moments(initial, basis, message, 0)
    message[slots : slots + 1, :] = box_moments(initial, box_basis)
    products = lax.dot_general(
        parts[...], parts[...], (((1,), (1,)), ((), ())), preferred_element_type=jnp.float32
    )
    mixed = products[rank : 2 * rank, 0:rank] + products[2 * rank : 3 * rank, 0:rank]
    gram = products[0:rank, 0:rank] + (
        mixed + mixed.T + products[rank : 2 * rank, rank : 2 * rank]
    )
    start, half = slots + TILE_ROWS, rank // 2
    message[start : start + half, 0:rank] = gram[0:half]
    message[start : start + half, rank : 2 * rank] = gram[half:rank]
    for copy in copies[4 + 2 * CHUNKS :]:
        copy.wait()


def join_kernel(subs, *refs):
    messages, (moments, blocks) = refs[:subs], refs[subs:]
    slots, span = moments.shape[0] // subs, blocks.shape[0] // subs
    for sub, message in enumerate(messages):
        moments[sub * slots : (sub + 1) * slots, :] = message[0:slots, :]
        blocks[sub * span : (sub + 1) * span, :] = message[slots : slots + span, :]


def split_rows(rows):
    return jnp.concatenate(split_three(rows)).astype(jnp.bfloat16)


def write_weights(coupling, weights):
    for place in range(coupling.shape[0]):
        parts = jnp.concatenate(split_three(coupling[place].T), axis=1)
        weights[place] = parts.astype(jnp.bfloat16)


def coupled_rows(chosen, weights):
    total = None
    for place in range(weights.shape[0]):
        product = jnp.dot(chosen(place), weights[place], preferred_element_type=jnp.float32)
        total = product if total is None else total + product
    count, rank = total.shape[0] // 3, total.shape[1] // 3
    part = [
        [total[row * count : (row + 1) * count, at * rank : (at + 1) * rank] for at in range(3)]
        for row in range(3)
    ]
    return part[0][0] + (
        (part[0][1] + part[1][0]) + (part[0][2] + part[2][0] + part[1][1])
    )


def leaf_part(moments, picks, weights):
    slots = picks.shape[0] // weights.shape[0]
    parts = [
        jnp.dot(
            picks[...], part.astype(jnp.bfloat16), preferred_element_type=jnp.float32
        ).astype(jnp.bfloat16)
        for part in split_three(moments)
    ]

    def chosen(place):
        return jnp.concatenate([part[place * slots : (place + 1) * slots] for part in parts])

    return coupled_rows(chosen, weights)


def wide_transpose(rows):
    count, lanes = rows.shape
    return jnp.concatenate([rows, jnp.zeros((count, LANES - lanes), rows.dtype)], axis=1).T


def add_leaf_far(counts, local, basis, near):
    slots, rank, width = basis.shape
    columns = wide_transpose(local)
    for leaf in range(slots):
        far = jnp.sum(basis[leaf] * columns[0:rank, leaf : leaf + 1], axis=0, keepdims=True)
        near[leaf : leaf + 1, :] = jnp.where(
            leaf < counts[0], near[leaf : leaf + 1, :] + far, 0.0
        )


def first_near_kernel(subs, box, counts, *refs):
    geometry, (moments, coupling, box_coupling, basis) = refs[:subs], refs[subs : subs + 4]
    near_source, far_source, near, initial, values, picks = refs[subs + 4 : subs + 10]
    weights, box_weights = refs[subs + 10 : subs + 12]
    features, squares, fields, inner, near_list, far_list, arrived = refs[subs + 12 :]
    copies = copy_all([(near_source, near_list), (far_source, far_list)], arrived)
    slots, height, width = geometry[0].shape
    neighbours = near_list.shape[0]
    rank = coupling.shape[1]
    row = iota((height, width), 0)
    scale_square = jnp.where(row < 3, -2.0, 0.0)
    ones = jnp.where(row == 7, 1.0, 0.0)
    scale_normal = jnp.where((row >= 3) & (row < 6), -KERNEL_SCALE, 0.0)

    for sub in range(subs):
        rows = geometry[sub]
        at = [rows[:, component, :] for component in range(7)]
        squares[sub * slots : (sub + 1) * slots, :] = at[0] * at[0] + at[1] * at[1] + at[2] * at[2]
        fields[sub * slots : (sub + 1) * slots, :] = at[6]
        inner[...] = (at[0] * at[3] + at[1] * at[4] + at[2] * at[5]) * KERNEL_SCALE

        def source(leaf, carry, rows=rows, sub=sub):
            place = sub * slots + leaf
            plain = rows[leaf]
            square = squares[pl.ds(place, 1), :] + SOFTEN
            distance = jnp.where(row == 6, square, plain * scale_square + ones)
            numerator = jnp.where(row == 6, inner[pl.ds(leaf, 1), :], plain * scale_normal)
            for part, value in enumerate((distance, numerator)):
                one, two, three = split_three(value)
                lanes = slice(part * width, (part + 1) * width)
                features[place, 0:16, lanes] = jnp.concatenate([one, two]).astype(jnp.bfloat16)
                features[place, 16:32, lanes] = jnp.concatenate([one, three]).astype(jnp.bfloat16)
            return carry

        lax.fori_loop(0, slots, source, 0, unroll=4)

    own = geometry[0]

    def target(leaf, carry):
        plain = own[leaf]
        shifted = pltpu.roll(plain, 3, 0)
        square = squares[pl.ds(leaf, 1), :]
        value = jnp.where(row < 3, plain, jnp.where(row < 6, shifted, jnp.where(row == 6, 1.0, square)))
        one, two, three = split_three(value)
        left = jnp.concatenate([one, one, two, two, three, one]).T.astype(jnp.bfloat16)
        total = jnp.zeros((width, width), jnp.float32)
        for column in range(neighbours):
            place = near_list[column, leaf] ^ (box[0] * slots)
            upper, lower = features[place, 0:16, :], features[place, 16:32, :]
            right = jnp.concatenate([upper, upper, lower], axis=0)
            both = jnp.dot(left, right, preferred_element_type=jnp.float32)
            inverse = lax.rsqrt(both[:, 0:width])
            tile = both[:, width : 2 * width] * (inverse * inverse * inverse)
            values[leaf * neighbours + column] = tile
            total = total + tile * fields[pl.ds(place, 1), :]
        near[pl.ds(leaf, 1), :] = jnp.sum(total.T, axis=0, keepdims=True)
        return carry

    for copy in copies:
        copy.wait()
    far_count, sources = far_list.shape[0], subs * slots
    far_rows = wide_transpose(far_list[...].astype(jnp.float32))
    leaves = (iota((slots, sources), 1) ^ (box[0] * slots)).astype(jnp.float32)
    for place in range(far_count):
        chosen = jnp.where(far_rows[0:slots, place : place + 1] == leaves, 1.0, 0.0)
        picks[place * slots : (place + 1) * slots, :] = chosen.astype(jnp.bfloat16)
    write_weights(coupling, weights)
    write_weights(box_coupling, box_weights)
    local = leaf_part(moments[:, 0:rank], picks, weights)
    initial[...] = fields[0:slots, :]
    lax.fori_loop(0, slots, target, 0, unroll=True)
    add_leaf_far(counts, local, basis, near)


def box_images(box_basis, coefficients, image):
    slots, rank, width = box_basis.shape
    spread = jnp.broadcast_to(coefficients, (rank, width))
    for leaf in range(slots):
        image[leaf : leaf + 1, :] += jnp.sum(box_basis[leaf] * spread, axis=0, keepdims=True)


def first_image_kernel(patches, span, box, *refs):
    boxes = refs[:patches]
    part, initial, basis, box_basis, box_coupling = refs[patches : patches + 5]
    message, basis_one, numbers, starts, image = refs[patches + 5 :]
    slots, rank, width = basis.shape
    height = boxes[0].shape[0]
    row_starts = [(ref, at) for ref in boxes for at in range(0, height, span)]
    count = len(row_starts)
    for place, (ref, at) in enumerate(row_starts):
        starts[place : place + 1, :] = ref[at : at + 1, :]
    number = (iota((count, LANES), 0) ^ box[0]).astype(jnp.float32)
    coupled = jnp.zeros((rank, rank), jnp.float32)
    for place in range(box_coupling.shape[0]):
        wanted = boxes[0][1:2, 2 + place : 3 + place]
        row = jnp.sum(jnp.where(number == wanted, starts[...], 0.0), axis=0, keepdims=True)
        coupled = coupled + box_coupling[place] * row[:, 0:rank]
    image[...] = part[...]
    box_images(box_basis, jnp.sum(coupled, axis=1, keepdims=True), image)
    sums = tree_sum(
        [
            tree_sum([ref[at + 1 : at + 2, :] for at in range(0, height, span)])
            for ref in boxes
        ]
    )
    square_sum, unknowns = sums[:, 0:1], width * sums[:, 1:2]
    start_scale = jnp.sqrt(square_sum / unknowns + EPSILON)
    one_one = square_sum / (start_scale * start_scale)
    basis_one[...] = initial[...] / start_scale
    message[0:slots, :] = image[...] / start_scale
    numbers[...] = jnp.broadcast_to(lane_row([one_one, unknowns, start_scale]), numbers.shape)
    write_moments(message, basis, message, slots)


def share_kernel(message, basis_one, box_basis, share):
    slots = basis_one.shape[0]
    first, one = message[0:slots, :], basis_one[...]
    products = [one * first, first * first]
    share[...] = jnp.zeros_like(share)
    share[0:1, :] = box_moments(message, box_basis)
    share[1:2, :] = lane_row([jnp.sum(product, keepdims=True) for product in products])


def second_near_kernel(subs, box, counts, *refs):
    messages = refs[:subs]
    picks, weights, basis, box_basis, basis_one, share, values = refs[subs : subs + 7]
    near_source, part, shares, fields, near_list, arrived = refs[subs + 7 :]
    copy = pltpu.make_async_copy(near_source, near_list, arrived)
    copy.start()
    slots, width = part.shape
    neighbours = near_list.shape[0]
    rank = basis.shape[1]
    for sub in range(subs):
        fields[sub * slots : (sub + 1) * slots, :] = messages[sub][0:slots, :]

    def target(leaf, carry):
        total = jnp.zeros((width, width), jnp.float32)
        for column in range(neighbours):
            place = near_list[column, leaf] ^ (box[0] * slots)
            total = total + values[leaf * neighbours + column] * fields[pl.ds(place, 1), :]
        part[pl.ds(leaf, 1), :] = jnp.sum(total.T, axis=0, keepdims=True)
        return carry

    moments = jnp.concatenate([ref[slots : 2 * slots, 0:rank] for ref in messages], axis=0)
    local = leaf_part(moments, picks, weights)
    copy.wait()
    lax.fori_loop(0, slots, target, 0, unroll=True)
    add_leaf_far(counts, local, basis, part)
    first, one, second = messages[0][0:slots, :], basis_one[...], part[...]
    products = [one * second, first * second, second * second]
    sums = lane_row([jnp.sum(product, keepdims=True) for product in products])
    sums = share[1:2, :] + pltpu.roll(sums, 2, 1)
    both = share[0:1, :] + pltpu.roll(box_moments(part, box_basis), rank, 1)
    shares[...] = jnp.where(iota(shares.shape, 0) % 2 == 0, both, sums)


def last_kernel(patches, span, box, *refs):
    boxes, (shares, message, basis_one, part, numbers) = refs[:patches], refs[patches : patches + 5]
    box_basis, box_weights = refs[patches + 5 : patches + 7]
    basis_three, hessenberg, gather, starts, lists, pairs, image = refs[patches + 7 :]
    slots, rank, width = box_basis.shape
    height = boxes[0].shape[0]
    count = patches * (height // span)
    for place, ref in enumerate(boxes):
        gather[place * height : (place + 1) * height, :] = ref[...]
    for other in range(count):
        row = (box[0] ^ other) * span
        starts[other : other + 1, :] = gather[pl.ds(row, 1), :]
        lists[other : other + 1, :] = gather[pl.ds(row + 1, 1), :]
        pairs[other : other + 1, :] = shares[2 * other : 2 * other + 1, :]
        pairs[count + other : count + other + 1, :] = shares[2 * other + 1 : 2 * other + 2, :]
    first_box, second_box = pairs[0:count, 0:rank], pairs[0:count, rank : 2 * rank]
    column = iota((count, 3 * count), 1)
    rows = []
    for place in range(box_weights.shape[0]):
        wanted = lists[:, 2 + place : 3 + place]
        for split in range(3):
            number = (column - split * count).astype(jnp.float32)
            rows.append(jnp.where(wanted == number, 1.0, 0.0))
    chosen_rows = jnp.dot(
        jnp.concatenate(rows).astype(jnp.bfloat16),
        split_rows(first_box),
        preferred_element_type=jnp.float32,
    ).astype(jnp.bfloat16)

    def chosen(place):
        return chosen_rows[place * 3 * count : (place + 1) * 3 * count]

    box_local = coupled_rows(chosen, box_weights)
    twice = jnp.concatenate([box_local, box_local], axis=1)
    columns = twice.T
    half = rank // 2
    low = iota((half, 2 * rank), 1) < rank
    quadratic = jnp.zeros((half, 2 * rank), jnp.float32)
    for other in range(count):
        row = (box[0] ^ other) * span + TILE_ROWS
        column = jnp.where(
            low, columns[0:half, other : other + 1], columns[half:rank, other : other + 1]
        )
        quadratic = quadratic + gather[pl.ds(row, half), :] * twice[other : other + 1, :] * column
    one_one, unknowns, start_scale = [numbers[0:1, place : place + 1] for place in range(3)]
    sums = jnp.sum(pairs[count : 2 * count, :], axis=0, keepdims=True)
    along, image_sq, one_part, first_part, part_sq = [
        sums[:, place : place + 1] for place in range(5)
    ]
    one_second = (
        one_part + jnp.sum(starts[:, 0:rank] * box_local, keepdims=True) / start_scale
    )
    first_second = first_part + jnp.sum(first_box * box_local, keepdims=True)
    second_sq = (
        part_sq
        + 2.0 * jnp.sum(second_box * box_local, keepdims=True)
        + jnp.sum(quadratic, keepdims=True)
    )
    upper_first = (0.5 * one_one + along) / unknowns
    shift = upper_first - 0.5
    residual_sq = image_sq - 2.0 * shift * along + shift * shift * one_one
    lower_first = jnp.sqrt(residual_sq / unknowns + EPSILON)
    one_two = (along - shift * one_one) / lower_first
    two_two = residual_sq / (lower_first * lower_first)
    k_one = (one_second - shift * along) / lower_first
    k_two = (
        (first_second - shift * image_sq) - shift * (one_second - shift * along)
    ) / (lower_first * lower_first)
    k_sq = (second_sq - 2.0 * shift * first_second + shift * shift * image_sq) / (
        lower_first * lower_first
    )
    upper_second = (0.5 * one_two + k_one) / unknowns
    middle_second = (0.5 * two_two + k_two - upper_second * one_two) / unknowns
    turn = middle_second - 0.5
    final_sq = (
        k_sq
        - 2.0 * upper_second * k_one
        - 2.0 * turn * k_two
        + upper_second * upper_second * one_one
        + 2.0 * upper_second * turn * one_two
        + turn * turn * two_two
    )
    lower_second = jnp.sqrt(final_sq / unknowns + EPSILON)
    image[...] = part[...]
    own = jnp.where(iota((rank, count), 1) == box[0], columns[0:rank], 0.0)
    box_images(box_basis, jnp.sum(own, axis=1, keepdims=True), image)
    one, first = basis_one[...], message[0:slots, :]
    two = (first - shift * one) / lower_first
    mapped = (image[...] - shift * first) / lower_first
    basis_three[...] = (mapped - upper_second * one - turn * two) / lower_second
    column, row = iota(hessenberg.shape, 0), iota(hessenberg.shape, 1)
    matrix = jnp.where(column == 0, upper_first, upper_second)
    matrix = jnp.where(row == 1, jnp.where(column == 0, lower_first, middle_second), matrix)
    hessenberg[...] = jnp.where(row == 2, jnp.where(column == 0, 0.0, lower_second), matrix)


def shards(
    points,
    normals,
    density,
    counts,
    near_list,
    leaf_far,
    leaf_basis,
    leaf_to_box_transfer,
    leaf_coupling,
    box_far,
    box_coupling,
):
    slots, _, width = points.shape
    neighbours = near_list.shape[1]
    far_count = leaf_far.shape[1]
    subs, patches = lax.axis_size("sub"), lax.axis_size("patch")
    sources = subs * slots
    rows = kept(slots, width)
    this_box = lax.axis_index("patch") * subs + lax.axis_index("sub")
    box = this_box.astype(jnp.int32).reshape(1)
    far_list = leaf_far.T
    rank = leaf_basis.shape[1]
    span = TILE_ROWS + rank // 2
    near_list = near_list.T
    list_scratch = [pltpu.SMEM(near_list.shape, jnp.int32), pltpu.SemaphoreType.DMA]
    block = pltpu.VMEM((sources, width), jnp.float32)

    matrices = [leaf_basis, leaf_coupling, box_coupling]
    geometry, message, box_basis, *matrices = device_call(
        start_kernel,
        [
            kept(slots, 8, width),
            kept(slots + span, LANES),
            kept(*leaf_basis.shape),
            *[kept(*matrix.shape) for matrix in matrices],
        ],
        [counts],
        [],
        [
            pltpu.VMEM((7, slots, width), jnp.float32),
            pltpu.VMEM((slots, width), jnp.float32),
            pltpu.SMEM(box_far.shape, jnp.int32),
            pltpu.VMEM(leaf_to_box_transfer.shape, jnp.float32),
            pltpu.VMEM((3 * rank, slots * width), jnp.bfloat16),
            pltpu.SemaphoreType.DMA((6 + 2 * CHUNKS,)),
        ],
        [
            points.transpose(1, 0, 2),
            normals.transpose(1, 0, 2),
            density,
            box_far,
            leaf_to_box_transfer,
            *matrices,
        ],
    )
    leaf_basis, leaf_coupling, box_coupling = matrices
    messages = from_peers(message, "sub")
    geometry = from_peers(geometry, "sub")
    moments, blocks = device_call(
        functools.partial(join_kernel, subs),
        [kept(sources, LANES), kept(subs * span, LANES)],
        [],
        messages,
        cost=FIRST,
    )
    boxes = from_peers(blocks, "patch")
    gather = pltpu.VMEM((patches * subs * span, LANES), jnp.float32)
    part, initial, values, picks, weights, box_weights = device_call(
        functools.partial(first_near_kernel, subs),
        [
            rows,
            rows,
            kept(slots * neighbours, width, width),
            kept(far_count * slots, sources, dtype=jnp.bfloat16),
            kept(far_count, rank, 3 * rank, dtype=jnp.bfloat16),
            kept(box_coupling.shape[0], rank, 3 * rank, dtype=jnp.bfloat16),
        ],
        [box, counts],
        [*geometry, moments, leaf_coupling, box_coupling, leaf_basis],
        [
            pltpu.VMEM((sources, 32, 2 * width), jnp.bfloat16),
            block,
            block,
            pltpu.VMEM((slots, width), jnp.float32),
            pltpu.SMEM(near_list.shape, jnp.int32),
            pltpu.VMEM(far_list.shape, jnp.int32),
            pltpu.SemaphoreType.DMA((2,)),
        ],
        [near_list, far_list],
    )
    message, basis_one, numbers = device_call(
        functools.partial(first_image_kernel, patches, span),
        [kept(2 * slots, LANES), rows, kept(TILE_ROWS, LANES)],
        [box],
        [*boxes, part, initial, leaf_basis, box_basis, box_coupling],
        [
            pltpu.VMEM((patches * subs, LANES), jnp.float32),
            pltpu.VMEM((slots, width), jnp.float32),
        ],
    )
    messages = from_peers(message, "sub")
    (share,) = device_call(
        share_kernel, [kept(TILE_ROWS, LANES)], [], [message, basis_one, box_basis]
    )
    part, shares = device_call(
        functools.partial(second_near_kernel, subs),
        [rows, kept(2 * patches * subs, LANES)],
        [box, counts],
        [*messages, picks, weights, leaf_basis, box_basis, basis_one, share, values],
        [block, *list_scratch],
        [near_list],
    )
    shares = lax.all_to_all(shares, ("patch", "sub"), 0, 0, tiled=True)
    basis_three, hessenberg = device_call(
        functools.partial(last_kernel, patches, span),
        [f32(slots, width), f32(2, 3)],
        [box],
        [*boxes, shares, message, basis_one, part, numbers, box_basis, box_weights],
        [
            gather,
            pltpu.VMEM((patches * subs, LANES), jnp.float32),
            pltpu.VMEM((patches * subs, LANES), jnp.float32),
            pltpu.VMEM((2 * patches * subs, LANES), jnp.float32),
            pltpu.VMEM((slots, width), jnp.float32),
        ],
    )
    return basis_three, hessenberg.T


def solution(mesh):
    spread = ("groups", "patch", "sub")
    in_specs = (
        P(spread, None, None),
        P(spread, None, None),
        P(spread, None),
        P(spread),
        P(spread, None),
        P(spread, None),
        P(spread, None, None),
        P(spread, None, None),
        P(),
        P(spread, None),
        P(),
    )
    out_specs = (P(spread, None), P("groups", None))
    return jax.shard_map(shards, mesh=mesh, in_specs=in_specs, out_specs=out_specs, check_vma=False)
```

```python
import functools
import math

import jax
import jax.numpy as jnp
from jax import lax
from jax.experimental import pallas as pl
from jax.experimental.pallas import tpu as pltpu
from jax.sharding import PartitionSpec as P

SOFTEN = 0.05
EPSILON = 1e-06
KERNEL_SCALE = 0.25 / math.pi
HIGH_PRECISION = lax.Precision.HIGHEST
LANES = 128
TILE_ROWS = 8
VMEM_LIMIT = 16 << 20
CHUNKS = 4
FIRST = pl.CostEstimate(flops=10**11, bytes_accessed=10**10, transcendentals=0)


def from_peers(value, axis):
    size = lax.axis_size(axis)
    arrived = [
        lax.ppermute(value, axis, [(i, i ^ turn) for i in range(size)]) for turn in range(1, size)
    ]
    return [value] + arrived


def tree_sum(parts):
    while len(parts) > 1:
        parts = [parts[i] + parts[i + 1] for i in range(0, len(parts), 2)]
    return parts[0]


def device_call(kernel, outputs, scalars, arrays, scratch=(), remote=(), cost=None):
    smem = pl.BlockSpec(memory_space=pltpu.SMEM)
    vmem = pl.BlockSpec(memory_space=pltpu.VMEM)
    hbm = pl.BlockSpec(memory_space=pltpu.HBM)
    return pl.pallas_call(
        kernel,
        out_shape=tuple(outputs),
        in_specs=[smem] * len(scalars) + [vmem] * len(arrays) + [hbm] * len(remote),
        out_specs=tuple([vmem] * len(outputs)),
        scratch_shapes=tuple(scratch),
        compiler_params=pltpu.CompilerParams(vmem_limit_bytes=VMEM_LIMIT),
        cost_estimate=cost,
    )(
        *scalars,
        *[pltpu.with_memory_space_constraint(array, pltpu.VMEM) for array in arrays],
        *[pltpu.with_memory_space_constraint(array, pltpu.HBM) for array in remote],
    )


def kept(*shape, dtype=jnp.float32):
    return pltpu.VMEM(shape, dtype)


def f32(*shape):
    return jax.ShapeDtypeStruct(shape, jnp.float32)


def iota(shape, dimension):
    return lax.broadcasted_iota(jnp.int32, shape, dimension)


def split_three(value):
    first = value.astype(jnp.bfloat16).astype(jnp.float32)
    rest = value - first
    second = rest.astype(jnp.bfloat16).astype(jnp.float32)
    third = (rest - second).astype(jnp.bfloat16).astype(jnp.float32)
    return first, second, third


def lane_row(entries):
    lane = iota((1, LANES), 1)
    row = jnp.zeros((1, LANES), jnp.float32)
    for place, entry in enumerate(entries):
        row = jnp.where(lane == place, entry, row)
    return row


def copy_all(pairs, arrived):
    copies = [
        pltpu.make_async_copy(source, target, arrived.at[place])
        for place, (source, target) in enumerate(pairs)
    ]
    for copy in copies:
        copy.start()
    return copies


def write_moments(vector, basis, message, start):
    slots, rank, _ = basis.shape
    lane = iota((rank, LANES), 1)
    columns = jnp.zeros((rank, LANES), jnp.float32)
    for leaf in range(slots):
        column = jnp.sum(basis[leaf] * vector[leaf : leaf + 1, :], axis=1, keepdims=True)
        columns = jnp.where(lane == leaf, column, columns)
    message[start : start + slots, :] = jnp.zeros((slots, LANES), jnp.float32)
    message[start : start + slots, 0:rank] = columns.T[0:slots]


def box_moments(vector, box_basis):
    slots, rank, width = box_basis.shape
    total = jnp.zeros((rank, width), jnp.float32)
    for leaf in range(slots):
        total = total + box_basis[leaf] * vector[leaf : leaf + 1, :]
    column = jnp.sum(total, axis=1, keepdims=True)
    diagonal = iota((rank, LANES), 0) == iota((rank, LANES), 1)
    return jnp.sum(jnp.where(diagonal, column, 0.0), axis=0, keepdims=True)


def start_kernel(counts, *refs):
    sources, (geometry, message, box_basis) = refs[:10], refs[10:13]
    basis, leaf_coupling, box_coupling, near_list, far_list = refs[13:18]
    at, initial, box_far, transfer, parts, arrived = refs[18:]
    dims, slots, width = sources[0].shape
    rank = basis.shape[1]
    targets = [at.at[0:dims], at.at[dims : 2 * dims], at.at[2 * dims], box_far]
    pairs = list(zip(sources[:4], targets))
    step = slots // CHUNKS
    for first in range(0, slots, step):
        for source, target in zip(sources[4:6], (transfer, basis)):
            pairs.append((source.at[first : first + step], target.at[first : first + step]))
    pairs += zip(sources[6:], (leaf_coupling, box_coupling, near_list, far_list))
    copies = copy_all(pairs, arrived)
    for copy in copies[:4]:
        copy.wait()
    for row in range(2 * dims):
        geometry[:, row, :] = at[row]
    vector = jnp.where(iota((slots, width), 0) < counts[0], at[2 * dims], 0.0)
    initial[...] = vector
    geometry[:, 2 * dims, :] = vector
    geometry[:, 2 * dims + 1, :] = jnp.zeros_like(vector)
    entries = [jnp.sum(vector * vector, keepdims=True)] + [
        jnp.full((1, 1), value, jnp.int32).astype(jnp.float32)
        for value in [counts[0]] + [box_far[0, place] for place in range(box_far.shape[1])]
    ]
    message[slots : slots + TILE_ROWS, :] = jnp.zeros((TILE_ROWS, LANES), jnp.float32)
    message[slots + 1 : slots + 2, :] = lane_row(entries)
    for leaf in range(slots):
        if leaf % step == 0:
            for copy in copies[4 + 2 * (leaf // step) : 6 + 2 * (leaf // step)]:
                copy.wait()
        product = jnp.dot(
            transfer[leaf],
            basis[leaf],
            precision=HIGH_PRECISION,
            preferred_element_type=jnp.float32,
        )
        product = jnp.where(leaf < counts[0], product, 0.0)
        box_basis[leaf] = product
        parts[:, leaf * width : (leaf + 1) * width] = split_rows(product)
    write_moments(initial, basis, message, 0)
    message[slots : slots + 1, :] = box_moments(initial, box_basis)
    products = lax.dot_general(
        parts[...], parts[...], (((1,), (1,)), ((), ())), preferred_element_type=jnp.float32
    )
    mixed = products[rank : 2 * rank, 0:rank] + products[2 * rank : 3 * rank, 0:rank]
    gram = products[0:rank, 0:rank] + (
        mixed + mixed.T + products[rank : 2 * rank, rank : 2 * rank]
    )
    start, half = slots + TILE_ROWS, rank // 2
    message[start : start + half, 0:rank] = gram[0:half]
    message[start : start + half, rank : 2 * rank] = gram[half:rank]
    for copy in copies[4 + 2 * CHUNKS :]:
        copy.wait()


def join_kernel(subs, *refs):
    messages, (moments, blocks) = refs[:subs], refs[subs:]
    slots, span = moments.shape[0] // subs, blocks.shape[0] // subs
    for sub, message in enumerate(messages):
        moments[sub * slots : (sub + 1) * slots, :] = message[0:slots, :]
        blocks[sub * span : (sub + 1) * span, :] = message[slots : slots + span, :]


def split_rows(rows):
    return jnp.concatenate(split_three(rows)).astype(jnp.bfloat16)


def write_weights(coupling, weights):
    for place in range(coupling.shape[0]):
        parts = jnp.concatenate(split_three(coupling[place].T), axis=1)
        weights[place] = parts.astype(jnp.bfloat16)


def coupled_rows(chosen, weights):
    total = None
    for place in range(weights.shape[0]):
        product = jnp.dot(chosen(place), weights[place], preferred_element_type=jnp.float32)
        total = product if total is None else total + product
    count, rank = total.shape[0] // 3, total.shape[1] // 3
    part = [
        [total[row * count : (row + 1) * count, at * rank : (at + 1) * rank] for at in range(3)]
        for row in range(3)
    ]
    return part[0][0] + (
        (part[0][1] + part[1][0]) + (part[0][2] + part[2][0] + part[1][1])
    )


def leaf_part(moments, picks, weights):
    slots = picks.shape[0] // weights.shape[0]
    parts = [
        jnp.dot(
            picks[...], part.astype(jnp.bfloat16), preferred_element_type=jnp.float32
        ).astype(jnp.bfloat16)
        for part in split_three(moments)
    ]

    def chosen(place):
        return jnp.concatenate([part[place * slots : (place + 1) * slots] for part in parts])

    return coupled_rows(chosen, weights)


def wide_transpose(rows):
    count, lanes = rows.shape
    return jnp.concatenate([rows, jnp.zeros((count, LANES - lanes), rows.dtype)], axis=1).T


def add_leaf_far(counts, local, basis, near):
    slots, rank, width = basis.shape
    columns = wide_transpose(local)
    for leaf in range(slots):
        far = jnp.sum(basis[leaf] * columns[0:rank, leaf : leaf + 1], axis=0, keepdims=True)
        near[leaf : leaf + 1, :] = jnp.where(
            leaf < counts[0], near[leaf : leaf + 1, :] + far, 0.0
        )


def leaf_kernel(box, counts, moments, coupling, box_coupling, basis, far_list, *refs):
    far, picks, weights, box_weights = refs
    slots, rank, width = basis.shape
    far_count, sources = far_list.shape[0], moments.shape[0]
    far_rows = wide_transpose(far_list[...].astype(jnp.float32))
    leaves = (iota((slots, sources), 1) ^ (box[0] * slots)).astype(jnp.float32)
    for place in range(far_count):
        chosen = jnp.where(far_rows[0:slots, place : place + 1] == leaves, 1.0, 0.0)
        picks[place * slots : (place + 1) * slots, :] = chosen.astype(jnp.bfloat16)
    write_weights(coupling, weights)
    write_weights(box_coupling, box_weights)
    far[...] = jnp.zeros((slots, width), jnp.float32)
    add_leaf_far(counts, leaf_part(moments[:, 0:rank], picks, weights), basis, far)


def first_near_kernel(subs, box, counts, *refs):
    geometry, (far, near_source) = refs[:subs], refs[subs : subs + 2]
    near, initial, values, features, squares, fields, inner, near_list, arrived = refs[subs + 2 :]
    copy = pltpu.make_async_copy(near_source, near_list, arrived)
    copy.start()
    slots, height, width = geometry[0].shape
    neighbours = near_list.shape[0]
    row = iota((height, width), 0)
    scale_square = jnp.where(row < 3, -2.0, 0.0)
    ones = jnp.where(row == 7, 1.0, 0.0)
    scale_normal = jnp.where((row >= 3) & (row < 6), -KERNEL_SCALE, 0.0)

    for sub in range(subs):
        rows = geometry[sub]
        at = [rows[:, component, :] for component in range(7)]
        squares[sub * slots : (sub + 1) * slots, :] = at[0] * at[0] + at[1] * at[1] + at[2] * at[2]
        fields[sub * slots : (sub + 1) * slots, :] = at[6]
        inner[...] = (at[0] * at[3] + at[1] * at[4] + at[2] * at[5]) * KERNEL_SCALE

        def source(leaf, carry, rows=rows, sub=sub):
            place = sub * slots + leaf
            plain = rows[leaf]
            square = squares[pl.ds(place, 1), :] + SOFTEN
            distance = jnp.where(row == 6, square, plain * scale_square + ones)
            numerator = jnp.where(row == 6, inner[pl.ds(leaf, 1), :], plain * scale_normal)
            for part, value in enumerate((distance, numerator)):
                one, two, three = split_three(value)
                lanes = slice(part * width, (part + 1) * width)
                features[place, 0:16, lanes] = jnp.concatenate([one, two]).astype(jnp.bfloat16)
                features[place, 16:32, lanes] = jnp.concatenate([one, three]).astype(jnp.bfloat16)
            return carry

        lax.fori_loop(0, slots, source, 0, unroll=True)

    own = geometry[0]

    def target(leaf, carry):
        plain = own[leaf]
        shifted = pltpu.roll(plain, 3, 0)
        square = squares[pl.ds(leaf, 1), :]
        value = jnp.where(row < 3, plain, jnp.where(row < 6, shifted, jnp.where(row == 6, 1.0, square)))
        one, two, three = split_three(value)
        left = jnp.concatenate([one, one, two, two, three, one]).T.astype(jnp.bfloat16)
        total = jnp.zeros((width, width), jnp.float32)
        for column in range(neighbours):
            place = near_list[column, leaf] ^ (box[0] * slots)
            upper, lower = features[place, 0:16, :], features[place, 16:32, :]
            right = jnp.concatenate([upper, upper, lower], axis=0)
            both = jnp.dot(left, right, preferred_element_type=jnp.float32)
            inverse = lax.rsqrt(both[:, 0:width])
            tile = both[:, width : 2 * width] * (inverse * inverse * inverse)
            values[leaf * neighbours + column] = tile
            total = total + tile * fields[pl.ds(place, 1), :]
        near[pl.ds(leaf, 1), :] = jnp.sum(total.T, axis=0, keepdims=True)
        return carry

    copy.wait()
    initial[...] = fields[0:slots, :]
    lax.fori_loop(0, slots, target, 0, unroll=True)
    in_use = iota((slots, width), 0) < counts[0]
    near[...] = jnp.where(in_use, near[...] + far[...], 0.0)


def box_images(box_basis, coefficients, image):
    slots, rank, width = box_basis.shape
    spread = jnp.broadcast_to(coefficients, (rank, width))
    for leaf in range(slots):
        image[leaf : leaf + 1, :] += jnp.sum(box_basis[leaf] * spread, axis=0, keepdims=True)


def first_image_kernel(patches, span, box, *refs):
    boxes = refs[:patches]
    part, initial, basis, box_basis, box_coupling = refs[patches : patches + 5]
    message, basis_one, numbers, starts, image = refs[patches + 5 :]
    slots, rank, width = basis.shape
    height = boxes[0].shape[0]
    row_starts = [(ref, at) for ref in boxes for at in range(0, height, span)]
    count = len(row_starts)
    for place, (ref, at) in enumerate(row_starts):
        starts[place : place + 1, :] = ref[at : at + 1, :]
    number = (iota((count, LANES), 0) ^ box[0]).astype(jnp.float32)
    coupled = jnp.zeros((rank, rank), jnp.float32)
    for place in range(box_coupling.shape[0]):
        wanted = boxes[0][1:2, 2 + place : 3 + place]
        row = jnp.sum(jnp.where(number == wanted, starts[...], 0.0), axis=0, keepdims=True)
        coupled = coupled + box_coupling[place] * row[:, 0:rank]
    image[...] = part[...]
    box_images(box_basis, jnp.sum(coupled, axis=1, keepdims=True), image)
    sums = tree_sum(
        [
            tree_sum([ref[at + 1 : at + 2, :] for at in range(0, height, span)])
            for ref in boxes
        ]
    )
    square_sum, unknowns = sums[:, 0:1], width * sums[:, 1:2]
    start_scale = jnp.sqrt(square_sum / unknowns + EPSILON)
    one_one = square_sum / (start_scale * start_scale)
    basis_one[...] = initial[...] / start_scale
    message[0:slots, :] = image[...] / start_scale
    numbers[...] = jnp.broadcast_to(lane_row([one_one, unknowns, start_scale]), numbers.shape)
    write_moments(message, basis, message, slots)


def share_kernel(message, basis_one, box_basis, share):
    slots = basis_one.shape[0]
    first, one = message[0:slots, :], basis_one[...]
    products = [one * first, first * first]
    share[...] = jnp.zeros_like(share)
    share[0:1, :] = box_moments(message, box_basis)
    share[1:2, :] = lane_row([jnp.sum(product, keepdims=True) for product in products])


def second_near_kernel(subs, box, counts, *refs):
    messages = refs[:subs]
    picks, weights, basis, box_basis, basis_one, share, values = refs[subs : subs + 7]
    near_source, part, shares, fields, near_list, arrived = refs[subs + 7 :]
    copy = pltpu.make_async_copy(near_source, near_list, arrived)
    copy.start()
    slots, width = part.shape
    neighbours = near_list.shape[0]
    rank = basis.shape[1]
    for sub in range(subs):
        fields[sub * slots : (sub + 1) * slots, :] = messages[sub][0:slots, :]

    def target(leaf, carry):
        total = jnp.zeros((width, width), jnp.float32)
        for column in range(neighbours):
            place = near_list[column, leaf] ^ (box[0] * slots)
            total = total + values[leaf * neighbours + column] * fields[pl.ds(place, 1), :]
        part[pl.ds(leaf, 1), :] = jnp.sum(total.T, axis=0, keepdims=True)
        return carry

    moments = jnp.concatenate([ref[slots : 2 * slots, 0:rank] for ref in messages], axis=0)
    local = leaf_part(moments, picks, weights)
    copy.wait()
    lax.fori_loop(0, slots, target, 0, unroll=True)
    add_leaf_far(counts, local, basis, part)
    first, one, second = messages[0][0:slots, :], basis_one[...], part[...]
    products = [one * second, first * second, second * second]
    sums = lane_row([jnp.sum(product, keepdims=True) for product in products])
    sums = share[1:2, :] + pltpu.roll(sums, 2, 1)
    both = share[0:1, :] + pltpu.roll(box_moments(part, box_basis), rank, 1)
    shares[...] = jnp.where(iota(shares.shape, 0) % 2 == 0, both, sums)


def last_kernel(patches, span, box, *refs):
    boxes, (shares, message, basis_one, part, numbers) = refs[:patches], refs[patches : patches + 5]
    box_basis, box_weights = refs[patches + 5 : patches + 7]
    basis_three, hessenberg, gather, starts, lists, pairs, image = refs[patches + 7 :]
    slots, rank, width = box_basis.shape
    height = boxes[0].shape[0]
    count = patches * (height // span)
    for place, ref in enumerate(boxes):
        gather[place * height : (place + 1) * height, :] = ref[...]
    for other in range(count):
        row = (box[0] ^ other) * span
        starts[other : other + 1, :] = gather[pl.ds(row, 1), :]
        lists[other : other + 1, :] = gather[pl.ds(row + 1, 1), :]
        pairs[other : other + 1, :] = shares[2 * other : 2 * other + 1, :]
        pairs[count + other : count + other + 1, :] = shares[2 * other + 1 : 2 * other + 2, :]
    first_box, second_box = pairs[0:count, 0:rank], pairs[0:count, rank : 2 * rank]
    column = iota((count, 3 * count), 1)
    rows = []
    for place in range(box_weights.shape[0]):
        wanted = lists[:, 2 + place : 3 + place]
        for split in range(3):
            number = (column - split * count).astype(jnp.float32)
            rows.append(jnp.where(wanted == number, 1.0, 0.0))
    chosen_rows = jnp.dot(
        jnp.concatenate(rows).astype(jnp.bfloat16),
        split_rows(first_box),
        preferred_element_type=jnp.float32,
    ).astype(jnp.bfloat16)

    def chosen(place):
        return chosen_rows[place * 3 * count : (place + 1) * 3 * count]

    box_local = coupled_rows(chosen, box_weights)
    twice = jnp.concatenate([box_local, box_local], axis=1)
    columns = twice.T
    half = rank // 2
    low = iota((half, 2 * rank), 1) < rank
    quadratic = jnp.zeros((half, 2 * rank), jnp.float32)
    for other in range(count):
        row = (box[0] ^ other) * span + TILE_ROWS
        column = jnp.where(
            low, columns[0:half, other : other + 1], columns[half:rank, other : other + 1]
        )
        quadratic = quadratic + gather[pl.ds(row, half), :] * twice[other : other + 1, :] * column
    one_one, unknowns, start_scale = [numbers[0:1, place : place + 1] for place in range(3)]
    sums = jnp.sum(pairs[count : 2 * count, :], axis=0, keepdims=True)
    along, image_sq, one_part, first_part, part_sq = [
        sums[:, place : place + 1] for place in range(5)
    ]
    one_second = (
        one_part + jnp.sum(starts[:, 0:rank] * box_local, keepdims=True) / start_scale
    )
    first_second = first_part + jnp.sum(first_box * box_local, keepdims=True)
    second_sq = (
        part_sq
        + 2.0 * jnp.sum(second_box * box_local, keepdims=True)
        + jnp.sum(quadratic, keepdims=True)
    )
    upper_first = (0.5 * one_one + along) / unknowns
    shift = upper_first - 0.5
    residual_sq = image_sq - 2.0 * shift * along + shift * shift * one_one
    lower_first = jnp.sqrt(residual_sq / unknowns + EPSILON)
    one_two = (along - shift * one_one) / lower_first
    two_two = residual_sq / (lower_first * lower_first)
    k_one = (one_second - shift * along) / lower_first
    k_two = (
        (first_second - shift * image_sq) - shift * (one_second - shift * along)
    ) / (lower_first * lower_first)
    k_sq = (second_sq - 2.0 * shift * first_second + shift * shift * image_sq) / (
        lower_first * lower_first
    )
    upper_second = (0.5 * one_two + k_one) / unknowns
    middle_second = (0.5 * two_two + k_two - upper_second * one_two) / unknowns
    turn = middle_second - 0.5
    final_sq = (
        k_sq
        - 2.0 * upper_second * k_one
        - 2.0 * turn * k_two
        + upper_second * upper_second * one_one
        + 2.0 * upper_second * turn * one_two
        + turn * turn * two_two
    )
    lower_second = jnp.sqrt(final_sq / unknowns + EPSILON)
    image[...] = part[...]
    own = jnp.where(iota((rank, count), 1) == box[0], columns[0:rank], 0.0)
    box_images(box_basis, jnp.sum(own, axis=1, keepdims=True), image)
    one, first = basis_one[...], message[0:slots, :]
    two = (first - shift * one) / lower_first
    mapped = (image[...] - shift * first) / lower_first
    basis_three[...] = (mapped - upper_second * one - turn * two) / lower_second
    column, row = iota(hessenberg.shape, 0), iota(hessenberg.shape, 1)
    matrix = jnp.where(column == 0, upper_first, upper_second)
    matrix = jnp.where(row == 1, jnp.where(column == 0, lower_first, middle_second), matrix)
    hessenberg[...] = jnp.where(row == 2, jnp.where(column == 0, 0.0, lower_second), matrix)


def shards(
    points,
    normals,
    density,
    counts,
    near_list,
    leaf_far,
    leaf_basis,
    leaf_to_box_transfer,
    leaf_coupling,
    box_far,
    box_coupling,
):
    slots, _, width = points.shape
    neighbours = near_list.shape[1]
    far_count = leaf_far.shape[1]
    subs, patches = lax.axis_size("sub"), lax.axis_size("patch")
    sources = subs * slots
    rows = kept(slots, width)
    this_box = lax.axis_index("patch") * subs + lax.axis_index("sub")
    box = this_box.astype(jnp.int32).reshape(1)
    far_list = leaf_far.T
    rank = leaf_basis.shape[1]
    span = TILE_ROWS + rank // 2
    near_list = near_list.T
    list_scratch = [pltpu.SMEM(near_list.shape, jnp.int32), pltpu.SemaphoreType.DMA]
    block = pltpu.VMEM((sources, width), jnp.float32)

    matrices, lists = [leaf_basis, leaf_coupling, box_coupling], [near_list, far_list]
    geometry, message, box_basis, *held = device_call(
        start_kernel,
        [
            kept(slots, 8, width),
            kept(slots + span, LANES),
            kept(*leaf_basis.shape),
            *[kept(*matrix.shape) for matrix in matrices],
            *[kept(*entries.shape, dtype=jnp.int32) for entries in lists],
        ],
        [counts],
        [],
        [
            pltpu.VMEM((7, slots, width), jnp.float32),
            pltpu.VMEM((slots, width), jnp.float32),
            pltpu.SMEM(box_far.shape, jnp.int32),
            pltpu.VMEM(leaf_to_box_transfer.shape, jnp.float32),
            pltpu.VMEM((3 * rank, slots * width), jnp.bfloat16),
            pltpu.SemaphoreType.DMA((8 + 2 * CHUNKS,)),
        ],
        [
            points.transpose(1, 0, 2),
            normals.transpose(1, 0, 2),
            density,
            box_far,
            leaf_to_box_transfer,
            *matrices,
            *lists,
        ],
    )
    leaf_basis, leaf_coupling, box_coupling, near_list, far_list = held
    messages = from_peers(message, "sub")
    geometry = from_peers(geometry, "sub")
    moments, blocks = device_call(
        functools.partial(join_kernel, subs),
        [kept(sources, LANES), kept(subs * span, LANES)],
        [],
        messages,
        cost=FIRST,
    )
    boxes = from_peers(blocks, "patch")
    gather = pltpu.VMEM((patches * subs * span, LANES), jnp.float32)
    far, picks, weights, box_weights = device_call(
        leaf_kernel,
        [
            rows,
            kept(far_count * slots, sources, dtype=jnp.bfloat16),
            kept(far_count, rank, 3 * rank, dtype=jnp.bfloat16),
            kept(box_coupling.shape[0], rank, 3 * rank, dtype=jnp.bfloat16),
        ],
        [box, counts],
        [moments, leaf_coupling, box_coupling, leaf_basis, far_list],
    )
    part, initial, values = device_call(
        functools.partial(first_near_kernel, subs),
        [rows, rows, kept(slots * neighbours, width, width)],
        [box, counts],
        [*geometry, far, near_list],
        [
            pltpu.VMEM((sources, 32, 2 * width), jnp.bfloat16),
            block,
            block,
            pltpu.VMEM((slots, width), jnp.float32),
            *list_scratch,
        ],
    )
    message, basis_one, numbers = device_call(
        functools.partial(first_image_kernel, patches, span),
        [kept(2 * slots, LANES), rows, kept(TILE_ROWS, LANES)],
        [box],
        [*boxes, part, initial, leaf_basis, box_basis, box_coupling],
        [
            pltpu.VMEM((patches * subs, LANES), jnp.float32),
            pltpu.VMEM((slots, width), jnp.float32),
        ],
    )
    messages = from_peers(message, "sub")
    (share,) = device_call(
        share_kernel, [kept(TILE_ROWS, LANES)], [], [message, basis_one, box_basis]
    )
    part, shares = device_call(
        functools.partial(second_near_kernel, subs),
        [rows, kept(2 * patches * subs, LANES)],
        [box, counts],
        [*messages, picks, weights, leaf_basis, box_basis, basis_one, share, values, near_list],
        [block, *list_scratch],
    )
    shares = lax.all_to_all(shares, ("patch", "sub"), 0, 0, tiled=True)
    basis_three, hessenberg = device_call(
        functools.partial(last_kernel, patches, span),
        [f32(slots, width), f32(2, 3)],
        [box],
        [*boxes, shares, message, basis_one, part, numbers, box_basis, box_weights],
        [
            gather,
            pltpu.VMEM((patches * subs, LANES), jnp.float32),
            pltpu.VMEM((patches * subs, LANES), jnp.float32),
            pltpu.VMEM((2 * patches * subs, LANES), jnp.float32),
            pltpu.VMEM((slots, width), jnp.float32),
        ],
    )
    return basis_three, hessenberg.T


def solution(mesh):
    spread = ("groups", "patch", "sub")
    in_specs = (
        P(spread, None, None),
        P(spread, None, None),
        P(spread, None),
        P(spread),
        P(spread, None),
        P(spread, None),
        P(spread, None, None),
        P(spread, None, None),
        P(),
        P(spread, None),
        P(),
    )
    out_specs = (P(spread, None), P("groups", None))
    return jax.shard_map(shards, mesh=mesh, in_specs=in_specs, out_specs=out_specs, check_vma=False)
```

```python
import functools
import math

import jax
import jax.numpy as jnp
from jax import lax
from jax.experimental import pallas as pl
from jax.experimental.pallas import tpu as pltpu
from jax.sharding import PartitionSpec as P

SOFTEN = 0.05
EPSILON = 1e-06
KERNEL_SCALE = 0.25 / math.pi
HIGH_PRECISION = lax.Precision.HIGHEST
LANES = 128
TILE_ROWS = 8
VMEM_LIMIT = 16 << 20
CHUNKS = 4
FIRST = pl.CostEstimate(flops=10**11, bytes_accessed=10**10, transcendentals=0)


def from_peers(value, axis):
    size = lax.axis_size(axis)
    arrived = [
        lax.ppermute(value, axis, [(i, i ^ turn) for i in range(size)]) for turn in range(1, size)
    ]
    return [value] + arrived


def tree_sum(parts):
    while len(parts) > 1:
        parts = [parts[i] + parts[i + 1] for i in range(0, len(parts), 2)]
    return parts[0]


def device_call(kernel, outputs, scalars, arrays, scratch=(), remote=(), cost=None):
    smem = pl.BlockSpec(memory_space=pltpu.SMEM)
    vmem = pl.BlockSpec(memory_space=pltpu.VMEM)
    hbm = pl.BlockSpec(memory_space=pltpu.HBM)
    return pl.pallas_call(
        kernel,
        out_shape=tuple(outputs),
        in_specs=[smem] * len(scalars) + [vmem] * len(arrays) + [hbm] * len(remote),
        out_specs=tuple([vmem] * len(outputs)),
        scratch_shapes=tuple(scratch),
        compiler_params=pltpu.CompilerParams(vmem_limit_bytes=VMEM_LIMIT),
        cost_estimate=cost,
    )(
        *scalars,
        *[pltpu.with_memory_space_constraint(array, pltpu.VMEM) for array in arrays],
        *[pltpu.with_memory_space_constraint(array, pltpu.HBM) for array in remote],
    )


def kept(*shape, dtype=jnp.float32):
    return pltpu.VMEM(shape, dtype)


def f32(*shape):
    return jax.ShapeDtypeStruct(shape, jnp.float32)


def iota(shape, dimension):
    return lax.broadcasted_iota(jnp.int32, shape, dimension)


def split_three(value):
    first = value.astype(jnp.bfloat16).astype(jnp.float32)
    rest = value - first
    second = rest.astype(jnp.bfloat16).astype(jnp.float32)
    third = (rest - second).astype(jnp.bfloat16).astype(jnp.float32)
    return first, second, third


def lane_row(entries):
    lane = iota((1, LANES), 1)
    row = jnp.zeros((1, LANES), jnp.float32)
    for place, entry in enumerate(entries):
        row = jnp.where(lane == place, entry, row)
    return row


def copy_all(pairs, arrived):
    copies = [
        pltpu.make_async_copy(source, target, arrived.at[place])
        for place, (source, target) in enumerate(pairs)
    ]
    for copy in copies:
        copy.start()
    return copies


def add_moment(columns, vector, basis, leaf):
    column = jnp.sum(basis[leaf] * vector[leaf : leaf + 1, :], axis=1, keepdims=True)
    return jnp.where(iota(columns.shape, 1) == leaf, column, columns)


def write_moments(columns, message, start, slots):
    rank = columns.shape[0]
    message[start : start + slots, :] = jnp.zeros((slots, LANES), jnp.float32)
    message[start : start + slots, 0:rank] = columns.T[0:slots]


def sum_lanes(rows):
    column = jnp.sum(rows, axis=1, keepdims=True)
    diagonal = iota((rows.shape[0], LANES), 0) == iota((rows.shape[0], LANES), 1)
    return jnp.sum(jnp.where(diagonal, column, 0.0), axis=0, keepdims=True)


def box_moments(vector, box_basis):
    slots, rank, width = box_basis.shape
    total = jnp.zeros((rank, width), jnp.float32)
    for leaf in range(slots):
        total = total + box_basis[leaf] * vector[leaf : leaf + 1, :]
    return sum_lanes(total)


def start_kernel(counts, *refs):
    sources, (geometry, message, box_basis) = refs[:10], refs[10:13]
    basis, leaf_coupling, box_coupling, near_list, far_list = refs[13:18]
    at, initial, box_far, transfer, parts, arrived = refs[18:]
    dims, slots, width = sources[0].shape
    rank = basis.shape[1]
    targets = [at.at[0:dims], at.at[dims : 2 * dims], at.at[2 * dims], box_far]
    pairs = list(zip(sources[:4], targets))
    step = slots // CHUNKS
    for first in range(0, slots, step):
        for source, target in zip(sources[4:6], (transfer, basis)):
            pairs.append((source.at[first : first + step], target.at[first : first + step]))
    pairs += zip(sources[6:], (leaf_coupling, box_coupling, near_list, far_list))
    copies = copy_all(pairs, arrived)
    for copy in copies[:4]:
        copy.wait()
    for row in range(2 * dims):
        geometry[:, row, :] = at[row]
    vector = jnp.where(iota((slots, width), 0) < counts[0], at[2 * dims], 0.0)
    initial[...] = vector
    geometry[:, 2 * dims, :] = vector
    geometry[:, 2 * dims + 1, :] = jnp.zeros_like(vector)
    entries = [jnp.sum(vector * vector, keepdims=True)] + [
        jnp.full((1, 1), value, jnp.int32).astype(jnp.float32)
        for value in [counts[0]] + [box_far[0, place] for place in range(box_far.shape[1])]
    ]
    message[slots : slots + TILE_ROWS, :] = jnp.zeros((TILE_ROWS, LANES), jnp.float32)
    message[slots + 1 : slots + 2, :] = lane_row(entries)
    columns = jnp.zeros((rank, LANES), jnp.float32)
    products = jnp.zeros((3 * rank, 3 * rank), jnp.float32)
    for leaf in range(slots):
        if leaf % step == 0:
            for copy in copies[4 + 2 * (leaf // step) : 6 + 2 * (leaf // step)]:
                copy.wait()
        columns = add_moment(columns, vector, basis, leaf)
        product = jnp.dot(
            transfer[leaf],
            basis[leaf],
            precision=HIGH_PRECISION,
            preferred_element_type=jnp.float32,
        )
        product = jnp.where(leaf < counts[0], product, 0.0)
        box_basis[leaf] = product
        parts[:, leaf * width : (leaf + 1) * width] = split_rows(product)
        if leaf % step == step - 1:
            chunk = parts[:, (leaf + 1 - step) * width : (leaf + 1) * width]
            products = products + lax.dot_general(
                chunk, chunk, (((1,), (1,)), ((), ())), preferred_element_type=jnp.float32
            )
    write_moments(columns, message, 0, slots)
    message[slots : slots + 1, :] = box_moments(initial, box_basis)
    mixed = products[rank : 2 * rank, 0:rank] + products[2 * rank : 3 * rank, 0:rank]
    gram = products[0:rank, 0:rank] + (
        mixed + mixed.T + products[rank : 2 * rank, rank : 2 * rank]
    )
    start, half = slots + TILE_ROWS, rank // 2
    message[start : start + half, 0:rank] = gram[0:half]
    message[start : start + half, rank : 2 * rank] = gram[half:rank]
    for copy in copies[4 + 2 * CHUNKS :]:
        copy.wait()


def join_kernel(subs, *refs):
    messages, (moments, blocks) = refs[:subs], refs[subs + 1 :]
    slots, span = moments.shape[0] // subs, blocks.shape[0] // subs
    for sub, message in enumerate(messages):
        moments[sub * slots : (sub + 1) * slots, :] = message[0:slots, :]
        blocks[sub * span : (sub + 1) * span, :] = message[slots : slots + span, :]


def split_rows(rows):
    return jnp.concatenate(split_three(rows)).astype(jnp.bfloat16)


def write_weights(coupling, weights):
    for place in range(coupling.shape[0]):
        parts = jnp.concatenate(split_three(coupling[place].T), axis=1)
        weights[place] = parts.astype(jnp.bfloat16)


def coupled_rows(chosen, weights):
    total = None
    for place in range(weights.shape[0]):
        product = jnp.dot(chosen(place), weights[place], preferred_element_type=jnp.float32)
        total = product if total is None else total + product
    count, rank = total.shape[0] // 3, total.shape[1] // 3
    part = [
        [total[row * count : (row + 1) * count, at * rank : (at + 1) * rank] for at in range(3)]
        for row in range(3)
    ]
    return part[0][0] + (
        (part[0][1] + part[1][0]) + (part[0][2] + part[2][0] + part[1][1])
    )


def leaf_part(moments, picks, weights):
    slots = picks.shape[0] // weights.shape[0]
    parts = [
        jnp.dot(
            picks[...], part.astype(jnp.bfloat16), preferred_element_type=jnp.float32
        ).astype(jnp.bfloat16)
        for part in split_three(moments)
    ]

    def chosen(place):
        return jnp.concatenate([part[place * slots : (place + 1) * slots] for part in parts])

    return coupled_rows(chosen, weights)


def wide_transpose(rows):
    count, lanes = rows.shape
    return jnp.concatenate([rows, jnp.zeros((count, LANES - lanes), rows.dtype)], axis=1).T


def leaf_far_row(counts, columns, basis, leaf, near):
    rank = basis.shape[1]
    far = jnp.sum(basis[leaf] * columns[0:rank, leaf : leaf + 1], axis=0, keepdims=True)
    return jnp.where(leaf < counts[0], near + far, 0.0)


def weights_kernel(box, coupling, box_coupling, far_list, *refs):
    picks, weights, box_weights = refs
    far_count, slots = far_list.shape
    far_rows = wide_transpose(far_list[...].astype(jnp.float32))
    leaves = (iota((slots, picks.shape[1]), 1) ^ (box[0] * slots)).astype(jnp.float32)
    for place in range(far_count):
        chosen = jnp.where(far_rows[0:slots, place : place + 1] == leaves, 1.0, 0.0)
        picks[place * slots : (place + 1) * slots, :] = chosen.astype(jnp.bfloat16)
    write_weights(coupling, weights)
    write_weights(box_coupling, box_weights)


def leaf_kernel(counts, moments, basis, picks, weights, far):
    slots, rank, width = basis.shape
    columns = wide_transpose(leaf_part(moments[:, 0:rank], picks, weights))
    for leaf in range(slots):
        far[leaf : leaf + 1, :] = leaf_far_row(counts, columns, basis, leaf, 0.0)


def first_near_kernel(subs, box, counts, *refs):
    geometry, (far, near_source) = refs[:subs], refs[subs : subs + 2]
    near, initial, values, features, squares, fields, inner, near_list, arrived = refs[subs + 2 :]
    copy = pltpu.make_async_copy(near_source, near_list, arrived)
    copy.start()
    slots, height, width = geometry[0].shape
    neighbours = near_list.shape[0]
    row = iota((height, width), 0)
    scale_square = jnp.where(row < 3, -2.0, 0.0)
    ones = jnp.where(row == 7, 1.0, 0.0)
    scale_normal = jnp.where((row >= 3) & (row < 6), -KERNEL_SCALE, 0.0)

    for sub in range(subs):
        rows = geometry[sub]
        at = [rows[:, component, :] for component in range(7)]
        squares[sub * slots : (sub + 1) * slots, :] = at[0] * at[0] + at[1] * at[1] + at[2] * at[2]
        fields[sub * slots : (sub + 1) * slots, :] = at[6]
        inner[...] = (at[0] * at[3] + at[1] * at[4] + at[2] * at[5]) * KERNEL_SCALE

        def source(leaf, carry, rows=rows, sub=sub):
            place = sub * slots + leaf
            plain = rows[leaf]
            square = squares[pl.ds(place, 1), :] + SOFTEN
            distance = jnp.where(row == 6, square, plain * scale_square + ones)
            numerator = jnp.where(row == 6, inner[pl.ds(leaf, 1), :], plain * scale_normal)
            for part, value in enumerate((distance, numerator)):
                one, two, three = split_three(value)
                lanes = slice(part * width, (part + 1) * width)
                features[place, 0:16, lanes] = jnp.concatenate([one, two]).astype(jnp.bfloat16)
                features[place, 16:32, lanes] = jnp.concatenate([one, three]).astype(jnp.bfloat16)
            return carry

        lax.fori_loop(0, slots, source, 0, unroll=True)

    own = geometry[0]

    def target(leaf, carry):
        plain = own[leaf]
        shifted = pltpu.roll(plain, 3, 0)
        square = squares[pl.ds(leaf, 1), :]
        value = jnp.where(row < 3, plain, jnp.where(row < 6, shifted, jnp.where(row == 6, 1.0, square)))
        one, two, three = split_three(value)
        left = jnp.concatenate([one, one, two, two, three, one]).T.astype(jnp.bfloat16)
        total = jnp.zeros((width, width), jnp.float32)
        for column in range(neighbours):
            place = near_list[column, leaf] ^ (box[0] * slots)
            upper, lower = features[place, 0:16, :], features[place, 16:32, :]
            right = jnp.concatenate([upper, upper, lower], axis=0)
            both = jnp.dot(left, right, preferred_element_type=jnp.float32)
            inverse = lax.rsqrt(both[:, 0:width])
            tile = both[:, width : 2 * width] * (inverse * inverse * inverse)
            values[leaf * neighbours + column] = tile
            total = total + tile * fields[pl.ds(place, 1), :]
        near[pl.ds(leaf, 1), :] = jnp.sum(total.T, axis=0, keepdims=True)
        return carry

    copy.wait()
    initial[...] = fields[0:slots, :]
    lax.fori_loop(0, slots, target, 0, unroll=True)
    in_use = iota((slots, width), 0) < counts[0]
    near[...] = jnp.where(in_use, near[...] + far[...], 0.0)


def box_images(box_basis, coefficients, image):
    slots, rank, width = box_basis.shape
    spread = jnp.broadcast_to(coefficients, (rank, width))
    for leaf in range(slots):
        image[leaf : leaf + 1, :] += jnp.sum(box_basis[leaf] * spread, axis=0, keepdims=True)


def first_image_kernel(patches, span, box, *refs):
    boxes = refs[:patches]
    part, initial, basis, box_basis, box_coupling = refs[patches : patches + 5]
    message, basis_one, numbers, starts, image = refs[patches + 5 :]
    slots, rank, width = basis.shape
    height = boxes[0].shape[0]
    row_starts = [(ref, at) for ref in boxes for at in range(0, height, span)]
    count = len(row_starts)
    for place, (ref, at) in enumerate(row_starts):
        starts[place : place + 1, :] = ref[at : at + 1, :]
    number = (iota((count, LANES), 0) ^ box[0]).astype(jnp.float32)
    coupled = jnp.zeros((rank, rank), jnp.float32)
    for place in range(box_coupling.shape[0]):
        wanted = boxes[0][1:2, 2 + place : 3 + place]
        row = jnp.sum(jnp.where(number == wanted, starts[...], 0.0), axis=0, keepdims=True)
        coupled = coupled + box_coupling[place] * row[:, 0:rank]
    image[...] = part[...]
    box_images(box_basis, jnp.sum(coupled, axis=1, keepdims=True), image)
    sums = tree_sum(
        [
            tree_sum([ref[at + 1 : at + 2, :] for at in range(0, height, span)])
            for ref in boxes
        ]
    )
    square_sum, unknowns = sums[:, 0:1], width * sums[:, 1:2]
    start_scale = jnp.sqrt(square_sum / unknowns + EPSILON)
    one_one = square_sum / (start_scale * start_scale)
    basis_one[...] = initial[...] / start_scale
    vector = image[...] / start_scale
    message[0:slots, :] = vector
    numbers[...] = jnp.broadcast_to(lane_row([one_one, unknowns, start_scale]), numbers.shape)
    columns = jnp.zeros((rank, LANES), jnp.float32)
    for leaf in range(slots):
        columns = add_moment(columns, vector, basis, leaf)
    write_moments(columns, message, slots, slots)


def share_kernel(message, basis_one, box_basis, share):
    slots = basis_one.shape[0]
    first, one = message[0:slots, :], basis_one[...]
    products = [one * first, first * first]
    share[...] = jnp.zeros_like(share)
    share[0:1, :] = box_moments(message, box_basis)
    share[1:2, :] = lane_row([jnp.sum(product, keepdims=True) for product in products])


def second_near_kernel(subs, box, counts, *refs):
    messages = refs[:subs]
    picks, weights, basis, box_basis, basis_one, share, values = refs[subs : subs + 7]
    near_source, part, shares, fields, near_list, arrived = refs[subs + 7 :]
    copy = pltpu.make_async_copy(near_source, near_list, arrived)
    copy.start()
    slots, width = part.shape
    neighbours = near_list.shape[0]
    rank = basis.shape[1]
    for sub in range(subs):
        fields[sub * slots : (sub + 1) * slots, :] = messages[sub][0:slots, :]

    moments = jnp.concatenate([ref[slots : 2 * slots, 0:rank] for ref in messages], axis=0)
    columns = wide_transpose(leaf_part(moments, picks, weights))
    copy.wait()
    box_sum = jnp.zeros(box_basis.shape[1:], jnp.float32)
    for leaf in range(slots):
        total = jnp.zeros((width, width), jnp.float32)
        for column in range(neighbours):
            place = near_list[column, leaf] ^ (box[0] * slots)
            total = total + values[leaf * neighbours + column] * fields[pl.ds(place, 1), :]
        near = jnp.sum(total.T, axis=0, keepdims=True)
        near = leaf_far_row(counts, columns, basis, leaf, near)
        part[leaf : leaf + 1, :] = near
        box_sum = box_sum + box_basis[leaf] * near
    first, one, second = messages[0][0:slots, :], basis_one[...], part[...]
    products = [one * second, first * second, second * second]
    sums = lane_row([jnp.sum(product, keepdims=True) for product in products])
    sums = share[1:2, :] + pltpu.roll(sums, 2, 1)
    both = share[0:1, :] + pltpu.roll(sum_lanes(box_sum), rank, 1)
    shares[...] = jnp.where(iota(shares.shape, 0) % 2 == 0, both, sums)


def last_kernel(patches, span, box, *refs):
    boxes, (shares, message, basis_one, part, numbers) = refs[:patches], refs[patches : patches + 5]
    box_basis, box_weights = refs[patches + 5 : patches + 7]
    basis_three, hessenberg, gather, starts, lists, pairs, image = refs[patches + 7 :]
    slots, rank, width = box_basis.shape
    height = boxes[0].shape[0]
    count = patches * (height // span)
    for place, ref in enumerate(boxes):
        gather[place * height : (place + 1) * height, :] = ref[...]
    for other in range(count):
        row = (box[0] ^ other) * span
        starts[other : other + 1, :] = gather[pl.ds(row, 1), :]
        lists[other : other + 1, :] = gather[pl.ds(row + 1, 1), :]
        pairs[other : other + 1, :] = shares[2 * other : 2 * other + 1, :]
        pairs[count + other : count + other + 1, :] = shares[2 * other + 1 : 2 * other + 2, :]
    first_box, second_box = pairs[0:count, 0:rank], pairs[0:count, rank : 2 * rank]
    column = iota((count, 3 * count), 1)
    rows = []
    for place in range(box_weights.shape[0]):
        wanted = lists[:, 2 + place : 3 + place]
        for split in range(3):
            number = (column - split * count).astype(jnp.float32)
            rows.append(jnp.where(wanted == number, 1.0, 0.0))
    chosen_rows = jnp.dot(
        jnp.concatenate(rows).astype(jnp.bfloat16),
        split_rows(first_box),
        preferred_element_type=jnp.float32,
    ).astype(jnp.bfloat16)

    def chosen(place):
        return chosen_rows[place * 3 * count : (place + 1) * 3 * count]

    box_local = coupled_rows(chosen, box_weights)
    twice = jnp.concatenate([box_local, box_local], axis=1)
    columns = twice.T
    half = rank // 2
    low = iota((half, 2 * rank), 1) < rank
    quadratic = jnp.zeros((half, 2 * rank), jnp.float32)
    for other in range(count):
        row = (box[0] ^ other) * span + TILE_ROWS
        column = jnp.where(
            low, columns[0:half, other : other + 1], columns[half:rank, other : other + 1]
        )
        quadratic = quadratic + gather[pl.ds(row, half), :] * twice[other : other + 1, :] * column
    one_one, unknowns, start_scale = [numbers[0:1, place : place + 1] for place in range(3)]
    sums = jnp.sum(pairs[count : 2 * count, :], axis=0, keepdims=True)
    along, image_sq, one_part, first_part, part_sq = [
        sums[:, place : place + 1] for place in range(5)
    ]
    one_second = (
        one_part + jnp.sum(starts[:, 0:rank] * box_local, keepdims=True) / start_scale
    )
    first_second = first_part + jnp.sum(first_box * box_local, keepdims=True)
    second_sq = (
        part_sq
        + 2.0 * jnp.sum(second_box * box_local, keepdims=True)
        + jnp.sum(quadratic, keepdims=True)
    )
    upper_first = (0.5 * one_one + along) / unknowns
    shift = upper_first - 0.5
    residual_sq = image_sq - 2.0 * shift * along + shift * shift * one_one
    lower_first = jnp.sqrt(residual_sq / unknowns + EPSILON)
    one_two = (along - shift * one_one) / lower_first
    two_two = residual_sq / (lower_first * lower_first)
    k_one = (one_second - shift * along) / lower_first
    k_two = (
        (first_second - shift * image_sq) - shift * (one_second - shift * along)
    ) / (lower_first * lower_first)
    k_sq = (second_sq - 2.0 * shift * first_second + shift * shift * image_sq) / (
        lower_first * lower_first
    )
    upper_second = (0.5 * one_two + k_one) / unknowns
    middle_second = (0.5 * two_two + k_two - upper_second * one_two) / unknowns
    turn = middle_second - 0.5
    final_sq = (
        k_sq
        - 2.0 * upper_second * k_one
        - 2.0 * turn * k_two
        + upper_second * upper_second * one_one
        + 2.0 * upper_second * turn * one_two
        + turn * turn * two_two
    )
    lower_second = jnp.sqrt(final_sq / unknowns + EPSILON)
    image[...] = part[...]
    own = jnp.where(iota((rank, count), 1) == box[0], columns[0:rank], 0.0)
    box_images(box_basis, jnp.sum(own, axis=1, keepdims=True), image)
    one, first = basis_one[...], message[0:slots, :]
    two = (first - shift * one) / lower_first
    mapped = (image[...] - shift * first) / lower_first
    basis_three[...] = (mapped - upper_second * one - turn * two) / lower_second
    column, row = iota(hessenberg.shape, 0), iota(hessenberg.shape, 1)
    matrix = jnp.where(column == 0, upper_first, upper_second)
    matrix = jnp.where(row == 1, jnp.where(column == 0, lower_first, middle_second), matrix)
    hessenberg[...] = jnp.where(row == 2, jnp.where(column == 0, 0.0, lower_second), matrix)


def shards(
    points,
    normals,
    density,
    counts,
    near_list,
    leaf_far,
    leaf_basis,
    leaf_to_box_transfer,
    leaf_coupling,
    box_far,
    box_coupling,
):
    slots, _, width = points.shape
    neighbours = near_list.shape[1]
    far_count = leaf_far.shape[1]
    subs, patches = lax.axis_size("sub"), lax.axis_size("patch")
    sources = subs * slots
    rows = kept(slots, width)
    this_box = lax.axis_index("patch") * subs + lax.axis_index("sub")
    box = this_box.astype(jnp.int32).reshape(1)
    far_list = leaf_far.T
    rank = leaf_basis.shape[1]
    span = TILE_ROWS + rank // 2
    near_list = near_list.T
    list_scratch = [pltpu.SMEM(near_list.shape, jnp.int32), pltpu.SemaphoreType.DMA]
    block = pltpu.VMEM((sources, width), jnp.float32)

    matrices, lists = [leaf_basis, leaf_coupling, box_coupling], [near_list, far_list]
    geometry, message, box_basis, *held = device_call(
        start_kernel,
        [
            kept(slots, 8, width),
            kept(slots + span, LANES),
            kept(*leaf_basis.shape),
            *[kept(*matrix.shape) for matrix in matrices],
            *[kept(*entries.shape, dtype=jnp.int32) for entries in lists],
        ],
        [counts],
        [],
        [
            pltpu.VMEM((7, slots, width), jnp.float32),
            pltpu.VMEM((slots, width), jnp.float32),
            pltpu.SMEM(box_far.shape, jnp.int32),
            pltpu.VMEM(leaf_to_box_transfer.shape, jnp.float32),
            pltpu.VMEM((3 * rank, slots * width), jnp.bfloat16),
            pltpu.SemaphoreType.DMA((8 + 2 * CHUNKS,)),
        ],
        [
            points.transpose(1, 0, 2),
            normals.transpose(1, 0, 2),
            density,
            box_far,
            leaf_to_box_transfer,
            *matrices,
            *lists,
        ],
    )
    leaf_basis, leaf_coupling, box_coupling, near_list, far_list = held
    messages = from_peers(message, "sub")
    geometry = from_peers(geometry, "sub")
    picks, weights, box_weights = device_call(
        weights_kernel,
        [
            kept(far_count * slots, sources, dtype=jnp.bfloat16),
            kept(far_count, rank, 3 * rank, dtype=jnp.bfloat16),
            kept(box_coupling.shape[0], rank, 3 * rank, dtype=jnp.bfloat16),
        ],
        [box],
        [leaf_coupling, box_coupling, far_list],
    )
    moments, blocks = device_call(
        functools.partial(join_kernel, subs),
        [kept(sources, LANES), kept(subs * span, LANES)],
        [],
        [*messages, box_weights],
        cost=FIRST,
    )
    boxes = from_peers(blocks, "patch")
    gather = pltpu.VMEM((patches * subs * span, LANES), jnp.float32)
    (far,) = device_call(leaf_kernel, [rows], [counts], [moments, leaf_basis, picks, weights])
    part, initial, values = device_call(
        functools.partial(first_near_kernel, subs),
        [rows, rows, kept(slots * neighbours, width, width)],
        [box, counts],
        [*geometry, far, near_list],
        [
            pltpu.VMEM((sources, 32, 2 * width), jnp.bfloat16),
            block,
            block,
            pltpu.VMEM((slots, width), jnp.float32),
            *list_scratch,
        ],
    )
    message, basis_one, numbers = device_call(
        functools.partial(first_image_kernel, patches, span),
        [kept(2 * slots, LANES), rows, kept(TILE_ROWS, LANES)],
        [box],
        [*boxes, part, initial, leaf_basis, box_basis, box_coupling],
        [
            pltpu.VMEM((patches * subs, LANES), jnp.float32),
            pltpu.VMEM((slots, width), jnp.float32),
        ],
    )
    messages = from_peers(message, "sub")
    (share,) = device_call(
        share_kernel, [kept(TILE_ROWS, LANES)], [], [message, basis_one, box_basis]
    )
    part, shares = device_call(
        functools.partial(second_near_kernel, subs),
        [rows, kept(2 * patches * subs, LANES)],
        [box, counts],
        [*messages, picks, weights, leaf_basis, box_basis, basis_one, share, values, near_list],
        [block, *list_scratch],
    )
    shares = lax.all_to_all(shares, ("patch", "sub"), 0, 0, tiled=True)
    basis_three, hessenberg = device_call(
        functools.partial(last_kernel, patches, span),
        [f32(slots, width), f32(2, 3)],
        [box],
        [*boxes, shares, message, basis_one, part, numbers, box_basis, box_weights],
        [
            gather,
            pltpu.VMEM((patches * subs, LANES), jnp.float32),
            pltpu.VMEM((patches * subs, LANES), jnp.float32),
            pltpu.VMEM((2 * patches * subs, LANES), jnp.float32),
            pltpu.VMEM((slots, width), jnp.float32),
        ],
    )
    return basis_three, hessenberg.T


def solution(mesh):
    spread = ("groups", "patch", "sub")
    in_specs = (
        P(spread, None, None),
        P(spread, None, None),
        P(spread, None),
        P(spread),
        P(spread, None),
        P(spread, None),
        P(spread, None, None),
        P(spread, None, None),
        P(),
        P(spread, None),
        P(),
    )
    out_specs = (P(spread, None), P("groups", None))
    return jax.shard_map(shards, mesh=mesh, in_specs=in_specs, out_specs=out_specs, check_vma=False)
```

```python
import functools
import math

import jax
import jax.numpy as jnp
from jax import lax
from jax.experimental import pallas as pl
from jax.experimental.pallas import tpu as pltpu
from jax.sharding import PartitionSpec as P

SOFTEN = 0.05
EPSILON = 1e-06
KERNEL_SCALE = 0.25 / math.pi
HIGH_PRECISION = lax.Precision.HIGHEST
LANES = 128
TILE_ROWS = 8
VMEM_LIMIT = 16 << 20
CHUNKS = 2
FIRST = pl.CostEstimate(flops=10**11, bytes_accessed=10**10, transcendentals=0)


def from_peers(value, axis):
    size = lax.axis_size(axis)
    arrived = [
        lax.ppermute(value, axis, [(i, i ^ turn) for i in range(size)]) for turn in range(1, size)
    ]
    return [value] + arrived


def tree_sum(parts):
    while len(parts) > 1:
        parts = [parts[i] + parts[i + 1] for i in range(0, len(parts), 2)]
    return parts[0]


def device_call(kernel, outputs, scalars, arrays, scratch=(), remote=(), cost=None):
    smem = pl.BlockSpec(memory_space=pltpu.SMEM)
    vmem = pl.BlockSpec(memory_space=pltpu.VMEM)
    hbm = pl.BlockSpec(memory_space=pltpu.HBM)
    return pl.pallas_call(
        kernel,
        out_shape=tuple(outputs),
        in_specs=[smem] * len(scalars) + [vmem] * len(arrays) + [hbm] * len(remote),
        out_specs=tuple([vmem] * len(outputs)),
        scratch_shapes=tuple(scratch),
        compiler_params=pltpu.CompilerParams(vmem_limit_bytes=VMEM_LIMIT),
        cost_estimate=cost,
    )(
        *scalars,
        *[pltpu.with_memory_space_constraint(array, pltpu.VMEM) for array in arrays],
        *[pltpu.with_memory_space_constraint(array, pltpu.HBM) for array in remote],
    )


def kept(*shape, dtype=jnp.float32):
    return pltpu.VMEM(shape, dtype)


def f32(*shape):
    return jax.ShapeDtypeStruct(shape, jnp.float32)


def iota(shape, dimension):
    return lax.broadcasted_iota(jnp.int32, shape, dimension)


def split_three(value):
    first = value.astype(jnp.bfloat16).astype(jnp.float32)
    rest = value - first
    second = rest.astype(jnp.bfloat16).astype(jnp.float32)
    third = (rest - second).astype(jnp.bfloat16).astype(jnp.float32)
    return first, second, third


def lane_row(entries):
    lane = iota((1, LANES), 1)
    row = jnp.zeros((1, LANES), jnp.float32)
    for place, entry in enumerate(entries):
        row = jnp.where(lane == place, entry, row)
    return row


def copy_all(pairs, arrived):
    copies = [
        pltpu.make_async_copy(source, target, arrived.at[place])
        for place, (source, target) in enumerate(pairs)
    ]
    for copy in copies:
        copy.start()
    return copies


def add_moment(columns, vector, basis, leaf):
    column = jnp.sum(basis[leaf] * vector[leaf : leaf + 1, :], axis=1, keepdims=True)
    return jnp.where(iota(columns.shape, 1) == leaf, column, columns)


def write_moments(columns, message, start, slots):
    rank = columns.shape[0]
    message[start : start + slots, :] = jnp.zeros((slots, LANES), jnp.float32)
    message[start : start + slots, 0:rank] = columns.T[0:slots]


def sum_lanes(rows):
    column = jnp.sum(rows, axis=1, keepdims=True)
    diagonal = iota((rows.shape[0], LANES), 0) == iota((rows.shape[0], LANES), 1)
    return jnp.sum(jnp.where(diagonal, column, 0.0), axis=0, keepdims=True)


def box_moments(vector, box_basis):
    slots, rank, width = box_basis.shape
    total = jnp.zeros((rank, width), jnp.float32)
    for leaf in range(slots):
        total = total + box_basis[leaf] * vector[leaf : leaf + 1, :]
    return sum_lanes(total)


def start_kernel(counts, *refs):
    sources, (geometry, message, box_basis) = refs[:10], refs[10:13]
    basis, leaf_coupling, box_coupling, near_list, far_list = refs[13:18]
    at, initial, box_far, transfer, parts, arrived = refs[18:]
    dims, slots, width = sources[0].shape
    rank = basis.shape[1]
    targets = [at.at[0:dims], at.at[dims : 2 * dims], at.at[2 * dims], box_far]
    pairs = list(zip(sources[:4], targets))
    step = slots // CHUNKS
    for first in range(0, slots, step):
        for source, target in zip(sources[4:6], (transfer, basis)):
            pairs.append((source.at[first : first + step], target.at[first : first + step]))
    pairs += zip(sources[6:], (leaf_coupling, box_coupling, near_list, far_list))
    copies = copy_all(pairs, arrived)
    for copy in copies[:4]:
        copy.wait()
    for row in range(2 * dims):
        geometry[:, row, :] = at[row]
    vector = jnp.where(iota((slots, width), 0) < counts[0], at[2 * dims], 0.0)
    initial[...] = vector
    geometry[:, 2 * dims, :] = vector
    geometry[:, 2 * dims + 1, :] = jnp.zeros_like(vector)
    entries = [jnp.sum(vector * vector, keepdims=True)] + [
        jnp.full((1, 1), value, jnp.int32).astype(jnp.float32)
        for value in [counts[0]] + [box_far[0, place] for place in range(box_far.shape[1])]
    ]
    message[slots : slots + TILE_ROWS, :] = jnp.zeros((TILE_ROWS, LANES), jnp.float32)
    message[slots + 1 : slots + 2, :] = lane_row(entries)
    columns = jnp.zeros((rank, LANES), jnp.float32)
    for leaf in range(slots):
        if leaf % step == 0:
            for copy in copies[4 + 2 * (leaf // step) : 6 + 2 * (leaf // step)]:
                copy.wait()
        columns = add_moment(columns, vector, basis, leaf)
        product = jnp.dot(
            transfer[leaf],
            basis[leaf],
            precision=HIGH_PRECISION,
            preferred_element_type=jnp.float32,
        )
        product = jnp.where(leaf < counts[0], product, 0.0)
        box_basis[leaf] = product
        parts[:, leaf * width : (leaf + 1) * width] = split_rows(product)
    write_moments(columns, message, 0, slots)
    message[slots : slots + 1, :] = box_moments(initial, box_basis)
    products = lax.dot_general(
        parts[...], parts[...], (((1,), (1,)), ((), ())), preferred_element_type=jnp.float32
    )
    mixed = products[rank : 2 * rank, 0:rank] + products[2 * rank : 3 * rank, 0:rank]
    gram = products[0:rank, 0:rank] + (
        mixed + mixed.T + products[rank : 2 * rank, rank : 2 * rank]
    )
    start, half = slots + TILE_ROWS, rank // 2
    message[start : start + half, 0:rank] = gram[0:half]
    message[start : start + half, rank : 2 * rank] = gram[half:rank]
    for copy in copies[4 + 2 * CHUNKS :]:
        copy.wait()


def join_kernel(subs, *refs):
    messages, (moments, blocks) = refs[:subs], refs[subs + 1 :]
    slots, span = moments.shape[0] // subs, blocks.shape[0] // subs
    for sub, message in enumerate(messages):
        moments[sub * slots : (sub + 1) * slots, :] = message[0:slots, :]
        blocks[sub * span : (sub + 1) * span, :] = message[slots : slots + span, :]


def split_rows(rows):
    return jnp.concatenate(split_three(rows)).astype(jnp.bfloat16)


def write_weights(coupling, weights):
    for place in range(coupling.shape[0]):
        parts = jnp.concatenate(split_three(coupling[place].T), axis=1)
        weights[place] = parts.astype(jnp.bfloat16)


def coupled_rows(chosen, weights):
    total = None
    for place in range(weights.shape[0]):
        product = jnp.dot(chosen(place), weights[place], preferred_element_type=jnp.float32)
        total = product if total is None else total + product
    count, rank = total.shape[0] // 3, total.shape[1] // 3
    part = [
        [total[row * count : (row + 1) * count, at * rank : (at + 1) * rank] for at in range(3)]
        for row in range(3)
    ]
    return part[0][0] + (
        (part[0][1] + part[1][0]) + (part[0][2] + part[2][0] + part[1][1])
    )


def leaf_part(moments, picks, weights):
    slots = picks.shape[0] // weights.shape[0]
    parts = [
        jnp.dot(
            picks[...], part.astype(jnp.bfloat16), preferred_element_type=jnp.float32
        ).astype(jnp.bfloat16)
        for part in split_three(moments)
    ]

    def chosen(place):
        return jnp.concatenate([part[place * slots : (place + 1) * slots] for part in parts])

    return coupled_rows(chosen, weights)


def wide_transpose(rows):
    count, lanes = rows.shape
    return jnp.concatenate([rows, jnp.zeros((count, LANES - lanes), rows.dtype)], axis=1).T


def leaf_far_row(counts, columns, basis, leaf, near):
    rank = basis.shape[1]
    far = jnp.sum(basis[leaf] * columns[0:rank, leaf : leaf + 1], axis=0, keepdims=True)
    return jnp.where(leaf < counts[0], near + far, 0.0)


def weights_kernel(box, coupling, box_coupling, far_list, *refs):
    picks, weights, box_weights = refs
    far_count, slots = far_list.shape
    far_rows = wide_transpose(far_list[...].astype(jnp.float32))
    leaves = (iota((slots, picks.shape[1]), 1) ^ (box[0] * slots)).astype(jnp.float32)
    for place in range(far_count):
        chosen = jnp.where(far_rows[0:slots, place : place + 1] == leaves, 1.0, 0.0)
        picks[place * slots : (place + 1) * slots, :] = chosen.astype(jnp.bfloat16)
    write_weights(coupling, weights)
    write_weights(box_coupling, box_weights)


def leaf_kernel(counts, moments, basis, picks, weights, far):
    slots, rank, width = basis.shape
    columns = wide_transpose(leaf_part(moments[:, 0:rank], picks, weights))
    for leaf in range(slots):
        far[leaf : leaf + 1, :] = leaf_far_row(counts, columns, basis, leaf, 0.0)


def first_near_kernel(subs, box, counts, *refs):
    geometry, (far, near_source) = refs[:subs], refs[subs : subs + 2]
    near, initial, values, features, squares, fields, inner, near_list, arrived = refs[subs + 2 :]
    copy = pltpu.make_async_copy(near_source, near_list, arrived)
    copy.start()
    slots, height, width = geometry[0].shape
    neighbours = near_list.shape[0]
    row = iota((height, width), 0)
    scale_square = jnp.where(row < 3, -2.0, 0.0)
    ones = jnp.where(row == 7, 1.0, 0.0)
    scale_normal = jnp.where((row >= 3) & (row < 6), -KERNEL_SCALE, 0.0)

    for sub in range(subs):
        rows = geometry[sub]
        at = [rows[:, component, :] for component in range(7)]
        squares[sub * slots : (sub + 1) * slots, :] = at[0] * at[0] + at[1] * at[1] + at[2] * at[2]
        fields[sub * slots : (sub + 1) * slots, :] = at[6]
        inner[...] = (at[0] * at[3] + at[1] * at[4] + at[2] * at[5]) * KERNEL_SCALE

        def source(leaf, carry, rows=rows, sub=sub):
            place = sub * slots + leaf
            plain = rows[leaf]
            square = squares[pl.ds(place, 1), :] + SOFTEN
            distance = jnp.where(row == 6, square, plain * scale_square + ones)
            numerator = jnp.where(row == 6, inner[pl.ds(leaf, 1), :], plain * scale_normal)
            for part, value in enumerate((distance, numerator)):
                one, two, three = split_three(value)
                lanes = slice(part * width, (part + 1) * width)
                features[place, 0:16, lanes] = jnp.concatenate([one, two]).astype(jnp.bfloat16)
                features[place, 16:32, lanes] = jnp.concatenate([one, three]).astype(jnp.bfloat16)
            return carry

        lax.fori_loop(0, slots, source, 0, unroll=True)

    own = geometry[0]

    def target(leaf, carry):
        plain = own[leaf]
        shifted = pltpu.roll(plain, 3, 0)
        square = squares[pl.ds(leaf, 1), :]
        value = jnp.where(row < 3, plain, jnp.where(row < 6, shifted, jnp.where(row == 6, 1.0, square)))
        one, two, three = split_three(value)
        left = jnp.concatenate([one, one, two, two, three, one]).T.astype(jnp.bfloat16)
        total = jnp.zeros((width, width), jnp.float32)
        for column in range(neighbours):
            place = near_list[column, leaf] ^ (box[0] * slots)
            upper, lower = features[place, 0:16, :], features[place, 16:32, :]
            right = jnp.concatenate([upper, upper, lower], axis=0)
            both = jnp.dot(left, right, preferred_element_type=jnp.float32)
            inverse = lax.rsqrt(both[:, 0:width])
            tile = both[:, width : 2 * width] * (inverse * inverse * inverse)
            values[leaf * neighbours + column] = tile
            total = total + tile * fields[pl.ds(place, 1), :]
        near[pl.ds(leaf, 1), :] = jnp.sum(total.T, axis=0, keepdims=True)
        return carry

    copy.wait()
    initial[...] = fields[0:slots, :]
    lax.fori_loop(0, slots, target, 0, unroll=True)
    in_use = iota((slots, width), 0) < counts[0]
    near[...] = jnp.where(in_use, near[...] + far[...], 0.0)


def box_images(box_basis, coefficients, image):
    slots, rank, width = box_basis.shape
    spread = jnp.broadcast_to(coefficients, (rank, width))
    for leaf in range(slots):
        image[leaf : leaf + 1, :] += jnp.sum(box_basis[leaf] * spread, axis=0, keepdims=True)


def first_image_kernel(patches, span, box, *refs):
    boxes = refs[:patches]
    part, initial, basis, box_basis, box_coupling = refs[patches : patches + 5]
    message, basis_one, numbers, starts, image = refs[patches + 5 :]
    slots, rank, width = basis.shape
    height = boxes[0].shape[0]
    row_starts = [(ref, at) for ref in boxes for at in range(0, height, span)]
    count = len(row_starts)
    for place, (ref, at) in enumerate(row_starts):
        starts[place : place + 1, :] = ref[at : at + 1, :]
    number = (iota((count, LANES), 0) ^ box[0]).astype(jnp.float32)
    coupled = jnp.zeros((rank, rank), jnp.float32)
    for place in range(box_coupling.shape[0]):
        wanted = boxes[0][1:2, 2 + place : 3 + place]
        row = jnp.sum(jnp.where(number == wanted, starts[...], 0.0), axis=0, keepdims=True)
        coupled = coupled + box_coupling[place] * row[:, 0:rank]
    image[...] = part[...]
    box_images(box_basis, jnp.sum(coupled, axis=1, keepdims=True), image)
    sums = tree_sum(
        [
            tree_sum([ref[at + 1 : at + 2, :] for at in range(0, height, span)])
            for ref in boxes
        ]
    )
    square_sum, unknowns = sums[:, 0:1], width * sums[:, 1:2]
    start_scale = jnp.sqrt(square_sum / unknowns + EPSILON)
    one_one = square_sum / (start_scale * start_scale)
    basis_one[...] = initial[...] / start_scale
    vector = image[...] / start_scale
    message[0:slots, :] = vector
    numbers[...] = jnp.broadcast_to(lane_row([one_one, unknowns, start_scale]), numbers.shape)
    columns = jnp.zeros((rank, LANES), jnp.float32)
    for leaf in range(slots):
        columns = add_moment(columns, vector, basis, leaf)
    write_moments(columns, message, slots, slots)


def share_kernel(patches, span, box, *refs):
    boxes, (message, basis_one, box_basis) = refs[:patches], refs[patches : patches + 3]
    share, starts, rows, grams, gather, lists = refs[patches + 3 :]
    slots, rank, _ = box_basis.shape
    first, one = message[0:slots, :], basis_one[...]
    products = [one * first, first * first]
    share[...] = jnp.zeros_like(share)
    share[0:1, :] = box_moments(message, box_basis)
    share[1:2, :] = lane_row([jnp.sum(product, keepdims=True) for product in products])
    height, count, half = boxes[0].shape[0], starts.shape[0], rank // 2
    for place, ref in enumerate(boxes):
        gather[place * height : (place + 1) * height, :] = ref[...]
    for other in range(count):
        row = (box[0] ^ other) * span
        starts[other : other + 1, :] = gather[pl.ds(row, 1), :]
        lists[other : other + 1, :] = gather[pl.ds(row + 1, 1), :]
        grams[other * half : (other + 1) * half, :] = gather[pl.ds(row + TILE_ROWS, half), :]
    column = iota((count, 3 * count), 1)
    chosen = []
    for place in range(rows.shape[0] // (3 * count)):
        wanted = lists[:, 2 + place : 3 + place]
        for split in range(3):
            number = (column - split * count).astype(jnp.float32)
            chosen.append(jnp.where(wanted == number, 1.0, 0.0))
    rows[...] = jnp.concatenate(chosen).astype(jnp.bfloat16)


def second_near_kernel(subs, box, counts, *refs):
    messages = refs[:subs]
    picks, weights, basis, box_basis, basis_one, share, values = refs[subs : subs + 7]
    near_source, part, shares, fields, near_list, arrived = refs[subs + 7 :]
    copy = pltpu.make_async_copy(near_source, near_list, arrived)
    copy.start()
    slots, width = part.shape
    neighbours = near_list.shape[0]
    rank = basis.shape[1]
    for sub in range(subs):
        fields[sub * slots : (sub + 1) * slots, :] = messages[sub][0:slots, :]

    moments = jnp.concatenate([ref[slots : 2 * slots, 0:rank] for ref in messages], axis=0)
    columns = wide_transpose(leaf_part(moments, picks, weights))
    copy.wait()
    box_sum = jnp.zeros(box_basis.shape[1:], jnp.float32)
    for leaf in range(slots):
        total = jnp.zeros((width, width), jnp.float32)
        for column in range(neighbours):
            place = near_list[column, leaf] ^ (box[0] * slots)
            total = total + values[leaf * neighbours + column] * fields[pl.ds(place, 1), :]
        near = jnp.sum(total.T, axis=0, keepdims=True)
        near = leaf_far_row(counts, columns, basis, leaf, near)
        part[leaf : leaf + 1, :] = near
        box_sum = box_sum + box_basis[leaf] * near
    first, one, second = messages[0][0:slots, :], basis_one[...], part[...]
    products = [one * second, first * second, second * second]
    sums = lane_row([jnp.sum(product, keepdims=True) for product in products])
    sums = share[1:2, :] + pltpu.roll(sums, 2, 1)
    both = share[0:1, :] + pltpu.roll(sum_lanes(box_sum), rank, 1)
    shares[...] = jnp.where(iota(shares.shape, 0) % 2 == 0, both, sums)


def last_kernel(box, *refs):
    shares, message, basis_one, part, numbers, starts, rows, grams = refs[:8]
    box_basis, box_weights, basis_three, hessenberg, pairs, image = refs[8:]
    slots, rank, width = box_basis.shape
    count = starts.shape[0]
    for other in range(count):
        pairs[other : other + 1, :] = shares[2 * other : 2 * other + 1, :]
        pairs[count + other : count + other + 1, :] = shares[2 * other + 1 : 2 * other + 2, :]
    first_box, second_box = pairs[0:count, 0:rank], pairs[0:count, rank : 2 * rank]
    chosen_rows = jnp.dot(
        rows[...], split_rows(first_box), preferred_element_type=jnp.float32
    ).astype(jnp.bfloat16)

    def chosen(place):
        return chosen_rows[place * 3 * count : (place + 1) * 3 * count]

    box_local = coupled_rows(chosen, box_weights)
    twice = jnp.concatenate([box_local, box_local], axis=1)
    columns = twice.T
    half = rank // 2
    low = iota((half, 2 * rank), 1) < rank
    quadratic = jnp.zeros((half, 2 * rank), jnp.float32)
    for other in range(count):
        column = jnp.where(
            low, columns[0:half, other : other + 1], columns[half:rank, other : other + 1]
        )
        gram = grams[other * half : (other + 1) * half, :]
        quadratic = quadratic + gram * twice[other : other + 1, :] * column
    one_one, unknowns, start_scale = [numbers[0:1, place : place + 1] for place in range(3)]
    sums = jnp.sum(pairs[count : 2 * count, :], axis=0, keepdims=True)
    along, image_sq, one_part, first_part, part_sq = [
        sums[:, place : place + 1] for place in range(5)
    ]
    one_second = (
        one_part + jnp.sum(starts[:, 0:rank] * box_local, keepdims=True) / start_scale
    )
    first_second = first_part + jnp.sum(first_box * box_local, keepdims=True)
    second_sq = (
        part_sq
        + 2.0 * jnp.sum(second_box * box_local, keepdims=True)
        + jnp.sum(quadratic, keepdims=True)
    )
    upper_first = (0.5 * one_one + along) / unknowns
    shift = upper_first - 0.5
    residual_sq = image_sq - 2.0 * shift * along + shift * shift * one_one
    lower_first = jnp.sqrt(residual_sq / unknowns + EPSILON)
    one_two = (along - shift * one_one) / lower_first
    two_two = residual_sq / (lower_first * lower_first)
    k_one = (one_second - shift * along) / lower_first
    k_two = (
        (first_second - shift * image_sq) - shift * (one_second - shift * along)
    ) / (lower_first * lower_first)
    k_sq = (second_sq - 2.0 * shift * first_second + shift * shift * image_sq) / (
        lower_first * lower_first
    )
    upper_second = (0.5 * one_two + k_one) / unknowns
    middle_second = (0.5 * two_two + k_two - upper_second * one_two) / unknowns
    turn = middle_second - 0.5
    final_sq = (
        k_sq
        - 2.0 * upper_second * k_one
        - 2.0 * turn * k_two
        + upper_second * upper_second * one_one
        + 2.0 * upper_second * turn * one_two
        + turn * turn * two_two
    )
    lower_second = jnp.sqrt(final_sq / unknowns + EPSILON)
    image[...] = part[...]
    own = jnp.where(iota((rank, count), 1) == box[0], columns[0:rank], 0.0)
    box_images(box_basis, jnp.sum(own, axis=1, keepdims=True), image)
    one, first = basis_one[...], message[0:slots, :]
    two = (first - shift * one) / lower_first
    mapped = (image[...] - shift * first) / lower_first
    basis_three[...] = (mapped - upper_second * one - turn * two) / lower_second
    column, row = iota(hessenberg.shape, 0), iota(hessenberg.shape, 1)
    matrix = jnp.where(column == 0, upper_first, upper_second)
    matrix = jnp.where(row == 1, jnp.where(column == 0, lower_first, middle_second), matrix)
    hessenberg[...] = jnp.where(row == 2, jnp.where(column == 0, 0.0, lower_second), matrix)


def shards(
    points,
    normals,
    density,
    counts,
    near_list,
    leaf_far,
    leaf_basis,
    leaf_to_box_transfer,
    leaf_coupling,
    box_far,
    box_coupling,
):
    slots, _, width = points.shape
    neighbours = near_list.shape[1]
    far_count = leaf_far.shape[1]
    subs, patches = lax.axis_size("sub"), lax.axis_size("patch")
    sources = subs * slots
    rows = kept(slots, width)
    this_box = lax.axis_index("patch") * subs + lax.axis_index("sub")
    box = this_box.astype(jnp.int32).reshape(1)
    far_list = leaf_far.T
    rank = leaf_basis.shape[1]
    span = TILE_ROWS + rank // 2
    near_list = near_list.T
    list_scratch = [pltpu.SMEM(near_list.shape, jnp.int32), pltpu.SemaphoreType.DMA]
    block = pltpu.VMEM((sources, width), jnp.float32)

    matrices, lists = [leaf_basis, leaf_coupling, box_coupling], [near_list, far_list]
    geometry, message, box_basis, *held = device_call(
        start_kernel,
        [
            kept(slots, 8, width),
            kept(slots + span, LANES),
            kept(*leaf_basis.shape),
            *[kept(*matrix.shape) for matrix in matrices],
            *[kept(*entries.shape, dtype=jnp.int32) for entries in lists],
        ],
        [counts],
        [],
        [
            pltpu.VMEM((7, slots, width), jnp.float32),
            pltpu.VMEM((slots, width), jnp.float32),
            pltpu.SMEM(box_far.shape, jnp.int32),
            pltpu.VMEM(leaf_to_box_transfer.shape, jnp.float32),
            pltpu.VMEM((3 * rank, slots * width), jnp.bfloat16),
            pltpu.SemaphoreType.DMA((8 + 2 * CHUNKS,)),
        ],
        [
            points.transpose(1, 0, 2),
            normals.transpose(1, 0, 2),
            density,
            box_far,
            leaf_to_box_transfer,
            *matrices,
            *lists,
        ],
    )
    leaf_basis, leaf_coupling, box_coupling, near_list, far_list = held
    messages = from_peers(message, "sub")
    geometry = from_peers(geometry, "sub")
    picks, weights, box_weights = device_call(
        weights_kernel,
        [
            kept(far_count * slots, sources, dtype=jnp.bfloat16),
            kept(far_count, rank, 3 * rank, dtype=jnp.bfloat16),
            kept(box_coupling.shape[0], rank, 3 * rank, dtype=jnp.bfloat16),
        ],
        [box],
        [leaf_coupling, box_coupling, far_list],
    )
    moments, blocks = device_call(
        functools.partial(join_kernel, subs),
        [kept(sources, LANES), kept(subs * span, LANES)],
        [],
        [*messages, box_weights],
        cost=FIRST,
    )
    boxes = from_peers(blocks, "patch")
    (far,) = device_call(leaf_kernel, [rows], [counts], [moments, leaf_basis, picks, weights])
    part, initial, values = device_call(
        functools.partial(first_near_kernel, subs),
        [rows, rows, kept(slots * neighbours, width, width)],
        [box, counts],
        [*geometry, far, near_list],
        [
            pltpu.VMEM((sources, 32, 2 * width), jnp.bfloat16),
            block,
            block,
            pltpu.VMEM((slots, width), jnp.float32),
            *list_scratch,
        ],
    )
    message, basis_one, numbers = device_call(
        functools.partial(first_image_kernel, patches, span),
        [kept(2 * slots, LANES), rows, kept(TILE_ROWS, LANES)],
        [box],
        [*boxes, part, initial, leaf_basis, box_basis, box_coupling],
        [
            pltpu.VMEM((patches * subs, LANES), jnp.float32),
            pltpu.VMEM((slots, width), jnp.float32),
        ],
    )
    messages = from_peers(message, "sub")
    count, places = patches * subs, box_far.shape[1]
    share, starts, chosen, grams = device_call(
        functools.partial(share_kernel, patches, span),
        [
            kept(TILE_ROWS, LANES),
            kept(count, LANES),
            kept(places * 3 * count, 3 * count, dtype=jnp.bfloat16),
            kept(count * (rank // 2), LANES),
        ],
        [box],
        [*boxes, message, basis_one, box_basis],
        [
            pltpu.VMEM((count * span, LANES), jnp.float32),
            pltpu.VMEM((count, LANES), jnp.float32),
        ],
    )
    part, shares = device_call(
        functools.partial(second_near_kernel, subs),
        [rows, kept(2 * patches * subs, LANES)],
        [box, counts],
        [*messages, picks, weights, leaf_basis, box_basis, basis_one, share, values, near_list],
        [block, *list_scratch],
    )
    shares = lax.all_to_all(shares, ("patch", "sub"), 0, 0, tiled=True)
    basis_three, hessenberg = device_call(
        last_kernel,
        [f32(slots, width), f32(2, 3)],
        [box],
        [
            shares,
            message,
            basis_one,
            part,
            numbers,
            starts,
            chosen,
            grams,
            box_basis,
            box_weights,
        ],
        [
            pltpu.VMEM((2 * count, LANES), jnp.float32),
            pltpu.VMEM((slots, width), jnp.float32),
        ],
    )
    return basis_three, hessenberg.T


def solution(mesh):
    spread = ("groups", "patch", "sub")
    in_specs = (
        P(spread, None, None),
        P(spread, None, None),
        P(spread, None),
        P(spread),
        P(spread, None),
        P(spread, None),
        P(spread, None, None),
        P(spread, None, None),
        P(),
        P(spread, None),
        P(),
    )
    out_specs = (P(spread, None), P("groups", None))
    return jax.shard_map(shards, mesh=mesh, in_specs=in_specs, out_specs=out_specs, check_vma=False)
```

```python
import functools
import math

import jax
import jax.numpy as jnp
from jax import lax
from jax.experimental import pallas as pl
from jax.experimental.pallas import tpu as pltpu
from jax.sharding import PartitionSpec as P

SOFTEN = 0.05
EPSILON = 1e-06
KERNEL_SCALE = 0.25 / math.pi
HIGH_PRECISION = lax.Precision.HIGHEST
LANES = 128
TILE_ROWS = 8
VMEM_LIMIT = 16 << 20
CHUNKS = 2
FIRST = pl.CostEstimate(flops=10**11, bytes_accessed=10**10, transcendentals=0)


def from_peers(value, axis):
    size = lax.axis_size(axis)
    arrived = [
        lax.ppermute(value, axis, [(i, i ^ turn) for i in range(size)]) for turn in range(1, size)
    ]
    return [value] + arrived


def tree_sum(parts):
    while len(parts) > 1:
        parts = [parts[i] + parts[i + 1] for i in range(0, len(parts), 2)]
    return parts[0]


def device_call(kernel, outputs, scalars, arrays, scratch=(), remote=(), cost=None):
    smem = pl.BlockSpec(memory_space=pltpu.SMEM)
    vmem = pl.BlockSpec(memory_space=pltpu.VMEM)
    hbm = pl.BlockSpec(memory_space=pltpu.HBM)
    return pl.pallas_call(
        kernel,
        out_shape=tuple(outputs),
        in_specs=[smem] * len(scalars) + [vmem] * len(arrays) + [hbm] * len(remote),
        out_specs=tuple([vmem] * len(outputs)),
        scratch_shapes=tuple(scratch),
        compiler_params=pltpu.CompilerParams(vmem_limit_bytes=VMEM_LIMIT),
        cost_estimate=cost,
    )(
        *scalars,
        *[pltpu.with_memory_space_constraint(array, pltpu.VMEM) for array in arrays],
        *[pltpu.with_memory_space_constraint(array, pltpu.HBM) for array in remote],
    )


def kept(*shape, dtype=jnp.float32):
    return pltpu.VMEM(shape, dtype)


def f32(*shape):
    return jax.ShapeDtypeStruct(shape, jnp.float32)


def iota(shape, dimension):
    return lax.broadcasted_iota(jnp.int32, shape, dimension)


def split_three(value):
    first = value.astype(jnp.bfloat16).astype(jnp.float32)
    rest = value - first
    second = rest.astype(jnp.bfloat16).astype(jnp.float32)
    third = (rest - second).astype(jnp.bfloat16).astype(jnp.float32)
    return first, second, third


def lane_row(entries):
    lane = iota((1, LANES), 1)
    row = jnp.zeros((1, LANES), jnp.float32)
    for place, entry in enumerate(entries):
        row = jnp.where(lane == place, entry, row)
    return row


def copy_all(pairs, arrived):
    copies = [
        pltpu.make_async_copy(source, target, arrived.at[place])
        for place, (source, target) in enumerate(pairs)
    ]
    for copy in copies:
        copy.start()
    return copies


def add_moment(columns, vector, basis, leaf):
    column = jnp.sum(basis[leaf] * vector[leaf : leaf + 1, :], axis=1, keepdims=True)
    return jnp.where(iota(columns.shape, 1) == leaf, column, columns)


def write_moments(columns, message, start, slots):
    rank = columns.shape[0]
    message[start : start + slots, :] = jnp.zeros((slots, LANES), jnp.float32)
    message[start : start + slots, 0:rank] = columns.T[0:slots]


def sum_lanes(rows):
    column = jnp.sum(rows, axis=1, keepdims=True)
    diagonal = iota((rows.shape[0], LANES), 0) == iota((rows.shape[0], LANES), 1)
    return jnp.sum(jnp.where(diagonal, column, 0.0), axis=0, keepdims=True)


def box_moments(vector, box_basis):
    slots, rank, width = box_basis.shape
    total = jnp.zeros((rank, width), jnp.float32)
    for leaf in range(slots):
        total = total + box_basis[leaf] * vector[leaf : leaf + 1, :]
    return sum_lanes(total)


def start_kernel(counts, *refs):
    sources, (geometry, message, box_basis) = refs[:10], refs[10:13]
    basis, leaf_coupling, box_coupling, near_list, far_list = refs[13:18]
    at, initial, box_far, transfer, parts, arrived = refs[18:]
    dims, slots, width = sources[0].shape
    rank = basis.shape[1]
    targets = [at.at[0:dims], at.at[dims : 2 * dims], at.at[2 * dims], box_far]
    pairs = list(zip(sources[:4], targets))
    step = slots // CHUNKS
    for first in range(0, slots, step):
        for source, target in zip(sources[4:6], (transfer, basis)):
            pairs.append((source.at[first : first + step], target.at[first : first + step]))
    pairs += zip(sources[6:], (leaf_coupling, box_coupling, near_list, far_list))
    copies = copy_all(pairs, arrived)
    for copy in copies[:4]:
        copy.wait()
    for row in range(2 * dims):
        geometry[:, row, :] = at[row]
    vector = jnp.where(iota((slots, width), 0) < counts[0], at[2 * dims], 0.0)
    initial[...] = vector
    geometry[:, 2 * dims, :] = vector
    geometry[:, 2 * dims + 1, :] = jnp.zeros_like(vector)
    entries = [jnp.sum(vector * vector, keepdims=True)] + [
        jnp.full((1, 1), value, jnp.int32).astype(jnp.float32)
        for value in [counts[0]] + [box_far[0, place] for place in range(box_far.shape[1])]
    ]
    message[slots : slots + TILE_ROWS, :] = jnp.zeros((TILE_ROWS, LANES), jnp.float32)
    message[slots + 1 : slots + 2, :] = lane_row(entries)
    columns = jnp.zeros((rank, LANES), jnp.float32)
    for leaf in range(slots):
        if leaf % step == 0:
            for copy in copies[4 + 2 * (leaf // step) : 6 + 2 * (leaf // step)]:
                copy.wait()
        columns = add_moment(columns, vector, basis, leaf)
        product = jnp.dot(
            transfer[leaf],
            basis[leaf],
            precision=HIGH_PRECISION,
            preferred_element_type=jnp.float32,
        )
        product = jnp.where(leaf < counts[0], product, 0.0)
        box_basis[leaf] = product
        parts[:, leaf * width : (leaf + 1) * width] = split_rows(product)
    write_moments(columns, message, 0, slots)
    message[slots : slots + 1, :] = box_moments(initial, box_basis)
    products = lax.dot_general(
        parts[...], parts[...], (((1,), (1,)), ((), ())), preferred_element_type=jnp.float32
    )
    mixed = products[rank : 2 * rank, 0:rank] + products[2 * rank : 3 * rank, 0:rank]
    gram = products[0:rank, 0:rank] + (
        mixed + mixed.T + products[rank : 2 * rank, rank : 2 * rank]
    )
    start, half = slots + TILE_ROWS, rank // 2
    message[start : start + half, 0:rank] = gram[0:half]
    message[start : start + half, rank : 2 * rank] = gram[half:rank]
    for copy in copies[4 + 2 * CHUNKS :]:
        copy.wait()


def join_kernel(subs, *refs):
    messages, (moments, blocks) = refs[:subs], refs[subs + 1 :]
    slots, span = moments.shape[0] // subs, blocks.shape[0] // subs
    for sub, message in enumerate(messages):
        moments[sub * slots : (sub + 1) * slots, :] = message[0:slots, :]
        blocks[sub * span : (sub + 1) * span, :] = message[slots : slots + span, :]


def split_rows(rows):
    return jnp.concatenate(split_three(rows)).astype(jnp.bfloat16)


def write_weights(coupling, weights):
    for place in range(coupling.shape[0]):
        parts = jnp.concatenate(split_three(coupling[place].T), axis=1)
        weights[place] = parts.astype(jnp.bfloat16)


def coupled_rows(chosen, weights):
    total = None
    for place in range(weights.shape[0]):
        product = jnp.dot(chosen(place), weights[place], preferred_element_type=jnp.float32)
        total = product if total is None else total + product
    count, rank = total.shape[0] // 3, total.shape[1] // 3
    part = [
        [total[row * count : (row + 1) * count, at * rank : (at + 1) * rank] for at in range(3)]
        for row in range(3)
    ]
    return part[0][0] + (
        (part[0][1] + part[1][0]) + (part[0][2] + part[2][0] + part[1][1])
    )


def leaf_part(moments, picks, weights):
    slots = picks.shape[0] // weights.shape[0]
    parts = [
        jnp.dot(
            picks[...], part.astype(jnp.bfloat16), preferred_element_type=jnp.float32
        ).astype(jnp.bfloat16)
        for part in split_three(moments)
    ]

    def chosen(place):
        return jnp.concatenate([part[place * slots : (place + 1) * slots] for part in parts])

    return coupled_rows(chosen, weights)


def wide_transpose(rows):
    count, lanes = rows.shape
    return jnp.concatenate([rows, jnp.zeros((count, LANES - lanes), rows.dtype)], axis=1).T


def leaf_far_row(counts, columns, basis, leaf, near):
    rank = basis.shape[1]
    far = jnp.sum(basis[leaf] * columns[0:rank, leaf : leaf + 1], axis=0, keepdims=True)
    return jnp.where(leaf < counts[0], near + far, 0.0)


def weights_kernel(box, coupling, box_coupling, far_list, *refs):
    picks, weights, box_weights = refs
    far_count, slots = far_list.shape
    far_rows = wide_transpose(far_list[...].astype(jnp.float32))
    leaves = (iota((slots, picks.shape[1]), 1) ^ (box[0] * slots)).astype(jnp.float32)
    for place in range(far_count):
        chosen = jnp.where(far_rows[0:slots, place : place + 1] == leaves, 1.0, 0.0)
        picks[place * slots : (place + 1) * slots, :] = chosen.astype(jnp.bfloat16)
    write_weights(coupling, weights)
    write_weights(box_coupling, box_weights)


def leaf_kernel(moments, picks, weights, columns):
    rank = weights.shape[1]
    columns[...] = wide_transpose(leaf_part(moments[:, 0:rank], picks, weights))


def first_near_kernel(subs, box, counts, *refs):
    geometry, (columns, basis, near_source) = refs[:subs], refs[subs : subs + 3]
    near, initial, values, features, squares, fields, inner, near_list, arrived = refs[subs + 3 :]
    copy = pltpu.make_async_copy(near_source, near_list, arrived)
    copy.start()
    slots, height, width = geometry[0].shape
    neighbours = near_list.shape[0]
    row = iota((height, width), 0)
    scale_square = jnp.where(row < 3, -2.0, 0.0)
    ones = jnp.where(row == 7, 1.0, 0.0)
    scale_normal = jnp.where((row >= 3) & (row < 6), -KERNEL_SCALE, 0.0)

    for sub in range(subs):
        rows = geometry[sub]
        at = [rows[:, component, :] for component in range(7)]
        squares[sub * slots : (sub + 1) * slots, :] = at[0] * at[0] + at[1] * at[1] + at[2] * at[2]
        fields[sub * slots : (sub + 1) * slots, :] = at[6]
        inner[...] = (at[0] * at[3] + at[1] * at[4] + at[2] * at[5]) * KERNEL_SCALE

        def source(leaf, carry, rows=rows, sub=sub):
            place = sub * slots + leaf
            plain = rows[leaf]
            square = squares[pl.ds(place, 1), :] + SOFTEN
            distance = jnp.where(row == 6, square, plain * scale_square + ones)
            numerator = jnp.where(row == 6, inner[pl.ds(leaf, 1), :], plain * scale_normal)
            for part, value in enumerate((distance, numerator)):
                one, two, three = split_three(value)
                lanes = slice(part * width, (part + 1) * width)
                features[place, 0:16, lanes] = jnp.concatenate([one, two]).astype(jnp.bfloat16)
                features[place, 16:32, lanes] = jnp.concatenate([one, three]).astype(jnp.bfloat16)
            return carry

        lax.fori_loop(0, slots, source, 0, unroll=True)

    own = geometry[0]

    copy.wait()
    initial[...] = fields[0:slots, :]
    locals_of = columns[...]
    for leaf in range(slots):
        plain = own[leaf]
        shifted = pltpu.roll(plain, 3, 0)
        square = squares[pl.ds(leaf, 1), :]
        value = jnp.where(row < 3, plain, jnp.where(row < 6, shifted, jnp.where(row == 6, 1.0, square)))
        one, two, three = split_three(value)
        left = jnp.concatenate([one, one, two, two, three, one]).T.astype(jnp.bfloat16)
        total = jnp.zeros((width, width), jnp.float32)
        for column in range(neighbours):
            place = near_list[column, leaf] ^ (box[0] * slots)
            upper, lower = features[place, 0:16, :], features[place, 16:32, :]
            right = jnp.concatenate([upper, upper, lower], axis=0)
            both = jnp.dot(left, right, preferred_element_type=jnp.float32)
            inverse = lax.rsqrt(both[:, 0:width])
            tile = both[:, width : 2 * width] * (inverse * inverse * inverse)
            values[leaf * neighbours + column] = tile
            total = total + tile * fields[pl.ds(place, 1), :]
        near_row = jnp.sum(total.T, axis=0, keepdims=True)
        near[leaf : leaf + 1, :] = leaf_far_row(counts, locals_of, basis, leaf, near_row)


def box_images(box_basis, coefficients, image):
    slots, rank, width = box_basis.shape
    spread = jnp.broadcast_to(coefficients, (rank, width))
    for leaf in range(slots):
        image[leaf : leaf + 1, :] += jnp.sum(box_basis[leaf] * spread, axis=0, keepdims=True)


def first_image_kernel(patches, span, box, *refs):
    boxes = refs[:patches]
    part, initial, basis, box_basis, box_coupling = refs[patches : patches + 5]
    message, basis_one, numbers, starts, image = refs[patches + 5 :]
    slots, rank, width = basis.shape
    height = boxes[0].shape[0]
    row_starts = [(ref, at) for ref in boxes for at in range(0, height, span)]
    count = len(row_starts)
    for place, (ref, at) in enumerate(row_starts):
        starts[place : place + 1, :] = ref[at : at + 1, :]
    number = (iota((count, LANES), 0) ^ box[0]).astype(jnp.float32)
    coupled = jnp.zeros((rank, rank), jnp.float32)
    for place in range(box_coupling.shape[0]):
        wanted = boxes[0][1:2, 2 + place : 3 + place]
        row = jnp.sum(jnp.where(number == wanted, starts[...], 0.0), axis=0, keepdims=True)
        coupled = coupled + box_coupling[place] * row[:, 0:rank]
    image[...] = part[...]
    box_images(box_basis, jnp.sum(coupled, axis=1, keepdims=True), image)
    sums = tree_sum(
        [
            tree_sum([ref[at + 1 : at + 2, :] for at in range(0, height, span)])
            for ref in boxes
        ]
    )
    square_sum, unknowns = sums[:, 0:1], width * sums[:, 1:2]
    start_scale = jnp.sqrt(square_sum / unknowns + EPSILON)
    one_one = square_sum / (start_scale * start_scale)
    basis_one[...] = initial[...] / start_scale
    vector = image[...] / start_scale
    message[0:slots, :] = vector
    numbers[...] = jnp.broadcast_to(lane_row([one_one, unknowns, start_scale]), numbers.shape)
    columns = jnp.zeros((rank, LANES), jnp.float32)
    for leaf in range(slots):
        columns = add_moment(columns, vector, basis, leaf)
    write_moments(columns, message, slots, slots)


def share_kernel(patches, span, box, *refs):
    boxes, (message, basis_one, box_basis) = refs[:patches], refs[patches : patches + 3]
    share, starts, rows, grams, gather, lists = refs[patches + 3 :]
    slots, rank, _ = box_basis.shape
    first, one = message[0:slots, :], basis_one[...]
    products = [one * first, first * first]
    share[...] = jnp.zeros_like(share)
    share[0:1, :] = box_moments(message, box_basis)
    share[1:2, :] = lane_row([jnp.sum(product, keepdims=True) for product in products])
    height, count, half = boxes[0].shape[0], starts.shape[0], rank // 2
    for place, ref in enumerate(boxes):
        gather[place * height : (place + 1) * height, :] = ref[...]
    for other in range(count):
        row = (box[0] ^ other) * span
        starts[other : other + 1, :] = gather[pl.ds(row, 1), :]
        lists[other : other + 1, :] = gather[pl.ds(row + 1, 1), :]
        grams[other * half : (other + 1) * half, :] = gather[pl.ds(row + TILE_ROWS, half), :]
    column = iota((count, 3 * count), 1)
    chosen = []
    for place in range(rows.shape[0] // (3 * count)):
        wanted = lists[:, 2 + place : 3 + place]
        for split in range(3):
            number = (column - split * count).astype(jnp.float32)
            chosen.append(jnp.where(wanted == number, 1.0, 0.0))
    rows[...] = jnp.concatenate(chosen).astype(jnp.bfloat16)


def second_near_kernel(subs, box, counts, *refs):
    messages = refs[:subs]
    picks, weights, basis, box_basis, basis_one, share, values = refs[subs : subs + 7]
    near_source, part, shares, fields, near_list, arrived = refs[subs + 7 :]
    copy = pltpu.make_async_copy(near_source, near_list, arrived)
    copy.start()
    slots, width = part.shape
    neighbours = near_list.shape[0]
    rank = basis.shape[1]
    for sub in range(subs):
        fields[sub * slots : (sub + 1) * slots, :] = messages[sub][0:slots, :]

    moments = jnp.concatenate([ref[slots : 2 * slots, 0:rank] for ref in messages], axis=0)
    columns = wide_transpose(leaf_part(moments, picks, weights))
    copy.wait()
    box_sum = jnp.zeros(box_basis.shape[1:], jnp.float32)
    for leaf in range(slots):
        total = jnp.zeros((width, width), jnp.float32)
        for column in range(neighbours):
            place = near_list[column, leaf] ^ (box[0] * slots)
            total = total + values[leaf * neighbours + column] * fields[pl.ds(place, 1), :]
        near = jnp.sum(total.T, axis=0, keepdims=True)
        near = leaf_far_row(counts, columns, basis, leaf, near)
        part[leaf : leaf + 1, :] = near
        box_sum = box_sum + box_basis[leaf] * near
    first, one, second = messages[0][0:slots, :], basis_one[...], part[...]
    products = [one * second, first * second, second * second]
    sums = lane_row([jnp.sum(product, keepdims=True) for product in products])
    sums = share[1:2, :] + pltpu.roll(sums, 2, 1)
    both = share[0:1, :] + pltpu.roll(sum_lanes(box_sum), rank, 1)
    shares[...] = jnp.where(iota(shares.shape, 0) % 2 == 0, both, sums)


def last_kernel(box, *refs):
    shares, message, basis_one, part, numbers, starts, rows, grams = refs[:8]
    box_basis, box_weights, basis_three, hessenberg, pairs, image = refs[8:]
    slots, rank, width = box_basis.shape
    count = starts.shape[0]
    for other in range(count):
        pairs[other : other + 1, :] = shares[2 * other : 2 * other + 1, :]
        pairs[count + other : count + other + 1, :] = shares[2 * other + 1 : 2 * other + 2, :]
    first_box, second_box = pairs[0:count, 0:rank], pairs[0:count, rank : 2 * rank]
    chosen_rows = jnp.dot(
        rows[...], split_rows(first_box), preferred_element_type=jnp.float32
    ).astype(jnp.bfloat16)

    def chosen(place):
        return chosen_rows[place * 3 * count : (place + 1) * 3 * count]

    box_local = coupled_rows(chosen, box_weights)
    twice = jnp.concatenate([box_local, box_local], axis=1)
    columns = twice.T
    half = rank // 2
    low = iota((half, 2 * rank), 1) < rank
    quadratic = jnp.zeros((half, 2 * rank), jnp.float32)
    for other in range(count):
        column = jnp.where(
            low, columns[0:half, other : other + 1], columns[half:rank, other : other + 1]
        )
        gram = grams[other * half : (other + 1) * half, :]
        quadratic = quadratic + gram * twice[other : other + 1, :] * column
    one_one, unknowns, start_scale = [numbers[0:1, place : place + 1] for place in range(3)]
    sums = jnp.sum(pairs[count : 2 * count, :], axis=0, keepdims=True)
    along, image_sq, one_part, first_part, part_sq = [
        sums[:, place : place + 1] for place in range(5)
    ]
    one_second = (
        one_part + jnp.sum(starts[:, 0:rank] * box_local, keepdims=True) / start_scale
    )
    first_second = first_part + jnp.sum(first_box * box_local, keepdims=True)
    second_sq = (
        part_sq
        + 2.0 * jnp.sum(second_box * box_local, keepdims=True)
        + jnp.sum(quadratic, keepdims=True)
    )
    upper_first = (0.5 * one_one + along) / unknowns
    shift = upper_first - 0.5
    residual_sq = image_sq - 2.0 * shift * along + shift * shift * one_one
    lower_first = jnp.sqrt(residual_sq / unknowns + EPSILON)
    one_two = (along - shift * one_one) / lower_first
    two_two = residual_sq / (lower_first * lower_first)
    k_one = (one_second - shift * along) / lower_first
    k_two = (
        (first_second - shift * image_sq) - shift * (one_second - shift * along)
    ) / (lower_first * lower_first)
    k_sq = (second_sq - 2.0 * shift * first_second + shift * shift * image_sq) / (
        lower_first * lower_first
    )
    upper_second = (0.5 * one_two + k_one) / unknowns
    middle_second = (0.5 * two_two + k_two - upper_second * one_two) / unknowns
    turn = middle_second - 0.5
    final_sq = (
        k_sq
        - 2.0 * upper_second * k_one
        - 2.0 * turn * k_two
        + upper_second * upper_second * one_one
        + 2.0 * upper_second * turn * one_two
        + turn * turn * two_two
    )
    lower_second = jnp.sqrt(final_sq / unknowns + EPSILON)
    image[...] = part[...]
    own = jnp.where(iota((rank, count), 1) == box[0], columns[0:rank], 0.0)
    box_images(box_basis, jnp.sum(own, axis=1, keepdims=True), image)
    one, first = basis_one[...], message[0:slots, :]
    two = (first - shift * one) / lower_first
    mapped = (image[...] - shift * first) / lower_first
    basis_three[...] = (mapped - upper_second * one - turn * two) / lower_second
    column, row = iota(hessenberg.shape, 0), iota(hessenberg.shape, 1)
    matrix = jnp.where(column == 0, upper_first, upper_second)
    matrix = jnp.where(row == 1, jnp.where(column == 0, lower_first, middle_second), matrix)
    hessenberg[...] = jnp.where(row == 2, jnp.where(column == 0, 0.0, lower_second), matrix)


def shards(
    points,
    normals,
    density,
    counts,
    near_list,
    leaf_far,
    leaf_basis,
    leaf_to_box_transfer,
    leaf_coupling,
    box_far,
    box_coupling,
):
    slots, _, width = points.shape
    neighbours = near_list.shape[1]
    far_count = leaf_far.shape[1]
    subs, patches = lax.axis_size("sub"), lax.axis_size("patch")
    sources = subs * slots
    rows = kept(slots, width)
    this_box = lax.axis_index("patch") * subs + lax.axis_index("sub")
    box = this_box.astype(jnp.int32).reshape(1)
    far_list = leaf_far.T
    rank = leaf_basis.shape[1]
    span = TILE_ROWS + rank // 2
    near_list = near_list.T
    list_scratch = [pltpu.SMEM(near_list.shape, jnp.int32), pltpu.SemaphoreType.DMA]
    block = pltpu.VMEM((sources, width), jnp.float32)

    matrices, lists = [leaf_basis, leaf_coupling, box_coupling], [near_list, far_list]
    geometry, message, box_basis, *held = device_call(
        start_kernel,
        [
            kept(slots, 8, width),
            kept(slots + span, LANES),
            kept(*leaf_basis.shape),
            *[kept(*matrix.shape) for matrix in matrices],
            *[kept(*entries.shape, dtype=jnp.int32) for entries in lists],
        ],
        [counts],
        [],
        [
            pltpu.VMEM((7, slots, width), jnp.float32),
            pltpu.VMEM((slots, width), jnp.float32),
            pltpu.SMEM(box_far.shape, jnp.int32),
            pltpu.VMEM(leaf_to_box_transfer.shape, jnp.float32),
            pltpu.VMEM((3 * rank, slots * width), jnp.bfloat16),
            pltpu.SemaphoreType.DMA((8 + 2 * CHUNKS,)),
        ],
        [
            points.transpose(1, 0, 2),
            normals.transpose(1, 0, 2),
            density,
            box_far,
            leaf_to_box_transfer,
            *matrices,
            *lists,
        ],
    )
    leaf_basis, leaf_coupling, box_coupling, near_list, far_list = held
    messages = from_peers(message, "sub")
    geometry = from_peers(geometry, "sub")
    picks, weights, box_weights = device_call(
        weights_kernel,
        [
            kept(far_count * slots, sources, dtype=jnp.bfloat16),
            kept(far_count, rank, 3 * rank, dtype=jnp.bfloat16),
            kept(box_coupling.shape[0], rank, 3 * rank, dtype=jnp.bfloat16),
        ],
        [box],
        [leaf_coupling, box_coupling, far_list],
    )
    moments, blocks = device_call(
        functools.partial(join_kernel, subs),
        [kept(sources, LANES), kept(subs * span, LANES)],
        [],
        [*messages, box_weights],
        cost=FIRST,
    )
    boxes = from_peers(blocks, "patch")
    (columns,) = device_call(leaf_kernel, [kept(LANES, slots)], [], [moments, picks, weights])
    part, initial, values = device_call(
        functools.partial(first_near_kernel, subs),
        [rows, rows, kept(slots * neighbours, width, width)],
        [box, counts],
        [*geometry, columns, leaf_basis, near_list],
        [
            pltpu.VMEM((sources, 32, 2 * width), jnp.bfloat16),
            block,
            block,
            pltpu.VMEM((slots, width), jnp.float32),
            *list_scratch,
        ],
    )
    message, basis_one, numbers = device_call(
        functools.partial(first_image_kernel, patches, span),
        [kept(2 * slots, LANES), rows, kept(TILE_ROWS, LANES)],
        [box],
        [*boxes, part, initial, leaf_basis, box_basis, box_coupling],
        [
            pltpu.VMEM((patches * subs, LANES), jnp.float32),
            pltpu.VMEM((slots, width), jnp.float32),
        ],
    )
    messages = from_peers(message, "sub")
    count, places = patches * subs, box_far.shape[1]
    share, starts, chosen, grams = device_call(
        functools.partial(share_kernel, patches, span),
        [
            kept(TILE_ROWS, LANES),
            kept(count, LANES),
            kept(places * 3 * count, 3 * count, dtype=jnp.bfloat16),
            kept(count * (rank // 2), LANES),
        ],
        [box],
        [*boxes, message, basis_one, box_basis],
        [
            pltpu.VMEM((count * span, LANES), jnp.float32),
            pltpu.VMEM((count, LANES), jnp.float32),
        ],
    )
    part, shares = device_call(
        functools.partial(second_near_kernel, subs),
        [rows, kept(2 * patches * subs, LANES)],
        [box, counts],
        [*messages, picks, weights, leaf_basis, box_basis, basis_one, share, values, near_list],
        [block, *list_scratch],
    )
    shares = lax.all_to_all(shares, ("patch", "sub"), 0, 0, tiled=True)
    basis_three, hessenberg = device_call(
        last_kernel,
        [f32(slots, width), f32(2, 3)],
        [box],
        [
            shares,
            message,
            basis_one,
            part,
            numbers,
            starts,
            chosen,
            grams,
            box_basis,
            box_weights,
        ],
        [
            pltpu.VMEM((2 * count, LANES), jnp.float32),
            pltpu.VMEM((slots, width), jnp.float32),
        ],
    )
    return basis_three, hessenberg.T


def solution(mesh):
    spread = ("groups", "patch", "sub")
    in_specs = (
        P(spread, None, None),
        P(spread, None, None),
        P(spread, None),
        P(spread),
        P(spread, None),
        P(spread, None),
        P(spread, None, None),
        P(spread, None, None),
        P(),
        P(spread, None),
        P(),
    )
    out_specs = (P(spread, None), P("groups", None))
    return jax.shard_map(shards, mesh=mesh, in_specs=in_specs, out_specs=out_specs, check_vma=False)
```
